32 devices in a mesh: grp: 2 (over x), ctx: 16 (over z, y, core).
Axes of the slice: x: 2, y: 2, z: 4, core: 2. Of those that a mesh axis runs over, the one named last changes fastest.
Arguments:
- queries: bfloat16 [4, 12, 64, 128], P(None, 'grp'), parts along dimension 1, may hold values from -150 to 150
- key_cache: bfloat16 [12, 8, 2048, 128], P('grp', None, 'ctx'), parts along dimension 0, may hold values from -6 to 6
- value_cache: bfloat16 [12, 8, 2048, 128], P('grp', None, 'ctx'), parts along dimension 0, may hold values from -6 to 6
- row_lengths: int32 [12], P('grp'), parts along dimension 0, may hold values from 128 to 2048, as said below
- kept_tiles: int32 [4, 12, 16], P(None, 'grp'), parts along dimension 1, may hold values from 0 to 1, as said below
- tile_dest: int32 [12, 8, 16], P('grp'), parts along dimension 0, may hold values from 0 to 15, as said below
Outputs:
- attn_out: bfloat16 [4, 12, 64, 128], P(None, 'grp'), parts along dimension 1
- tile_mass: float32 [12, 8, 16], P('grp', None, 'ctx'), parts along dimension 0
- moved_keys: bfloat16 [12, 8, 2048, 128], P('grp', None, 'ctx'), parts along dimension 0
- moved_values: bfloat16 [12, 8, 2048, 128], P('grp', None, 'ctx'), parts along dimension 0
The draws below stay inside these ranges and needn't reach their ends.
There are 2 independent parts, one for each index of `grp`. The reference program is written for one: setup_inputs(seed, part) draws one part's arguments, and reference() takes and returns one part's arrays. A program takes and returns all parts, laid end to end along the dimension named above; each array names one. Nothing has to cross between parts.
Inputs may be any that keep to these rules, and one draw needn't show every extreme that they name: `row_lengths`: at least 128 positions of every row are filled; some row is filled to all 2048 positions. `kept_tiles`: A tile dropped at one step stays dropped at all later steps; tile 0 of every row is kept at every step. For each row and head, tile_dest is a permutation of the 16 tiles. The 1 tiles that one index of ctx holds for a row and head all go, in some order, to the index a per-row-and-head offset further along ctx, wrapping around; that offset is the same for every index. No offset is used by more than 3 row-head pairs, and some offset is used by exactly 3. The offsets 16 // 2 and 1 are used by some row-head pair in every draw.
All inputs are finite; a program needn't handle non-finite values.
Results may differ from the reference program's by a relative error of at most 0.0027.
Values may be sent and summed in bfloat16 or wider, within the bound.
No kernel may reach another device: no remote copies, remote signals or barrier semaphores. Data moves between devices by JAX's collectives and lax.ppermute only.
A program may use at most 64 MiB of HBM per device.

```python
import jax
import jax.numpy as jnp
from jax import lax

QH = 64
KVH = 8
HD = 128
TILE = 128
STEPS = 4
ROWS = 6
TILES_DEV = 1
TILES = 16
SLOTS = 2048
N_CTX = 16


def draw_key_cache(key, part):
    drawn = jnp.clip(jax.random.normal(jax.random.fold_in(key, 32), (ROWS, KVH, SLOTS, HD), jnp.float32), -6.0, 6.0)
    return drawn.astype(jnp.bfloat16)


def draw_queries(key, part):
    drawn = 3.0 * jnp.clip(jax.random.normal(jax.random.fold_in(key, 33), (STEPS, ROWS, QH, HD), jnp.float32), -6.0, 6.0)
    return drawn.astype(jnp.bfloat16)


def draw_row_lengths(key, part):
    drawn = jax.random.randint(jax.random.fold_in(key, 41), (ROWS,), TILE, SLOTS + 1)
    longest = jax.random.randint(jax.random.fold_in(key, 42), (), 0, ROWS)
    return drawn.at[longest].set(SLOTS).astype(jnp.int32)


def draw_kept_tiles(key, part):
    evict_step = jax.random.randint(jax.random.fold_in(key, 51), (ROWS, TILES), 0, 2 * STEPS)
    evict_step = evict_step.at[:, 0].set(2 * STEPS)
    steps_index = jnp.arange(STEPS, dtype=jnp.int32)[:, None, None]
    return (steps_index < evict_step[None, :, :]).astype(jnp.int32)


def swap_front(values, wanted, place):
    where_found = jnp.argmax((values == wanted).astype(jnp.int32))
    current = values[place]
    return values.at[where_found].set(current).at[place].set(wanted)


def draw_tile_dest(key, part):
    pair_count = ROWS * KVH
    pair_order = jax.random.permutation(jax.random.fold_in(key, 61), pair_count)
    shift_pick = jax.random.permutation(jax.random.fold_in(key, 62), N_CTX).astype(jnp.int32)
    shift_pick = swap_front(shift_pick, N_CTX // 2, 0)
    shift_pick = swap_front(shift_pick, 1, 1)
    offsets = shift_pick[pair_order % N_CTX].reshape(ROWS, KVH)
    slot_scores = jax.random.randint(jax.random.fold_in(key, 63), (ROWS, KVH, N_CTX, TILES_DEV), 0, 1 << 20)
    slot_scores = slot_scores * TILES_DEV + jnp.arange(TILES_DEV, dtype=jnp.int32)
    slot_order = jnp.argsort(slot_scores, axis=-1, stable=True)
    devices = jnp.arange(N_CTX, dtype=jnp.int32)[None, None, :, None]
    target = (devices + offsets[:, :, None, None]) % N_CTX * TILES_DEV + slot_order
    return target.reshape(ROWS, KVH, TILES).astype(jnp.int32)


def shard_levels(rng, dims, shards, smallest, largest):
    loudness = 1.0
    for dim, shards_of in shards:
        draws = jax.random.uniform(jax.random.fold_in(jax.random.fold_in(rng, 6), dim), (shards_of,), jnp.float32, smallest / len(shards), largest / len(shards))
        loudness = loudness * jnp.repeat(jnp.exp(draws), dims[dim] // shards_of).reshape((-1,) + (1,) * (len(dims) - 1 - dim))
    return loudness


def normal_values(key, dims, width, reach, cuts=(), kind=jnp.bfloat16):
    loudness = shard_levels(key, dims, cuts, -0.22, 0.18) if cuts else 1.0
    result = jax.random.normal(key, dims, jnp.float32) * width * loudness
    return jnp.minimum(jnp.maximum(result, -reach), reach).astype(kind)


def setup_inputs(seed: int = 0, part: int = 0) -> dict:
    splits = jax.random.split(jax.random.key(seed), 7)
    own_keys = jax.random.split(jax.random.fold_in(splits[6], part), 7)
    return {
        "queries": draw_queries(jax.random.fold_in(jax.random.fold_in(splits[6], part), 71), part),
        "key_cache": draw_key_cache(jax.random.fold_in(jax.random.fold_in(splits[6], part), 71), part),
        "value_cache": normal_values(own_keys[2], (ROWS, KVH, SLOTS, HD), 1.0, 6.0, ((2, 16),)),
        "row_lengths": draw_row_lengths(jax.random.fold_in(jax.random.fold_in(splits[6], part), 71), part),
        "kept_tiles": draw_kept_tiles(jax.random.fold_in(jax.random.fold_in(splits[6], part), 71), part),
        "tile_dest": draw_tile_dest(jax.random.fold_in(jax.random.fold_in(splits[6], part), 71), part),
    }


absent_score = -1e30


def row_attention(inputs):
    query_row, key_row, value_row, length, kept_row = inputs
    group_size = QH // KVH
    block_len = TILES_DEV * TILE
    grouped = query_row.astype(jnp.float32).reshape(STEPS, KVH, group_size, HD)
    key_blocks = key_row.astype(jnp.float32).reshape(KVH, N_CTX, block_len, HD)
    value_blocks = value_row.astype(jnp.float32).reshape(KVH, N_CTX, block_len, HD)
    scores = jnp.einsum("shgd,hnbd->shgnb", grouped, key_blocks) * (HD ** -0.5)
    positions = jnp.arange(SLOTS, dtype=jnp.int32)
    live_mask = (jnp.repeat(kept_row, TILE, axis=1) > 0) & (positions[None, :] < length)
    live_mask = live_mask.reshape(STEPS, 1, 1, N_CTX, block_len)
    block_peak = jnp.max(jnp.where(live_mask, scores, absent_score), axis=-1)
    weights = jnp.where(live_mask, jnp.exp(scores - block_peak[..., None]), 0.0)
    block_total = jnp.sum(weights, axis=-1)
    rounded = lax.optimization_barrier(weights.astype(jnp.bfloat16)).astype(jnp.float32)
    block_out = jnp.einsum("shgnb,hnbd->shgnd", rounded, value_blocks)
    score_peak = jnp.max(block_peak, axis=-1)
    factor = jnp.exp(block_peak - score_peak[..., None])
    denominator = jnp.sum(block_total * factor, axis=-1)
    summed = jnp.sum(block_out * factor[..., None], axis=3)
    attended = (summed / denominator[..., None]).astype(jnp.bfloat16).reshape(STEPS, QH, HD)
    coefficient = factor / denominator[..., None]
    tile_sums = jnp.einsum("shgnb,shgn->hnb", weights, coefficient, precision=lax.Precision.HIGHEST)
    tile_sums = tile_sums.reshape(KVH, N_CTX, TILES_DEV, TILE).sum(-1).reshape(KVH, TILES)
    return attended, tile_sums


def relocate(cache, tile_dest):
    tile_blocks = cache.reshape(ROWS, KVH, TILES, TILE, HD)
    row_index = jnp.arange(ROWS, dtype=jnp.int32)[:, None, None]
    head_index = jnp.arange(KVH, dtype=jnp.int32)[None, :, None]
    placed = jnp.zeros_like(tile_blocks).at[row_index, head_index, tile_dest].set(tile_blocks)
    return placed.reshape(cache.shape)


def reference(queries, key_cache, value_cache, row_lengths, kept_tiles, tile_dest):
    attended, tile_mass = lax.map(
        row_attention,
        (jnp.moveaxis(queries, 1, 0), key_cache, value_cache, row_lengths, jnp.moveaxis(kept_tiles, 1, 0)),
    )
    attn_out = jnp.moveaxis(attended, 0, 1)
    return attn_out, tile_mass, relocate(key_cache, tile_dest), relocate(value_cache, tile_dest)
```

```python
import functools

import jax
import jax.numpy as jnp
from jax import lax
from jax.experimental import pallas as pl
from jax.experimental.pallas import tpu as pltpu
from jax.sharding import PartitionSpec as P

absent_score = -1e30
LANES = 128
F32 = jnp.float32
BF16 = jnp.bfloat16
VMEM = pl.BlockSpec(memory_space=pltpu.VMEM)
SMEM = pl.BlockSpec(memory_space=pltpu.SMEM)
ANY = pl.BlockSpec(memory_space=pl.ANY)
PARAMS = pltpu.CompilerParams(vmem_limit_bytes=32 * 1024 * 1024)


def cost(flops, bytes_accessed):
    return pl.CostEstimate(flops=flops, bytes_accessed=bytes_accessed, transcendentals=0)


def each_slot(dest_ref, count_ref, devices, tiles_dev, group, body):
    rows, heads, _ = dest_ref.shape

    def clear(i, carry):
        count_ref[i] = 0
        return carry

    lax.fori_loop(0, devices, clear, 0)

    def step(pair, carry):
        row, head = pair // heads, lax.rem(pair, heads)
        offset = lax.rem(dest_ref[row, head, 0] // tiles_dev, devices)
        rank = count_ref[offset]
        count_ref[offset] = rank + 1
        body(pair, row, head, offset, jnp.minimum(rank, group - 1))
        return carry

    lax.fori_loop(0, rows * heads, step, 0)


def attend_kernel(
    devices, tiles_dev, group, levels,
    me_ref, dest_ref, len_ref, kept_ref, q_ref, k_ref, v_ref,
    buf_ref, stats_ref, *rest,
):
    chunks = rest[:levels]
    k_vm, v_vm, count_ref, move_sem, load_sem = rest[levels:]
    rows, heads, span, width = k_ref.shape
    steps, _, q_heads, _ = q_ref.shape
    per = q_heads // heads
    tile = span // tiles_dev
    me = me_ref[0]

    loads = []
    for row in range(rows):
        for which, (src, dst) in enumerate(((k_ref, k_vm), (v_ref, v_vm))):
            copy = pltpu.make_async_copy(src.at[row], dst.at[row], load_sem.at[which, row])
            copy.start()
            loads.append(copy)

    def send(pair, row, head, offset, rank):
        slot = lax.rem(me + offset, devices) * group + rank
        pltpu.make_async_copy(k_ref.at[row, head], buf_ref.at[slot, 0], move_sem.at[0]).start()
        pltpu.make_async_copy(v_ref.at[row, head], buf_ref.at[slot, 1], move_sem.at[1]).start()

    each_slot(dest_ref, count_ref, devices, tiles_dev, group, send)

    lane = lax.broadcasted_iota(jnp.int32, (per, tile), 1)
    pair_lane = lax.broadcasted_iota(jnp.int32, (steps * per, LANES), 1)
    peaks = jnp.full((steps * per, LANES), absent_score, F32)
    totals = jnp.zeros((steps * per, LANES), F32)
    order = [jnp.bitwise_xor(lax.rem(me, levels), level) for level in range(levels)]
    scale = width ** -0.5
    for row in range(rows):
        loads[2 * row].wait()
        loads[2 * row + 1].wait()
        queries = [q_ref[step, row].astype(F32) for step in order]
        live = []
        for step in order:
            parts = []
            for j in range(tiles_dev):
                column = me * tiles_dev + j
                limit = jnp.where(kept_ref[row, step, column] > 0, len_ref[row] - column * tile, 0)
                parts.append(lane < limit)
            live.append(parts[0] if tiles_dev == 1 else jnp.concatenate(parts, axis=1))
        live = jnp.concatenate(live, axis=0)
        for head in range(heads):
            q = jnp.concatenate([x[head * per:(head + 1) * per] for x in queries], axis=0).astype(BF16)
            scores = lax.dot_general(
                q, k_vm[row, head], (((1,), (1,)), ((), ())), preferred_element_type=F32
            ) * scale
            peak = jnp.max(jnp.where(live, scores, absent_score), axis=1, keepdims=True)
            weights = jnp.where(live, jnp.exp(scores - peak), 0.0)
            total = jnp.sum(weights, axis=1, keepdims=True)
            out = jnp.dot(weights.astype(BF16), v_vm[row, head], preferred_element_type=F32)
            pair = row * heads + head
            for level in range(levels):
                chunks[level][pair * per:(pair + 1) * per, :] = out[level * per:(level + 1) * per]
            here = pair_lane == pair
            peaks = jnp.where(here, peak, peaks)
            totals = jnp.where(here, total, totals)
    base = rows * q_heads
    for level in range(levels):
        chunks[level][base:base + per, :] = peaks[level * per:(level + 1) * per]
        chunks[level][base + per:base + 2 * per, :] = totals[level * per:(level + 1) * per]
    stats_ref[0] = peaks
    stats_ref[1] = totals
    pltpu.make_async_copy(k_ref, k_ref, move_sem.at[0]).wait()
    pltpu.make_async_copy(v_ref, v_ref, move_sem.at[1]).wait()


def merge(refs, pairs, per):
    base = pairs * per
    peaks = [ref[base:base + per, :] for ref in refs]
    totals = [ref[base + per:base + 2 * per, :] for ref in refs]
    peak = functools.reduce(jnp.maximum, peaks)
    factors = [jnp.exp(x - peak) for x in peaks]
    total = functools.reduce(jnp.add, [f * t for f, t in zip(factors, totals)])

    def summed(pair):
        return functools.reduce(jnp.add, [
            jnp.broadcast_to(f[:, pair:pair + 1], (per, ref.shape[1])) * ref[pair * per:(pair + 1) * per, :]
            for f, ref in zip(factors, refs)
        ])

    return peak, total, summed


def near_kernel(pairs, per, levels, parts, me_ref, *refs):
    ins, outs, work = refs[:levels], refs[levels:levels + parts], refs[levels + parts]
    peak, total, summed = merge(ins, pairs, per)
    share = pairs // parts
    for part in range(parts):
        for i in range(share):
            work[part, i * per:(i + 1) * per, :] = summed(part * share + i)
        base = share * per
        shift = (LANES - part * share) % LANES
        work[part, base:base + per, :] = pltpu.roll(peak, shift, 1) if shift else peak
        work[part, base + per:base + 2 * per, :] = pltpu.roll(total, shift, 1) if shift else total
    mine = me_ref[0] // levels
    for part in range(parts):
        outs[part][...] = work[jnp.bitwise_xor(mine, part)]


def far_kernel(share, per, parts, *refs):
    ins, out = refs[:parts], refs[parts]
    peak, total, summed = merge(ins, share, per)
    lane = lax.broadcasted_iota(jnp.int32, peak.shape, 1)
    total = jnp.where(lane < share, total, 1.0)
    peak = jnp.where(lane < share, peak, 0.0)

    def result(pair):
        return summed(pair) / jnp.broadcast_to(total[:, pair:pair + 1], (per, LANES))

    for pair in range(0, share, 2):
        both = jnp.concatenate([result(pair), result(pair + 1)], axis=0)
        out[pair * per:(pair + 2) * per, :] = both.astype(BF16)
    rest = jnp.concatenate([peak, total], axis=0)
    base = share * per
    for i in range(3):
        part = rest.astype(BF16)
        out[base + 2 * i * per:base + 2 * (i + 1) * per, :] = part
        rest = rest - part.astype(F32)


def join_kernel(levels, parts, me_ref, *refs):
    ins, out = refs[:parts], refs[parts]
    mine = me_ref[0] // levels
    for part in range(parts):
        out[jnp.bitwise_xor(mine, part)] = ins[part][...]


def finish_kernel(share, per, levels, parts, me_ref, stats_ref, *refs):
    ins, out, mass_ref = refs[:levels], refs[levels], refs[levels + 1]
    mine = lax.rem(me_ref[0], levels)
    base = share * per
    lane = lax.broadcasted_iota(jnp.int32, (per, LANES), 1)
    mass = jnp.zeros((per, LANES), F32)
    for level in range(levels):
        step = jnp.bitwise_xor(mine, level)
        peak = jnp.zeros((per, LANES), F32)
        total = jnp.ones((per, LANES), F32)
        for part in range(parts):
            out[step, part * base:(part + 1) * base, :] = ins[level][part, :base, :]
            both = functools.reduce(jnp.add, [
                ins[level][part, base + 2 * i * per:base + 2 * (i + 1) * per, :].astype(F32)
                for i in (2, 1, 0)
            ])
            if part:
                both = pltpu.roll(both, part * share, 1)
            here = (lane >= part * share) & (lane < (part + 1) * share)
            peak = jnp.where(here, both[:per], peak)
            total = jnp.where(here, both[per:], total)
        own_peak = stats_ref[0, level * per:(level + 1) * per, :]
        own_total = stats_ref[1, level * per:(level + 1) * per, :]
        coefficient = jnp.exp(jnp.minimum(own_peak - peak, 0.0)) / total
        mass = mass + own_total * coefficient
    mass_ref[...] = jnp.sum(mass, axis=0, keepdims=True)


def place_kernel(devices, tiles_dev, group, me_ref, dest_ref, got_ref, k_ref, v_ref, count_ref, sem):
    span = k_ref.shape[2]
    tile = span // tiles_dev
    me = me_ref[0]

    def take(pair, row, head, offset, rank):
        source = lax.rem(me + devices - offset, devices)
        slot = source * group + rank
        for which, ref in enumerate((k_ref, v_ref)):
            for j in range(tiles_dev):
                if tiles_dev == 1:
                    src, dst = got_ref.at[slot, which], ref.at[row, head]
                else:
                    target = lax.rem(dest_ref[row, head, source * tiles_dev + j], tiles_dev)
                    src = got_ref.at[slot, which, pl.ds(j * tile, tile)]
                    dst = ref.at[row, head, pl.ds(pl.multiple_of(target * tile, tile), tile)]
                pltpu.make_async_copy(src, dst, sem.at[which]).start()

    each_slot(dest_ref, count_ref, devices, tiles_dev, group, take)
    pltpu.make_async_copy(k_ref, k_ref, sem.at[0]).wait()
    pltpu.make_async_copy(v_ref, v_ref, sem.at[1]).wait()


def local(queries, key_cache, value_cache, row_lengths, kept_tiles, tile_dest):
    devices = lax.axis_size("ctx")
    rows, heads, span, width = key_cache.shape
    steps, _, q_heads, _ = queries.shape
    per = q_heads // heads
    pairs = rows * heads
    tiles_dev = tile_dest.shape[2] // devices
    group = -(-pairs // devices)
    levels = steps
    parts = devices // levels
    two_level = devices % levels == 0 and pairs % (2 * parts) == 0 and parts & (parts - 1) == 0
    share = pairs // parts if two_level else 0

    me = lax.axis_index("ctx").astype(jnp.int32).reshape(1)
    kept = jnp.transpose(kept_tiles, (1, 0, 2))
    chunk_rows = rows * q_heads + 2 * per

    attend = pl.pallas_call(
        functools.partial(attend_kernel, devices, tiles_dev, group, levels),
        out_shape=[
            jax.ShapeDtypeStruct((devices * group, 2, span, width), BF16),
            jax.ShapeDtypeStruct((2, steps * per, LANES), F32),
        ] + [jax.ShapeDtypeStruct((chunk_rows, width), F32)] * levels,
        in_specs=[SMEM, SMEM, SMEM, SMEM, VMEM, ANY, ANY],
        out_specs=[ANY, VMEM] + [VMEM] * levels,
        scratch_shapes=[
            pltpu.VMEM(key_cache.shape, BF16),
            pltpu.VMEM(value_cache.shape, BF16),
            pltpu.SMEM((devices,), jnp.int32),
            pltpu.SemaphoreType.DMA((2,)),
            pltpu.SemaphoreType.DMA((2, rows)),
        ],
        compiler_params=PARAMS,
        cost_estimate=cost(100_000_000, 12_000_000),
        name="attend",
    )
    buf, stats, *chunks = attend(me, tile_dest, row_lengths, kept, queries, key_cache, value_cache)
    got = lax.all_to_all(buf, "ctx", split_axis=0, concat_axis=0, tiled=True)

    if two_level:
        def near(x, level):
            perm = [(i, i // levels * levels + (i % levels ^ level)) for i in range(devices)]
            return lax.ppermute(x, "ctx", perm)

        def far(x, part):
            perm = [(i, (i // levels ^ part) * levels + i % levels) for i in range(devices)]
            return lax.ppermute(x, "ctx", perm)

        part_rows = share * per + 2 * per
        message_rows = share * per + 6 * per
        arrived = [chunks[0]] + [near(chunks[i], i) for i in range(1, levels)]
        pieces = pl.pallas_call(
            functools.partial(near_kernel, pairs, per, levels, parts),
            out_shape=[jax.ShapeDtypeStruct((part_rows, width), F32)] * parts,
            in_specs=[SMEM] + [VMEM] * levels,
            out_specs=[VMEM] * parts,
            scratch_shapes=[pltpu.VMEM((parts, part_rows, width), F32)],
            compiler_params=PARAMS,
            cost_estimate=cost(1_000_000, 2_000_000),
            name="near",
        )(me, *arrived)
        arrived = [pieces[0]] + [far(pieces[i], i) for i in range(1, parts)]
        message = pl.pallas_call(
            functools.partial(far_kernel, share, per, parts),
            out_shape=jax.ShapeDtypeStruct((message_rows, width), BF16),
            in_specs=[VMEM] * parts,
            out_specs=VMEM,
            compiler_params=PARAMS,
            cost_estimate=cost(1_000_000, 500_000),
            name="far",
        )(*arrived)
        arrived = [message] + [far(message, i) for i in range(1, parts)]
        joined = pl.pallas_call(
            functools.partial(join_kernel, levels, parts),
            out_shape=jax.ShapeDtypeStruct((parts, message_rows, width), BF16),
            in_specs=[SMEM] + [VMEM] * parts,
            out_specs=VMEM,
            compiler_params=PARAMS,
            cost_estimate=cost(1_000, 500_000),
            name="join",
        )(me, *arrived)
        arrived = [joined] + [near(joined, i) for i in range(1, levels)]
        attn_out, mass = pl.pallas_call(
            functools.partial(finish_kernel, share, per, levels, parts),
            out_shape=[
                jax.ShapeDtypeStruct((steps, rows * q_heads, width), BF16),
                jax.ShapeDtypeStruct((1, LANES), F32),
            ],
            in_specs=[SMEM, VMEM] + [VMEM] * levels,
            out_specs=[VMEM, VMEM],
            compiler_params=PARAMS,
            cost_estimate=cost(1_000, 1_000_000),
            name="finish",
        )(me, stats, *arrived)
        attn_out = attn_out.reshape(queries.shape)
        tile_mass = mass[0, :pairs].reshape(rows, heads, 1)
    else:
        mine = lax.rem(me[0], levels)
        order = jnp.bitwise_xor(mine, jnp.arange(levels))
        stacked = jnp.stack(chunks)[:, :rows * q_heads][order].reshape(steps, rows, heads, per, width)

        def by_pair(x):
            x = x.reshape(levels, per, LANES)[order][:, :, :pairs].reshape(steps, per, rows, heads)
            return jnp.transpose(x, (0, 2, 3, 1))

        peak, total = by_pair(stats[0]), by_pair(stats[1])
        factor = jnp.exp(peak - lax.pmax(peak, "ctx"))
        denominator, summed = lax.psum((total * factor, stacked * factor[..., None]), "ctx")
        attn_out = (summed / denominator[..., None]).astype(BF16).reshape(queries.shape)
        tile_mass = jnp.sum(total * factor / denominator, axis=(0, 3))[:, :, None]

    moved_keys, moved_values = pl.pallas_call(
        functools.partial(place_kernel, devices, tiles_dev, group),
        out_shape=[
            jax.ShapeDtypeStruct(key_cache.shape, BF16),
            jax.ShapeDtypeStruct(value_cache.shape, BF16),
        ],
        in_specs=[SMEM, SMEM, ANY],
        out_specs=[ANY, ANY],
        scratch_shapes=[pltpu.SMEM((devices,), jnp.int32), pltpu.SemaphoreType.DMA((2,))],
        compiler_params=PARAMS,
        cost_estimate=cost(1_000, 6_000_000),
        name="place",
    )(me, tile_dest, got)
    return attn_out, tile_mass, moved_keys, moved_values


def solution(mesh):
    in_specs = (
        P(None, "grp", None, None),
        P("grp", None, "ctx", None),
        P("grp", None, "ctx", None),
        P("grp"),
        P(None, "grp", None),
        P("grp", None, None),
    )
    out_specs = (
        P(None, "grp", None, None),
        P("grp", None, "ctx"),
        P("grp", None, "ctx", None),
        P("grp", None, "ctx", None),
    )
    return jax.shard_map(local, mesh=mesh, in_specs=in_specs, out_specs=out_specs, check_vma=False)
```

```python
import functools

import jax
import jax.numpy as jnp
from jax import lax
from jax.experimental import pallas as pl
from jax.experimental.pallas import tpu as pltpu
from jax.sharding import PartitionSpec as P

absent_score = -1e30
LANES = 128
FIELD = 32
F32 = jnp.float32
BF16 = jnp.bfloat16
VMEM = pl.BlockSpec(memory_space=pltpu.VMEM)
SMEM = pl.BlockSpec(memory_space=pltpu.SMEM)
HBM = pl.BlockSpec(memory_space=pltpu.HBM)
ANY = pl.BlockSpec(memory_space=pl.ANY)
PARAMS = pltpu.CompilerParams(vmem_limit_bytes=16 * 1024 * 1024)
WHOLE = pltpu.CompilerParams(vmem_limit_bytes=62 * 1024 * 1024)


def cost(flops, bytes_accessed):
    return pl.CostEstimate(flops=1000, bytes_accessed=1000, transcendentals=0)


def fill_table(dest, table, devices, tiles_dev, group):
    rows, heads, _ = dest.shape

    def clear(i, carry):
        table[i] = 0
        return carry

    lax.fori_loop(0, devices * (group + 1), clear, 0)

    def step(pair, carry):
        offset = lax.rem(dest[pair // heads, lax.rem(pair, heads), 0] // tiles_dev, devices)
        rank = table[devices * group + offset]
        table[devices * group + offset] = rank + 1
        table[offset * group + jnp.minimum(rank, group - 1)] = pair
        return carry

    lax.fori_loop(0, rows * heads, step, 0)


def stage(table, k_ref, v_ref, bufs, offsets, group, sem):
    heads = k_ref.shape[1]
    waits = []
    for i, (buf, offset) in enumerate(zip(bufs, offsets)):
        for k in range(group):
            pair = table[offset * group + k]
            row, head = pair // heads, lax.rem(pair, heads)
            pltpu.make_async_copy(k_ref.at[row, head], buf.at[k, 0], sem.at[i]).start()
            pltpu.make_async_copy(v_ref.at[row, head], buf.at[k, 1], sem.at[i]).start()
        waits.append(pltpu.make_async_copy(buf, buf, sem.at[i]))
    return waits


def stage_kernel(devices, tiles_dev, group, offsets, dest_hbm, k_ref, v_ref, table, *rest):
    bufs = rest[:len(offsets)]
    dest, load_sem, sem = rest[len(offsets):]
    copy = pltpu.make_async_copy(dest_hbm, dest, load_sem)
    copy.start()
    copy.wait()
    fill_table(dest, table, devices, tiles_dev, group)
    for wait in stage(table, k_ref, v_ref, bufs, offsets, group, sem):
        wait.wait()


def attend_kernel(
    devices, tiles_dev, group, levels, offsets,
    me_ref, table, len_hbm, kept_hbm, q_hbm, k_ref, v_ref,
    *rest,
):
    count = len(offsets)
    bufs, stats_ref, chunks = rest[:count], rest[count], rest[count + 1:count + 1 + levels]
    q_vm, k_vm, v_vm, work, len_ref, kept_ref, load_sem, small_sem, sem, out_sem = rest[count + 1 + levels:]
    rows, heads, span, width = k_ref.shape
    steps, _, q_heads, _ = q_hbm.shape
    per = q_heads // heads
    tile = span // tiles_dev
    me = me_ref[0]

    small = [
        pltpu.make_async_copy(len_hbm, len_ref, small_sem.at[0]),
        pltpu.make_async_copy(kept_hbm, kept_ref, small_sem.at[1]),
    ]
    for copy in small:
        copy.start()
    loads = []
    for row in range(rows):
        copies = [
            pltpu.make_async_copy(q_hbm.at[:, row], q_vm.at[row], load_sem.at[0, row]),
            pltpu.make_async_copy(k_ref.at[row], k_vm.at[row], load_sem.at[1, row]),
            pltpu.make_async_copy(v_ref.at[row], v_vm.at[row], load_sem.at[2, row]),
        ]
        for copy in copies:
            copy.start()
        loads.append(copies)
    waits = stage(table, k_ref, v_ref, bufs, offsets, group, sem)
    for copy in small:
        copy.wait()

    lane = lax.broadcasted_iota(jnp.int32, (per, tile), 1)
    pair_lane = lax.broadcasted_iota(jnp.int32, (steps * per, LANES), 1)
    peaks = jnp.full((steps * per, LANES), absent_score, F32)
    totals = jnp.zeros((steps * per, LANES), F32)
    order = [jnp.bitwise_xor(lax.rem(me, levels), level) for level in range(levels)]
    scale = width ** -0.5
    block = steps * per
    for row in range(rows):
        for copy in loads[row]:
            copy.wait()
        queries = [q_vm[row, step].astype(F32) for step in order]
        live = []
        for step in order:
            parts = []
            for j in range(tiles_dev):
                column = me * tiles_dev + j
                limit = jnp.where(kept_ref[row, step, column] > 0, len_ref[row] - column * tile, 0)
                parts.append(lane < limit)
            live.append(parts[0] if tiles_dev == 1 else jnp.concatenate(parts, axis=1))
        live = jnp.concatenate(live * heads, axis=0)
        scores = []
        for head in range(heads):
            q = jnp.concatenate([x[head * per:(head + 1) * per] for x in queries], axis=0).astype(BF16)
            scores.append(lax.dot_general(
                q, k_vm[row, head], (((1,), (1,)), ((), ())), preferred_element_type=F32
            ))
        scores = jnp.concatenate(scores, axis=0) * scale
        peak = jnp.max(jnp.where(live, scores, absent_score), axis=1, keepdims=True)
        weights = jnp.where(live, jnp.exp(scores - peak), 0.0)
        total = jnp.sum(weights, axis=1, keepdims=True)
        rounded = weights.astype(BF16)
        for head in range(heads):
            out = jnp.dot(
                rounded[head * block:(head + 1) * block], v_vm[row, head], preferred_element_type=F32
            )
            pair = row * heads + head
            for level in range(levels):
                work[level, pair * per:(pair + 1) * per, :] = out[level * per:(level + 1) * per]
            here = pair_lane == pair
            peaks = jnp.where(here, peak[head * block:(head + 1) * block], peaks)
            totals = jnp.where(here, total[head * block:(head + 1) * block], totals)
    base = rows * q_heads
    for level in range(levels):
        work[level, base:base + per, :] = peaks[level * per:(level + 1) * per]
        work[level, base + per:base + 2 * per, :] = totals[level * per:(level + 1) * per]
    stats_ref[0] = peaks
    stats_ref[1] = totals
    waits += [
        pltpu.make_async_copy(work.at[level], chunks[level], out_sem.at[level]) for level in range(levels)
    ]
    for copy in waits[-levels:]:
        copy.start()
    for copy in waits:
        copy.wait()


def merge(refs, pairs, per):
    base = pairs * per
    peaks = [ref[base:base + per, :] for ref in refs]
    totals = [ref[base + per:base + 2 * per, :] for ref in refs]
    peak = functools.reduce(jnp.maximum, peaks)
    factors = [jnp.exp(x - peak) for x in peaks]
    total = functools.reduce(jnp.add, [f * t for f, t in zip(factors, totals)])

    def summed(pair):
        return functools.reduce(jnp.add, [
            jnp.broadcast_to(f[:, pair:pair + 1], (per, ref.shape[1])) * ref[pair * per:(pair + 1) * per, :]
            for f, ref in zip(factors, refs)
        ])

    return peak, total, summed


def near_kernel(pairs, per, levels, parts, held, me_ref, *refs):
    ins, refs = refs[:levels], refs[levels + held:]
    outs, (work, sem) = refs[:parts], refs[parts + held:]
    peak, total, summed = merge(ins, pairs, per)
    share = pairs // parts
    for part in range(parts):
        for i in range(share):
            work[part, i * per:(i + 1) * per, :] = summed(part * share + i)
        base = share * per
        shift = (LANES - part * share) % LANES
        work[part, base:base + per, :] = pltpu.roll(peak, shift, 1) if shift else peak
        work[part, base + per:base + 2 * per, :] = pltpu.roll(total, shift, 1) if shift else total
    mine = me_ref[0] // levels
    copies = [
        pltpu.make_async_copy(work.at[jnp.bitwise_xor(mine, part)], outs[part], sem.at[part])
        for part in range(parts)
    ]
    for copy in copies:
        copy.start()
    for copy in copies:
        copy.wait()


def far_kernel(share, per, parts, held, *refs):
    ins, refs = refs[:parts], refs[parts + held:]
    out, (work, sem) = refs[0], refs[1 + held:]
    peak, total, summed = merge(ins, share, per)
    lane = lax.broadcasted_iota(jnp.int32, peak.shape, 1)
    total = jnp.where(lane < share, total, 1.0)
    peak = jnp.where(lane < share, peak, 0.0)

    def result(pair):
        return summed(pair) / jnp.broadcast_to(total[:, pair:pair + 1], (per, LANES))

    for pair in range(0, share, 2):
        both = jnp.concatenate([result(pair), result(pair + 1)], axis=0)
        work[pair * per:(pair + 2) * per, :] = both.astype(BF16)
    rest = jnp.concatenate([peak, total], axis=0)
    lane = lax.broadcasted_iota(jnp.int32, rest.shape, 1)
    packed = jnp.zeros_like(rest)
    for i in range(3):
        part = rest.astype(BF16).astype(F32)
        rest = rest - part
        here = (lane >= i * FIELD) & (lane < (i + 1) * FIELD)
        packed = jnp.where(here, pltpu.roll(part, i * FIELD, 1) if i else part, packed)
    work[share * per:(share + 2) * per, :] = packed.astype(BF16)
    copy = pltpu.make_async_copy(work, out, sem)
    copy.start()
    copy.wait()


def join_kernel(levels, parts, held, me_ref, *refs):
    ins, refs = refs[:parts], refs[parts + held:]
    out, sem = refs[0], refs[1 + held]
    mine = me_ref[0] // levels
    copies = [
        pltpu.make_async_copy(ins[part], out.at[jnp.bitwise_xor(mine, part)], sem.at[part])
        for part in range(parts)
    ]
    for copy in copies:
        copy.start()
    for copy in copies:
        copy.wait()


def finish_kernel(share, per, levels, parts, me_ref, stats_ref, *refs):
    ins, out, mass_ref = refs[:levels], refs[levels], refs[levels + 1]
    mine = lax.rem(me_ref[0], levels)
    base = share * per
    lane = lax.broadcasted_iota(jnp.int32, (per, LANES), 1)
    mass = jnp.zeros((per, LANES), F32)
    for level in range(levels):
        step = jnp.bitwise_xor(mine, level)
        peak = jnp.zeros((per, LANES), F32)
        total = jnp.ones((per, LANES), F32)
        for part in range(parts):
            out[step, part * base:(part + 1) * base, :] = ins[level][part, :base, :]
            packed = ins[level][part, base:base + 2 * per, :].astype(F32)
            fields = [pltpu.roll(packed, (part * share - i * FIELD) % LANES, 1) for i in (2, 1)]
            first = (part * share) % LANES
            fields.append(pltpu.roll(packed, first, 1) if first else packed)
            both = functools.reduce(jnp.add, fields)
            here = (lane >= part * share) & (lane < (part + 1) * share)
            peak = jnp.where(here, both[:per], peak)
            total = jnp.where(here, both[per:], total)
        own_peak = stats_ref[0, level * per:(level + 1) * per, :]
        own_total = stats_ref[1, level * per:(level + 1) * per, :]
        coefficient = jnp.exp(jnp.minimum(own_peak - peak, 0.0)) / total
        mass = mass + own_total * coefficient
    mass_ref[...] = jnp.sum(mass, axis=0, keepdims=True)


def hold_kernel(*refs):
    pass


def place_kernel(devices, tiles_dev, group, me_ref, table, dest_ref, k_own, v_own, *refs):
    got, (k_ref, v_ref, sem) = refs[:devices - 1], refs[devices - 1:]
    heads, span = k_ref.shape[1], k_ref.shape[2]
    tile = span // tiles_dev
    me = me_ref[0]
    for offset in range(devices):
        source = lax.rem(me + devices - offset, devices)
        for k in range(group):
            pair = table[offset * group + k]
            row, head = pair // heads, lax.rem(pair, heads)

            @pl.when(k < table[devices * group + offset])
            def _():
                for which, (own, ref) in enumerate(((k_own, k_ref), (v_own, v_ref))):
                    src = got[offset - 1].at[k, which] if offset else own.at[row, head]
                    if tiles_dev == 1:
                        pltpu.make_async_copy(src, ref.at[row, head], sem.at[which]).start()
                        continue
                    for j in range(tiles_dev):
                        target = lax.rem(dest_ref[row, head, source * tiles_dev + j], tiles_dev)
                        dst = ref.at[row, head, pl.ds(pl.multiple_of(target * tile, tile), tile)]
                        pltpu.make_async_copy(src.at[pl.ds(j * tile, tile)], dst, sem.at[which]).start()
    pltpu.make_async_copy(k_ref, k_ref, sem.at[0]).wait()
    pltpu.make_async_copy(v_ref, v_ref, sem.at[1]).wait()


def phases_of(devices):
    phases = [[], [], [], [], []]
    for offset in range(1, devices):
        reach = min(offset, devices - offset) * 16 / devices
        if reach == 8:
            phases[0].append(offset)
        elif reach == 4:
            phases[1].append(offset)
        elif reach > 6:
            phases[2].append(offset)
        elif reach > 5:
            phases[3].append(offset)
        else:
            phases[4].append(offset)
    return [sorted(x, key=lambda o: (-min(o, devices - o), o)) for x in phases]


def local(queries, key_cache, value_cache, row_lengths, kept_tiles, tile_dest):
    devices = lax.axis_size("ctx")
    rows, heads, span, width = key_cache.shape
    steps, _, q_heads, _ = queries.shape
    per = q_heads // heads
    pairs = rows * heads
    tiles_dev = tile_dest.shape[2] // devices
    group = -(-pairs // devices)
    levels = steps
    parts = devices // levels
    two_level = (
        devices == levels * parts and pairs % (2 * parts) == 0
        and parts & (parts - 1) == 0 and levels & (levels - 1) == 0
    )
    share = pairs // parts if two_level else 0
    phases = phases_of(devices)
    later = [offset for phase in phases[1:] for offset in phase]
    buf_type = jax.ShapeDtypeStruct((group, 2, span, width), BF16)
    got = {}

    def move(x, offset):
        return lax.ppermute(x, "ctx", [(i, (i + offset) % devices) for i in range(devices)])

    def send(offsets, bufs):
        for offset, buf in zip(offsets, bufs):
            got[offset] = move(buf, offset)

    me = lax.axis_index("ctx").astype(jnp.int32).reshape(1)
    kept = jnp.transpose(kept_tiles, (1, 0, 2))
    chunk_rows = rows * q_heads + 2 * per

    table, *bufs = pl.pallas_call(
        functools.partial(stage_kernel, devices, tiles_dev, group, phases[0]),
        out_shape=[jax.ShapeDtypeStruct((devices * (group + 1),), jnp.int32)] + [buf_type] * len(phases[0]),
        in_specs=[HBM, HBM, HBM],
        out_specs=[SMEM] + [HBM] * len(phases[0]),
        scratch_shapes=[
            pltpu.SMEM(tile_dest.shape, jnp.int32),
            pltpu.SemaphoreType.DMA,
            pltpu.SemaphoreType.DMA((len(phases[0]),)),
        ],
        compiler_params=WHOLE,
        cost_estimate=cost(1_000, 2_000_000),
        name="stage",
    )(tile_dest, key_cache, value_cache)
    send(phases[0], bufs)

    outs = pl.pallas_call(
        functools.partial(attend_kernel, devices, tiles_dev, group, levels, later),
        out_shape=[buf_type] * len(later) + [
            jax.ShapeDtypeStruct((2, steps * per, LANES), F32),
        ] + [jax.ShapeDtypeStruct((chunk_rows, width), F32)] * levels,
        in_specs=[SMEM, SMEM, HBM, HBM, HBM, HBM, HBM],
        out_specs=[HBM] * len(later) + [VMEM] + [HBM] * levels,
        scratch_shapes=[
            pltpu.VMEM((rows, steps, q_heads, width), BF16),
            pltpu.VMEM(key_cache.shape, BF16),
            pltpu.VMEM(value_cache.shape, BF16),
            pltpu.VMEM((levels, chunk_rows, width), F32),
            pltpu.SMEM(row_lengths.shape, jnp.int32),
            pltpu.SMEM(kept.shape, jnp.int32),
            pltpu.SemaphoreType.DMA((3, rows)),
            pltpu.SemaphoreType.DMA((2,)),
            pltpu.SemaphoreType.DMA((len(later),)),
            pltpu.SemaphoreType.DMA((levels,)),
        ],
        compiler_params=WHOLE,
        cost_estimate=cost(100_000_000, 12_000_000),
        name="attend",
    )(me, table, row_lengths, kept, queries, key_cache, value_cache)
    bufs = dict(zip(later, outs))
    stats, chunks = outs[len(later)], outs[len(later) + 1:]
    outs = pl.pallas_call(
        hold_kernel,
        out_shape=[jax.ShapeDtypeStruct(x.shape, F32) for x in chunks] + [buf_type] * len(phases[1]),
        in_specs=[HBM] * (levels + len(phases[1])) + [ANY] * len(phases[0]),
        out_specs=[HBM] * (levels + len(phases[1])),
        input_output_aliases={i: i for i in range(levels + len(phases[1]))},
        compiler_params=WHOLE,
        cost_estimate=cost(1_000, 1_000),
        name="hold",
    )(*chunks, *[bufs[offset] for offset in phases[1]], *[got[offset] for offset in phases[0]])
    chunks = outs[:levels]
    send(phases[1], outs[levels:])

    if two_level:
        def near(x, level):
            perm = [(i, i // levels * levels + (i % levels ^ level)) for i in range(devices)]
            return lax.ppermute(x, "ctx", perm)

        def far(x, part):
            perm = [(i, (i // levels ^ part) * levels + i % levels) for i in range(devices)]
            return lax.ppermute(x, "ctx", perm)

        def step(kernel, name, ins, in_specs, out_shape, scratch, phase, bytes_accessed):
            held = [bufs[offset] for offset in phase]
            results = pl.pallas_call(
                kernel,
                out_shape=out_shape + [buf_type] * len(held),
                in_specs=in_specs + [HBM] * len(held),
                out_specs=[HBM] * (len(out_shape) + len(held)),
                input_output_aliases={len(ins) + i: len(out_shape) + i for i in range(len(held))},
                scratch_shapes=scratch,
                compiler_params=WHOLE,
                cost_estimate=cost(1_000_000, bytes_accessed),
                name=name,
            )(*ins, *held)
            return results[:len(out_shape)], results[len(out_shape):]

        part_rows = share * per + 2 * per
        message_rows = share * per + 2 * per
        part_type = jax.ShapeDtypeStruct((part_rows, width), F32)
        message_type = jax.ShapeDtypeStruct((message_rows, width), BF16)
        joined_type = jax.ShapeDtypeStruct((parts, message_rows, width), BF16)

        arrived = [chunks[0]] + [near(chunks[i], i) for i in range(1, levels)]
        pieces, held = step(
            functools.partial(near_kernel, pairs, per, levels, parts, len(phases[2])), "near",
            [me, *arrived], [SMEM] + [VMEM] * levels, [part_type] * parts,
            [pltpu.VMEM((parts, part_rows, width), F32), pltpu.SemaphoreType.DMA((parts,))],
            phases[2], 2_000_000,
        )
        arrived = [pieces[0]] + [far(pieces[i], i) for i in range(1, parts)]
        send(phases[2], held)
        (message,), held = step(
            functools.partial(far_kernel, share, per, parts, len(phases[3])), "far",
            arrived, [VMEM] * parts, [message_type],
            [pltpu.VMEM((message_rows, width), BF16), pltpu.SemaphoreType.DMA],
            phases[3], 500_000,
        )
        arrived = [message] + [far(message, i) for i in range(1, parts)]
        send(phases[3], held)
        (joined,), held = step(
            functools.partial(join_kernel, levels, parts, len(phases[4])), "join",
            [me, *arrived], [SMEM] + [ANY] * parts, [joined_type],
            [pltpu.SemaphoreType.DMA((parts,))],
            phases[4], 500_000,
        )
        arrived = [joined] + [near(joined, i) for i in range(1, levels)]
        send(phases[4], held)
        attn_out, mass = pl.pallas_call(
            functools.partial(finish_kernel, share, per, levels, parts),
            out_shape=[
                jax.ShapeDtypeStruct((steps, rows * q_heads, width), BF16),
                jax.ShapeDtypeStruct((1, LANES), F32),
            ],
            in_specs=[SMEM, VMEM] + [VMEM] * levels,
            out_specs=[VMEM, VMEM],
            compiler_params=PARAMS,
            cost_estimate=cost(1_000, 1_000_000),
            name="finish",
        )(me, stats, *arrived)
        attn_out = attn_out.reshape(queries.shape)
        tile_mass = mass[0, :pairs].reshape(rows, heads, 1)
    else:
        for phase in phases[2:]:
            send(phase, [bufs[offset] for offset in phase])
        mine = lax.rem(me[0], levels)
        order = jnp.bitwise_xor(mine, jnp.arange(levels))
        stacked = jnp.stack(chunks)[:, :rows * q_heads][order].reshape(steps, rows, heads, per, width)

        def by_pair(x):
            x = x.reshape(levels, per, LANES)[order][:, :, :pairs].reshape(steps, per, rows, heads)
            return jnp.transpose(x, (0, 2, 3, 1))

        peak, total = by_pair(stats[0]), by_pair(stats[1])
        factor = jnp.exp(peak - lax.pmax(peak, "ctx"))
        denominator, summed = lax.psum((total * factor, stacked * factor[..., None]), "ctx")
        attn_out = (summed / denominator[..., None]).astype(BF16).reshape(queries.shape)
        tile_mass = jnp.sum(total * factor / denominator, axis=(0, 3))[:, :, None]

    moved_keys, moved_values = pl.pallas_call(
        functools.partial(place_kernel, devices, tiles_dev, group),
        out_shape=[
            jax.ShapeDtypeStruct(key_cache.shape, BF16),
            jax.ShapeDtypeStruct(value_cache.shape, BF16),
        ],
        in_specs=[SMEM, SMEM, SMEM, HBM, HBM] + [ANY] * (devices - 1),
        out_specs=[HBM, HBM],
        scratch_shapes=[pltpu.SemaphoreType.DMA((2,))],
        compiler_params=PARAMS,
        cost_estimate=cost(1_000, 6_000_000),
        name="place",
    )(me, table, tile_dest, key_cache, value_cache, *[got[offset] for offset in range(1, devices)])
    return attn_out, tile_mass, moved_keys, moved_values


def solution(mesh):
    in_specs = (
        P(None, "grp", None, None),
        P("grp", None, "ctx", None),
        P("grp", None, "ctx", None),
        P("grp"),
        P(None, "grp", None),
        P("grp", None, None),
    )
    out_specs = (
        P(None, "grp", None, None),
        P("grp", None, "ctx"),
        P("grp", None, "ctx", None),
        P("grp", None, "ctx", None),
    )
    return jax.shard_map(local, mesh=mesh, in_specs=in_specs, out_specs=out_specs, check_vma=False)
```

```python
import functools

import jax
import jax.numpy as jnp
from jax import lax
from jax.experimental import pallas as pl
from jax.experimental.pallas import tpu as pltpu
from jax.sharding import PartitionSpec as P

absent_score = -1e30
LANES = 128
FIELD = 32
F32 = jnp.float32
BF16 = jnp.bfloat16
VMEM = pl.BlockSpec(memory_space=pltpu.VMEM)
SMEM = pl.BlockSpec(memory_space=pltpu.SMEM)
HBM = pl.BlockSpec(memory_space=pltpu.HBM)
ANY = pl.BlockSpec(memory_space=pl.ANY)
PARAMS = pltpu.CompilerParams(vmem_limit_bytes=16 * 1024 * 1024)
WHOLE = pltpu.CompilerParams(vmem_limit_bytes=62 * 1024 * 1024)


COST = pl.CostEstimate(flops=1000, bytes_accessed=1000, transcendentals=0)


def each_slot(dest, row, counts, tiles_dev, devices, group, body):
    def step(head, carry):
        offset = lax.rem(dest[row, head, 0] // tiles_dev, devices)
        rank = counts[offset]
        counts[offset] = rank + 1
        body(head, offset, jnp.minimum(rank, group - 1))
        return carry

    lax.fori_loop(0, dest.shape[1], step, 0)


def clear(counts):
    def step(i, carry):
        counts[i] = 0
        return carry

    lax.fori_loop(0, counts.shape[0], step, 0)


def stage_kernel(
    devices, tiles_dev, group, me_ref, dest_hbm, k_ref, v_ref, buf, me_out, k_vm, v_vm, dest, counts, sem, load_sem
):
    rows = k_ref.shape[0]
    small = pltpu.make_async_copy(dest_hbm, dest, sem.at[0])
    small.start()
    loads = []
    for row in range(rows):
        for which, (src, dst) in enumerate(((k_ref, k_vm), (v_ref, v_vm))):
            copy = pltpu.make_async_copy(src.at[row], dst.at[row], load_sem.at[which, row])
            copy.start()
            loads.append(copy)
    me = me_ref[0]
    me_out[0] = me
    clear(counts)
    small.wait()
    for row in range(rows):
        loads[2 * row].wait()
        loads[2 * row + 1].wait()

        def send(head, offset, rank):
            slot = lax.rem(me + offset, devices) * group + rank
            pltpu.make_async_copy(k_vm.at[row, head], buf.at[slot, 0], sem.at[1]).start()
            pltpu.make_async_copy(v_vm.at[row, head], buf.at[slot, 1], sem.at[2]).start()

        each_slot(dest, row, counts, tiles_dev, devices, group, send)
    pltpu.make_async_copy(k_ref, k_vm, sem.at[1]).wait()
    pltpu.make_async_copy(v_ref, v_vm, sem.at[2]).wait()


def attend_kernel(
    tiles_dev, levels,
    me_ref, len_hbm, kept_hbm, q_hbm, k_ref, v_ref,
    stats_ref, *rest,
):
    chunks = rest[:levels]
    q_vm, k_vm, v_vm, work, len_ref, kept_ref, load_sem, small_sem, out_sem = rest[levels:]
    rows, heads, span, width = k_ref.shape
    steps, _, q_heads, _ = q_hbm.shape
    per = q_heads // heads
    tile = span // tiles_dev
    me = me_ref[0]

    small = [
        pltpu.make_async_copy(len_hbm, len_ref, small_sem.at[0]),
        pltpu.make_async_copy(kept_hbm, kept_ref, small_sem.at[1]),
    ]
    for copy in small:
        copy.start()
    loads = []
    for row in range(rows):
        copies = [
            pltpu.make_async_copy(q_hbm.at[:, row], q_vm.at[row], load_sem.at[0, row]),
            pltpu.make_async_copy(k_ref.at[row], k_vm.at[row], load_sem.at[1, row]),
            pltpu.make_async_copy(v_ref.at[row], v_vm.at[row], load_sem.at[2, row]),
        ]
        for copy in copies:
            copy.start()
        loads.append(copies)
    for copy in small:
        copy.wait()

    lane = lax.broadcasted_iota(jnp.int32, (per, tile), 1)
    pair_lane = lax.broadcasted_iota(jnp.int32, (steps * per, LANES), 1)
    peaks = jnp.full((steps * per, LANES), absent_score, F32)
    totals = jnp.zeros((steps * per, LANES), F32)
    each = steps // levels
    order = [
        jnp.bitwise_xor(lax.rem(me, levels), level) * each + i for level in range(levels) for i in range(each)
    ]
    scale = width ** -0.5
    block = steps * per
    for row in range(rows):
        for copy in loads[row]:
            copy.wait()
        queries = [q_vm[row, step].astype(F32) for step in order]
        live = []
        for step in order:
            parts = []
            for j in range(tiles_dev):
                column = me * tiles_dev + j
                limit = jnp.where(kept_ref[row, step, column] > 0, len_ref[row] - column * tile, 0)
                parts.append(lane < limit)
            live.append(parts[0] if tiles_dev == 1 else jnp.concatenate(parts, axis=1))
        live = jnp.concatenate(live * heads, axis=0)
        scores = []
        for head in range(heads):
            q = jnp.concatenate([x[head * per:(head + 1) * per] for x in queries], axis=0).astype(BF16)
            scores.append(lax.dot_general(
                q, k_vm[row, head], (((1,), (1,)), ((), ())), preferred_element_type=F32
            ))
        scores = jnp.concatenate(scores, axis=0) * scale
        peak = jnp.max(jnp.where(live, scores, absent_score), axis=1, keepdims=True)
        weights = jnp.where(live, jnp.exp(scores - peak), 0.0)
        total = jnp.sum(weights, axis=1, keepdims=True)
        rounded = weights.astype(BF16)
        for head in range(heads):
            out = jnp.dot(
                rounded[head * block:(head + 1) * block], v_vm[row, head], preferred_element_type=F32
            )
            pair = row * heads + head
            for i in range(steps):
                at = (i % each * rows * heads + pair) * per
                work[i // each, at:at + per, :] = out[i * per:(i + 1) * per]
            here = pair_lane == pair
            peaks = jnp.where(here, peak[head * block:(head + 1) * block], peaks)
            totals = jnp.where(here, total[head * block:(head + 1) * block], totals)
    for i in range(steps):
        base = each * rows * q_heads + i % each * 2 * per
        work[i // each, base:base + per, :] = peaks[i * per:(i + 1) * per]
        work[i // each, base + per:base + 2 * per, :] = totals[i * per:(i + 1) * per]
    stats_ref[0] = peaks
    stats_ref[1] = totals
    copies = [
        pltpu.make_async_copy(work.at[level], chunks[level], out_sem.at[level]) for level in range(levels)
    ]
    for copy in copies:
        copy.start()
    for copy in copies:
        copy.wait()


def merge(refs, first, base, pairs, per):
    peaks = [ref[base:base + per, :] for ref in refs]
    totals = [ref[base + per:base + 2 * per, :] for ref in refs]
    peak = functools.reduce(jnp.maximum, peaks)
    factors = [jnp.exp(x - peak) for x in peaks]
    total = functools.reduce(jnp.add, [f * t for f, t in zip(factors, totals)])

    def summed(pair):
        at = first + pair * per
        return functools.reduce(jnp.add, [
            jnp.broadcast_to(f[:, pair:pair + 1], (per, ref.shape[1])) * ref[at:at + per, :]
            for f, ref in zip(factors, refs)
        ])

    return peak, total, summed


def near_kernel(pairs, per, each, levels, parts, me_ref, *refs):
    ins, outs, (work, sem) = refs[:levels], refs[levels:levels + parts], refs[levels + parts:]
    share = pairs * each // parts
    base = share * per
    for i in range(each):
        peak, total, summed = merge(ins, i * pairs * per, (each * pairs + 2 * i) * per, pairs, per)
        for pair in range(pairs):
            unit = i * pairs + pair
            work[unit // share, unit % share * per:(unit % share + 1) * per, :] = summed(pair)
        for start in range(0, pairs, share):
            part = (i * pairs + start) // share
            shift = (LANES - start) % LANES
            work[part, base:base + per, :] = pltpu.roll(peak, shift, 1) if shift else peak
            work[part, base + per:base + 2 * per, :] = pltpu.roll(total, shift, 1) if shift else total
    mine = me_ref[0] // levels
    copies = [
        pltpu.make_async_copy(work.at[jnp.bitwise_xor(mine, part)], outs[part], sem.at[part])
        for part in range(parts)
    ]
    for copy in copies:
        copy.start()
    for copy in copies:
        copy.wait()


def far_kernel(share, per, parts, *refs):
    ins, (out, work, sem) = refs[:parts], refs[parts:]
    peak, total, summed = merge(ins, 0, share * per, share, per)
    lane = lax.broadcasted_iota(jnp.int32, peak.shape, 1)
    total = jnp.where(lane < share, total, 1.0)
    peak = jnp.where(lane < share, peak, 0.0)

    def result(pair):
        return summed(pair) / jnp.broadcast_to(total[:, pair:pair + 1], (per, LANES))

    for pair in range(0, share, 2):
        both = jnp.concatenate([result(pair), result(pair + 1)], axis=0)
        work[pair * per:(pair + 2) * per, :] = both.astype(BF16)
    rest = jnp.concatenate([peak, total], axis=0)
    lane = lax.broadcasted_iota(jnp.int32, rest.shape, 1)
    packed = jnp.zeros_like(rest)
    for i in range(3):
        part = rest.astype(BF16).astype(F32)
        rest = rest - part
        here = (lane >= i * FIELD) & (lane < (i + 1) * FIELD)
        packed = jnp.where(here, pltpu.roll(part, i * FIELD, 1) if i else part, packed)
    work[share * per:(share + 2) * per, :] = packed.astype(BF16)
    copy = pltpu.make_async_copy(work, out, sem)
    copy.start()
    copy.wait()


def join_kernel(levels, parts, me_ref, *refs):
    ins, (out, sem) = refs[:parts], refs[parts:]
    mine = me_ref[0] // levels
    copies = [
        pltpu.make_async_copy(ins[part], out.at[jnp.bitwise_xor(mine, part)], sem.at[part])
        for part in range(parts)
    ]
    for copy in copies:
        copy.start()
    for copy in copies:
        copy.wait()


def finish_kernel(pairs, share, per, each, levels, parts, me_ref, stats_ref, *refs):
    ins, out, mass_ref = refs[:levels], refs[levels], refs[levels + 1]
    mine = lax.rem(me_ref[0], levels)
    base = share * per
    lane = lax.broadcasted_iota(jnp.int32, (per, LANES), 1)
    mass = jnp.zeros((per, LANES), F32)
    for level in range(levels):
        for i in range(each):
            step = jnp.bitwise_xor(mine, level) * each + i
            peak = jnp.zeros((per, LANES), F32)
            total = jnp.ones((per, LANES), F32)
            for start in range(0, pairs, share):
                part = (i * pairs + start) // share
                out[step, start * per:start * per + base, :] = ins[level][part, :base, :]
                packed = ins[level][part, base:base + 2 * per, :].astype(F32)
                fields = [pltpu.roll(packed, (start - field * FIELD) % LANES, 1) for field in (2, 1)]
                fields.append(pltpu.roll(packed, start, 1) if start else packed)
                both = functools.reduce(jnp.add, fields)
                here = (lane >= start) & (lane < start + share)
                peak = jnp.where(here, both[:per], peak)
                total = jnp.where(here, both[per:], total)
            at = (level * each + i) * per
            coefficient = jnp.exp(jnp.minimum(stats_ref[0, at:at + per, :] - peak, 0.0)) / total
            mass = mass + stats_ref[1, at:at + per, :] * coefficient
    mass_ref[...] = jnp.sum(mass, axis=0, keepdims=True)


def place_kernel(
    devices, tiles_dev, group, me_ref, dest_hbm, got_ref, k_ref, v_ref, got_vm, dest, counts, pair_of, sem, load_sem
):
    rows, heads, span, _ = k_ref.shape
    tile = span // tiles_dev
    small = pltpu.make_async_copy(dest_hbm, dest, sem.at[2])
    small.start()
    loads = []
    for source in range(devices):
        part = pl.ds(source * group, group)
        copy = pltpu.make_async_copy(got_ref.at[part], got_vm.at[part], load_sem.at[source])
        copy.start()
        loads.append(copy)
    me = me_ref[0]
    clear(counts)

    def empty(i, carry):
        pair_of[i] = -1
        return carry

    lax.fori_loop(0, devices * group, empty, 0)
    small.wait()
    for row in range(rows):
        def note(head, offset, rank):
            pair_of[lax.rem(me + devices - offset, devices) * group + rank] = row * heads + head

        each_slot(dest, row, counts, tiles_dev, devices, group, note)
    for source in range(devices):
        loads[source].wait()
        for slot in range(source * group, (source + 1) * group):
            pair = pair_of[slot]

            @pl.when(pair >= 0)
            def _():
                row, head = pair // heads, lax.rem(pair, heads)
                for which, ref in enumerate((k_ref, v_ref)):
                    for j in range(tiles_dev):
                        if tiles_dev == 1:
                            src, dst = got_vm.at[slot, which], ref.at[row, head]
                        else:
                            target = lax.rem(dest[row, head, source * tiles_dev + j], tiles_dev)
                            src = got_vm.at[slot, which, pl.ds(j * tile, tile)]
                            dst = ref.at[row, head, pl.ds(pl.multiple_of(target * tile, tile), tile)]
                        pltpu.make_async_copy(src, dst, sem.at[which]).start()
    pltpu.make_async_copy(k_ref, k_ref, sem.at[0]).wait()
    pltpu.make_async_copy(v_ref, v_ref, sem.at[1]).wait()


def local(queries, key_cache, value_cache, row_lengths, kept_tiles, tile_dest):
    devices = lax.axis_size("ctx")
    rows, heads, span, width = key_cache.shape
    steps, _, q_heads, _ = queries.shape
    per = q_heads // heads
    pairs = rows * heads
    tiles_dev = tile_dest.shape[2] // devices
    group = -(-pairs // devices)
    levels = 2
    each = steps // levels
    parts = devices // levels
    two_level = (
        devices == levels * parts and steps == levels * each and parts & (parts - 1) == 0
        and pairs * each % parts == 0 and pairs % max(pairs * each // parts, 1) == 0
    )
    share = pairs * each // parts
    two_level = two_level and share % 2 == 0 and share <= FIELD and pairs <= LANES

    me = lax.axis_index("ctx").astype(jnp.int32).reshape(1)
    kept = jnp.transpose(kept_tiles, (1, 0, 2))
    chunk_rows = each * (rows * q_heads + 2 * per)

    buf, me_next = pl.pallas_call(
        functools.partial(stage_kernel, devices, tiles_dev, group),
        out_shape=[
            jax.ShapeDtypeStruct((devices * group, 2, span, width), BF16),
            jax.ShapeDtypeStruct((1,), jnp.int32),
        ],
        in_specs=[SMEM, HBM, HBM, HBM],
        out_specs=[HBM, SMEM],
        scratch_shapes=[
            pltpu.VMEM(key_cache.shape, BF16),
            pltpu.VMEM(value_cache.shape, BF16),
            pltpu.SMEM(tile_dest.shape, jnp.int32),
            pltpu.SMEM((devices,), jnp.int32),
            pltpu.SemaphoreType.DMA((3,)),
            pltpu.SemaphoreType.DMA((2, rows)),
        ],
        compiler_params=WHOLE,
        cost_estimate=COST,
        name="stage",
    )(me, tile_dest, key_cache, value_cache)
    got = lax.all_to_all(buf, "ctx", split_axis=0, concat_axis=0, tiled=True)

    stats, *chunks = pl.pallas_call(
        functools.partial(attend_kernel, tiles_dev, levels),
        out_shape=[
            jax.ShapeDtypeStruct((2, steps * per, LANES), F32),
        ] + [jax.ShapeDtypeStruct((chunk_rows, width), F32)] * levels,
        in_specs=[SMEM, HBM, HBM, HBM, HBM, HBM],
        out_specs=[VMEM] + [HBM] * levels,
        scratch_shapes=[
            pltpu.VMEM((rows, steps, q_heads, width), BF16),
            pltpu.VMEM(key_cache.shape, BF16),
            pltpu.VMEM(value_cache.shape, BF16),
            pltpu.VMEM((levels, chunk_rows, width), F32),
            pltpu.SMEM(row_lengths.shape, jnp.int32),
            pltpu.SMEM(kept.shape, jnp.int32),
            pltpu.SemaphoreType.DMA((3, rows)),
            pltpu.SemaphoreType.DMA((2,)),
            pltpu.SemaphoreType.DMA((levels,)),
        ],
        compiler_params=WHOLE,
        cost_estimate=COST,
        name="attend",
    )(me_next, row_lengths, kept, queries, key_cache, value_cache)

    if two_level:
        def near(x, level):
            perm = [(i, i // levels * levels + (i % levels ^ level)) for i in range(devices)]
            return lax.ppermute(x, "ctx", perm)

        def far(x, part):
            perm = [(i, (i // levels ^ part) * levels + i % levels) for i in range(devices)]
            return lax.ppermute(x, "ctx", perm)

        part_rows = share * per + 2 * per
        arrived = [chunks[0]] + [near(chunks[i], i) for i in range(1, levels)]
        pieces = pl.pallas_call(
            functools.partial(near_kernel, pairs, per, each, levels, parts),
            out_shape=[jax.ShapeDtypeStruct((part_rows, width), F32)] * parts,
            in_specs=[SMEM] + [VMEM] * levels,
            out_specs=[HBM] * parts,
            scratch_shapes=[pltpu.VMEM((parts, part_rows, width), F32), pltpu.SemaphoreType.DMA((parts,))],
            compiler_params=WHOLE,
            cost_estimate=COST,
            name="near",
        )(me, *arrived)
        arrived = [pieces[0]] + [far(pieces[i], i) for i in range(1, parts)]
        message = pl.pallas_call(
            functools.partial(far_kernel, share, per, parts),
            out_shape=jax.ShapeDtypeStruct((part_rows, width), BF16),
            in_specs=[VMEM] * parts,
            out_specs=HBM,
            scratch_shapes=[pltpu.VMEM((part_rows, width), BF16), pltpu.SemaphoreType.DMA],
            compiler_params=WHOLE,
            cost_estimate=COST,
            name="far",
        )(*arrived)
        arrived = [message] + [far(message, i) for i in range(1, parts)]
        joined = pl.pallas_call(
            functools.partial(join_kernel, levels, parts),
            out_shape=jax.ShapeDtypeStruct((parts, part_rows, width), BF16),
            in_specs=[SMEM] + [VMEM] * parts,
            out_specs=HBM,
            scratch_shapes=[pltpu.SemaphoreType.DMA((parts,))],
            compiler_params=WHOLE,
            cost_estimate=COST,
            name="join",
        )(me, *arrived)
        arrived = [joined] + [near(joined, i) for i in range(1, levels)]
        attn_out, mass = pl.pallas_call(
            functools.partial(finish_kernel, pairs, share, per, each, levels, parts),
            out_shape=[
                jax.ShapeDtypeStruct((steps, rows * q_heads, width), BF16),
                jax.ShapeDtypeStruct((1, LANES), F32),
            ],
            in_specs=[SMEM, VMEM] + [VMEM] * levels,
            out_specs=[VMEM, VMEM],
            compiler_params=PARAMS,
            cost_estimate=COST,
            name="finish",
        )(me, stats, *arrived)
        attn_out = attn_out.reshape(queries.shape)
        tile_mass = mass[0, :pairs].reshape(rows, heads, 1)
    else:
        order = jnp.bitwise_xor(lax.rem(me[0], levels), jnp.arange(levels))
        stacked = jnp.stack(chunks)[:, :each * rows * q_heads][order].reshape(steps, rows, heads, per, width)

        def by_pair(x):
            x = x.reshape(levels, each * per, LANES)[order][:, :, :pairs].reshape(steps, per, rows, heads)
            return jnp.transpose(x, (0, 2, 3, 1))

        peak, total = by_pair(stats[0]), by_pair(stats[1])
        factor = jnp.exp(peak - lax.pmax(peak, "ctx"))
        denominator, summed = lax.psum((total * factor, stacked * factor[..., None]), "ctx")
        attn_out = (summed / denominator[..., None]).astype(BF16).reshape(queries.shape)
        tile_mass = jnp.sum(total * factor / denominator, axis=(0, 3))[:, :, None]

    moved_keys, moved_values = pl.pallas_call(
        functools.partial(place_kernel, devices, tiles_dev, group),
        out_shape=[
            jax.ShapeDtypeStruct(key_cache.shape, BF16),
            jax.ShapeDtypeStruct(value_cache.shape, BF16),
        ],
        in_specs=[SMEM, HBM, HBM],
        out_specs=[HBM, HBM],
        scratch_shapes=[
            pltpu.VMEM(got.shape, BF16),
            pltpu.SMEM(tile_dest.shape, jnp.int32),
            pltpu.SMEM((devices,), jnp.int32),
            pltpu.SMEM((devices * group,), jnp.int32),
            pltpu.SemaphoreType.DMA((3,)),
            pltpu.SemaphoreType.DMA((devices,)),
        ],
        compiler_params=WHOLE,
        cost_estimate=COST,
        name="place",
    )(me, tile_dest, got)
    return attn_out, tile_mass, moved_keys, moved_values


def solution(mesh):
    in_specs = (
        P(None, "grp", None, None),
        P("grp", None, "ctx", None),
        P("grp", None, "ctx", None),
        P("grp"),
        P(None, "grp", None),
        P("grp", None, None),
    )
    out_specs = (
        P(None, "grp", None, None),
        P("grp", None, "ctx"),
        P("grp", None, "ctx", None),
        P("grp", None, "ctx", None),
    )
    return jax.shard_map(local, mesh=mesh, in_specs=in_specs, out_specs=out_specs, check_vma=False)
```

```python
import functools

import jax
import jax.numpy as jnp
from jax import lax
from jax.experimental import pallas as pl
from jax.experimental.pallas import tpu as pltpu
from jax.sharding import PartitionSpec as P

absent_score = -1e30
LANES = 128
FIELD = 32
F32 = jnp.float32
BF16 = jnp.bfloat16
VMEM = pl.BlockSpec(memory_space=pltpu.VMEM)
SMEM = pl.BlockSpec(memory_space=pltpu.SMEM)
HBM = pl.BlockSpec(memory_space=pltpu.HBM)
ANY = pl.BlockSpec(memory_space=pl.ANY)
PARAMS = pltpu.CompilerParams(vmem_limit_bytes=16 * 1024 * 1024)
WHOLE = pltpu.CompilerParams(vmem_limit_bytes=62 * 1024 * 1024)


COST = pl.CostEstimate(flops=1000, bytes_accessed=1000, transcendentals=0)


def stage_kernel(devices, group, me_ref, dest_hbm, k_ref, buf, table, k_vm, dest, counts, sem, load_sem):
    rows, heads = k_ref.shape[:2]
    small = pltpu.make_async_copy(dest_hbm, dest, sem.at[0])
    small.start()
    loads = []
    for row in range(rows):
        copy = pltpu.make_async_copy(k_ref.at[row], k_vm.at[row], load_sem.at[row])
        copy.start()
        loads.append(copy)
    me = me_ref[0]

    def clear(i, carry):
        counts[i] = 0
        for k in range(group):
            table[i * group + k] = -1
        return carry

    lax.fori_loop(0, devices, clear, 0)
    small.wait()
    for row in range(rows):
        loads[row].wait()

        def send(head, carry):
            offset = lax.rem(dest[row, head, 0], devices)
            rank = jnp.minimum(counts[offset], group - 1)
            counts[offset] = rank + 1
            table[offset * group + rank] = row * heads + head
            slot = lax.rem(me + offset, devices) * group + rank
            pltpu.make_async_copy(k_vm.at[row, head], buf.at[slot], sem.at[1]).start()
            return carry

        lax.fori_loop(0, heads, send, 0)
    pltpu.make_async_copy(k_ref, k_vm, sem.at[1]).wait()


def attend_kernel(
    devices, group, levels,
    me_ref, table, len_hbm, kept_hbm, q_hbm, k_ref, v_ref,
    stats_ref, *rest,
):
    chunks, bufs = rest[:levels // 2], rest[levels // 2:levels // 2 + devices - 1]
    q_vm, k_vm, v_vm, work, len_ref, kept_ref, load_sem, small_sem, out_sem, buf_sem = rest[levels // 2 + devices - 1:]
    rows, heads, tile, width = k_ref.shape
    steps, _, q_heads, _ = q_hbm.shape
    per = q_heads // heads
    me = me_ref[0]

    small = [
        pltpu.make_async_copy(len_hbm, len_ref, small_sem.at[0]),
        pltpu.make_async_copy(kept_hbm, kept_ref, small_sem.at[1]),
    ]
    for copy in small:
        copy.start()
    loads = []
    for row in range(rows):
        copies = [
            pltpu.make_async_copy(q_hbm.at[:, row], q_vm.at[row], load_sem.at[0, row]),
            pltpu.make_async_copy(k_ref.at[row], k_vm.at[row], load_sem.at[1, row]),
            pltpu.make_async_copy(v_ref.at[row], v_vm.at[row], load_sem.at[2, row]),
        ]
        for copy in copies:
            copy.start()
        loads.append(copies)
    for copy in small:
        copy.wait()

    lane = lax.broadcasted_iota(jnp.int32, (per, tile), 1)
    pair_lane = lax.broadcasted_iota(jnp.int32, (steps * per, LANES), 1)
    peaks = jnp.full((steps * per, LANES), absent_score, F32)
    totals = jnp.zeros((steps * per, LANES), F32)
    order = [jnp.bitwise_xor(place_of(me), level) for level in range(levels)]
    scale = width ** -0.5
    block = steps * per
    for row in range(rows):
        for copy in loads[row]:
            copy.wait()
        queries = [q_vm[row, step].astype(F32) for step in order]
        live = []
        for step in order:
            limit = jnp.where(kept_ref[row, step, me] > 0, len_ref[row] - me * tile, 0)
            live.append(lane < limit)
        live = jnp.concatenate(live * heads, axis=0)
        scores = []
        for head in range(heads):
            q = jnp.concatenate([x[head * per:(head + 1) * per] for x in queries], axis=0).astype(BF16)
            scores.append(lax.dot_general(
                q, k_vm[row, head], (((1,), (1,)), ((), ())), preferred_element_type=F32
            ))
        scores = jnp.concatenate(scores, axis=0) * scale
        peak = jnp.max(jnp.where(live, scores, absent_score), axis=1, keepdims=True)
        weights = jnp.where(live, jnp.exp(scores - peak), 0.0)
        total = jnp.sum(weights, axis=1, keepdims=True)
        rounded = weights.astype(BF16)
        for head in range(heads):
            out = jnp.dot(
                rounded[head * block:(head + 1) * block], v_vm[row, head], preferred_element_type=F32
            )
            pair = row * heads + head
            for i in range(levels):
                work[i, pair * per:(pair + 1) * per, :] = out[i * per:(i + 1) * per]
            here = pair_lane == pair
            peaks = jnp.where(here, peak[head * block:(head + 1) * block], peaks)
            totals = jnp.where(here, total[head * block:(head + 1) * block], totals)
    base = rows * q_heads
    for i in range(levels):
        work[i, base:base + per, :] = peaks[i * per:(i + 1) * per]
        work[i, base + per:base + 2 * per, :] = totals[i * per:(i + 1) * per]
    stats_ref[0] = peaks
    stats_ref[1] = totals
    copies = [
        pltpu.make_async_copy(work.at[pl.ds(2 * i, 2)], chunks[i], out_sem.at[i]) for i in range(levels // 2)
    ]
    for copy in copies:
        copy.start()
    for offset in range(1, devices):
        for k in range(group):
            pair = jnp.maximum(table[offset * group + k], 0)
            src = v_vm.at[pair // heads, lax.rem(pair, heads)]
            pltpu.make_async_copy(src, bufs[offset - 1].at[k], buf_sem.at[offset - 1]).start()
        copies.append(pltpu.make_async_copy(bufs[offset - 1], bufs[offset - 1], buf_sem.at[offset - 1]))
    for copy in copies:
        copy.wait()


def place_of(me):
    return lax.rem(me, 2) * 2 + lax.rem(me // 2, 2)


def merge(refs, first, base, pairs, per):
    peaks = [ref[base:base + per, :] for ref in refs]
    totals = [ref[base + per:base + 2 * per, :] for ref in refs]
    peak = functools.reduce(jnp.maximum, peaks)
    factors = [jnp.exp(x - peak) for x in peaks]
    total = functools.reduce(jnp.add, [f * t for f, t in zip(factors, totals)])

    def summed(pair):
        at = first + pair * per
        return functools.reduce(jnp.add, [
            jnp.broadcast_to(f[:, pair:pair + 1], (per, ref.shape[1])) * ref[at:at + per, :]
            for f, ref in zip(factors, refs)
        ])

    return peak, total, summed


def core_kernel(pairs, per, own_ref, got_ref, *outs):
    work, sem = outs[-2:]
    base = pairs * per
    for i in range(2):
        peak, total, summed = merge([own_ref.at[i], got_ref.at[i]], 0, base, pairs, per)
        for pair in range(pairs):
            work[i, pair * per:(pair + 1) * per, :] = summed(pair)
        work[i, base:base + per, :] = peak
        work[i, base + per:base + 2 * per, :] = total
    copies = [pltpu.make_async_copy(work.at[i], outs[i], sem.at[i]) for i in range(2)]
    for copy in copies:
        copy.start()
    for copy in copies:
        copy.wait()


def near_kernel(pairs, per, levels, parts, me_ref, *refs):
    ins, outs, (work, sem) = refs[:2], refs[2:2 + parts], refs[2 + parts:]
    share = pairs // parts
    base = share * per
    peak, total, summed = merge(ins, 0, pairs * per, pairs, per)
    for part in range(parts):
        for i in range(share):
            work[part, i * per:(i + 1) * per, :] = summed(part * share + i)
        shift = (LANES - part * share) % LANES
        work[part, base:base + per, :] = pltpu.roll(peak, shift, 1) if shift else peak
        work[part, base + per:base + 2 * per, :] = pltpu.roll(total, shift, 1) if shift else total
    mine = me_ref[0] // levels
    copies = [
        pltpu.make_async_copy(work.at[jnp.bitwise_xor(mine, part)], outs[part], sem.at[part])
        for part in range(parts)
    ]
    for copy in copies:
        copy.start()
    for copy in copies:
        copy.wait()


def far_kernel(share, per, parts, *refs):
    ins, (out, work, sem) = refs[:parts], refs[parts:]
    peak, total, summed = merge(ins, 0, share * per, share, per)
    lane = lax.broadcasted_iota(jnp.int32, peak.shape, 1)
    total = jnp.where(lane < share, total, 1.0)
    peak = jnp.where(lane < share, peak, 0.0)

    def result(pair):
        return summed(pair) / jnp.broadcast_to(total[:, pair:pair + 1], (per, LANES))

    for pair in range(0, share, 2):
        both = jnp.concatenate([result(pair), result(pair + 1)], axis=0)
        work[pair * per:(pair + 2) * per, :] = both.astype(BF16)
    rest = jnp.concatenate([peak, total], axis=0)
    lane = lax.broadcasted_iota(jnp.int32, rest.shape, 1)
    packed = jnp.zeros_like(rest)
    for i in range(3):
        part = rest.astype(BF16).astype(F32)
        rest = rest - part
        here = (lane >= i * FIELD) & (lane < (i + 1) * FIELD)
        packed = jnp.where(here, pltpu.roll(part, i * FIELD, 1) if i else part, packed)
    work[share * per:(share + 2) * per, :] = packed.astype(BF16)
    copy = pltpu.make_async_copy(work, out, sem)
    copy.start()
    copy.wait()


def join_kernel(levels, parts, me_ref, *refs):
    ins, (out, sem) = refs[:parts], refs[parts:]
    mine = me_ref[0] // levels
    copies = [
        pltpu.make_async_copy(ins[part], out.at[jnp.bitwise_xor(mine, part)], sem.at[part])
        for part in range(parts)
    ]
    for copy in copies:
        copy.start()
    for copy in copies:
        copy.wait()


def finish_kernel(pairs, share, per, heads, levels, parts, me_ref, stats_ref, *refs):
    ins, out, mass_ref = refs[:levels], refs[levels], refs[levels + 1]
    base = share * per
    lane = lax.broadcasted_iota(jnp.int32, (per, LANES), 1)
    mass = jnp.zeros((per, LANES), F32)
    for level in range(levels):
        step = jnp.bitwise_xor(place_of(me_ref[0]), level)
        peak = jnp.zeros((per, LANES), F32)
        total = jnp.ones((per, LANES), F32)
        for part in range(parts):
            start = part * share
            out[step, part * base:(part + 1) * base, :] = ins[level][part, :base, :]
            packed = ins[level][part, base:base + 2 * per, :].astype(F32)
            fields = [pltpu.roll(packed, (start - field * FIELD) % LANES, 1) for field in (2, 1)]
            fields.append(pltpu.roll(packed, start, 1) if start else packed)
            both = functools.reduce(jnp.add, fields)
            here = (lane >= start) & (lane < start + share)
            peak = jnp.where(here, both[:per], peak)
            total = jnp.where(here, both[per:], total)
        at = level * per
        coefficient = jnp.exp(jnp.minimum(stats_ref[0, at:at + per, :] - peak, 0.0)) / total
        mass = mass + stats_ref[1, at:at + per, :] * coefficient
    mass = jnp.sum(mass, axis=0, keepdims=True)
    for row in range(pairs // heads):
        mass_ref[row] = mass[:, row * heads:(row + 1) * heads]


def place_keys_kernel(devices, group, me_ref, table, got_ref, k_ref, got_vm, sem, load_sem):
    heads = k_ref.shape[1]
    me = me_ref[0]
    loads = []
    for offset in range(devices):
        source = lax.rem(me + devices - offset, devices)
        part = got_ref.at[pl.ds(source * group, group)]
        copy = pltpu.make_async_copy(part, got_vm.at[pl.ds(offset * group, group)], load_sem.at[offset])
        copy.start()
        loads.append(copy)
    for offset in range(devices):
        loads[offset].wait()
        put(table, offset, group, heads, got_vm, k_ref, sem)
    pltpu.make_async_copy(k_ref, k_ref, sem).wait()


def place_values_kernel(devices, group, table, own_ref, *refs):
    got, (v_ref, got_vm, sem, load_sem) = refs[:devices - 1], refs[devices - 1:]
    heads = v_ref.shape[1]
    loads = []
    for offset in range(devices):
        if offset:
            copies = [pltpu.make_async_copy(
                got[offset - 1], got_vm.at[pl.ds(offset * group, group)], load_sem.at[offset]
            )]
        else:
            copies = []
            for k in range(group):
                pair = jnp.maximum(table[k], 0)
                src = own_ref.at[pair // heads, lax.rem(pair, heads)]
                copies.append(pltpu.make_async_copy(src, got_vm.at[k], load_sem.at[devices + k]))
        for copy in copies:
            copy.start()
        loads.append(copies)
    for offset in range(devices):
        for copy in loads[offset]:
            copy.wait()
        put(table, offset, group, heads, got_vm, v_ref, sem)
    pltpu.make_async_copy(v_ref, v_ref, sem).wait()


def put(table, offset, group, heads, got_vm, ref, sem):
    for slot in range(offset * group, (offset + 1) * group):
        pair = table[slot]

        @pl.when(pair >= 0)
        def _():
            dst = ref.at[pair // heads, lax.rem(pair, heads)]
            pltpu.make_async_copy(got_vm.at[slot], dst, sem).start()


def local(queries, key_cache, value_cache, row_lengths, kept_tiles, tile_dest):
    devices = lax.axis_size("ctx")
    rows, heads, span, width = key_cache.shape
    steps, _, q_heads, _ = queries.shape
    per = q_heads // heads
    pairs = rows * heads
    group = -(-pairs // devices)
    levels = 4
    parts = devices // levels
    two_level = devices == levels * parts and parts & (parts - 1) == 0 and pairs % (2 * parts) == 0
    share = pairs // parts
    two_level = two_level and share <= FIELD and pairs <= LANES
    assert steps == levels and tile_dest.shape[2] == devices

    me = lax.axis_index("ctx").astype(jnp.int32).reshape(1)
    kept = jnp.transpose(kept_tiles, (1, 0, 2))
    chunk_rows = rows * q_heads + 2 * per
    buf_type = jax.ShapeDtypeStruct((group, span, width), BF16)

    keys_out, table = pl.pallas_call(
        functools.partial(stage_kernel, devices, group),
        out_shape=[
            jax.ShapeDtypeStruct((devices * group, span, width), BF16),
            jax.ShapeDtypeStruct((devices * group,), jnp.int32),
        ],
        in_specs=[SMEM, HBM, HBM],
        out_specs=[HBM, SMEM],
        scratch_shapes=[
            pltpu.VMEM(key_cache.shape, BF16),
            pltpu.SMEM(tile_dest.shape, jnp.int32),
            pltpu.SMEM((devices,), jnp.int32),
            pltpu.SemaphoreType.DMA((2,)),
            pltpu.SemaphoreType.DMA((rows,)),
        ],
        compiler_params=WHOLE,
        cost_estimate=COST,
        name="stage",
    )(me, tile_dest, key_cache)
    keys_in = lax.all_to_all(keys_out, "ctx", split_axis=0, concat_axis=0, tiled=True)

    stats, *outs = pl.pallas_call(
        functools.partial(attend_kernel, devices, group, levels),
        out_shape=[
            jax.ShapeDtypeStruct((2, steps * per, LANES), F32),
        ] + [jax.ShapeDtypeStruct((2, chunk_rows, width), F32)] * 2 + [buf_type] * (devices - 1),
        in_specs=[SMEM, SMEM, HBM, HBM, HBM, HBM, HBM],
        out_specs=[VMEM] + [HBM] * (devices + 1),
        scratch_shapes=[
            pltpu.VMEM((rows, steps, q_heads, width), BF16),
            pltpu.VMEM(key_cache.shape, BF16),
            pltpu.VMEM(value_cache.shape, BF16),
            pltpu.VMEM((levels, chunk_rows, width), F32),
            pltpu.SMEM(row_lengths.shape, jnp.int32),
            pltpu.SMEM(kept.shape, jnp.int32),
            pltpu.SemaphoreType.DMA((3, rows)),
            pltpu.SemaphoreType.DMA((2,)),
            pltpu.SemaphoreType.DMA((2,)),
            pltpu.SemaphoreType.DMA((devices - 1,)),
        ],
        compiler_params=WHOLE,
        cost_estimate=COST,
        name="attend",
    )(me, table, row_lengths, kept, queries, key_cache, value_cache)
    chunks, bufs = outs[:2], outs[2:]
    values_in = [
        lax.ppermute(bufs[offset - 1], "ctx", [(i, (i + offset) % devices) for i in range(devices)])
        for offset in range(1, devices)
    ]

    if two_level:
        def flip(x, bits):
            return lax.ppermute(x, "ctx", [(i, i ^ bits) for i in range(devices)])

        part_rows = share * per + 2 * per
        block_type = jax.ShapeDtypeStruct((chunk_rows, width), F32)
        kept_block, sent_block = pl.pallas_call(
            functools.partial(core_kernel, pairs, per),
            out_shape=[block_type] * 2,
            in_specs=[VMEM, VMEM],
            out_specs=[HBM, HBM],
            scratch_shapes=[pltpu.VMEM((2, chunk_rows, width), F32), pltpu.SemaphoreType.DMA((2,))],
            compiler_params=WHOLE,
            cost_estimate=COST,
            name="core",
        )(chunks[0], flip(chunks[1], 1))
        pieces = pl.pallas_call(
            functools.partial(near_kernel, pairs, per, levels, parts),
            out_shape=[jax.ShapeDtypeStruct((part_rows, width), F32)] * parts,
            in_specs=[SMEM, VMEM, VMEM],
            out_specs=[HBM] * parts,
            scratch_shapes=[pltpu.VMEM((parts, part_rows, width), F32), pltpu.SemaphoreType.DMA((parts,))],
            compiler_params=WHOLE,
            cost_estimate=COST,
            name="near",
        )(me, kept_block, flip(sent_block, 2))
        message = pl.pallas_call(
            functools.partial(far_kernel, share, per, parts),
            out_shape=jax.ShapeDtypeStruct((part_rows, width), BF16),
            in_specs=[VMEM] * parts,
            out_specs=HBM,
            scratch_shapes=[pltpu.VMEM((part_rows, width), BF16), pltpu.SemaphoreType.DMA],
            compiler_params=WHOLE,
            cost_estimate=COST,
            name="far",
        )(pieces[0], *[flip(pieces[i], levels * i) for i in range(1, parts)])
        joined = pl.pallas_call(
            functools.partial(join_kernel, levels, parts),
            out_shape=jax.ShapeDtypeStruct((parts, part_rows, width), BF16),
            in_specs=[SMEM] + [VMEM] * parts,
            out_specs=HBM,
            scratch_shapes=[pltpu.SemaphoreType.DMA((parts,))],
            compiler_params=WHOLE,
            cost_estimate=COST,
            name="join",
        )(me, message, *[flip(message, levels * i) for i in range(1, parts)])
        other = flip(joined, 2)
        attn_out, mass = pl.pallas_call(
            functools.partial(finish_kernel, pairs, share, per, heads, levels, parts),
            out_shape=[
                jax.ShapeDtypeStruct((steps, rows * q_heads, width), BF16),
                jax.ShapeDtypeStruct((rows, 1, heads), F32),
            ],
            in_specs=[SMEM, VMEM] + [VMEM] * levels,
            out_specs=[VMEM, VMEM],
            compiler_params=PARAMS,
            cost_estimate=COST,
            name="finish",
        )(me, stats, joined, other, flip(joined, 1), flip(other, 1))
        attn_out = attn_out.reshape(queries.shape)
        tile_mass = jnp.transpose(mass, (0, 2, 1))
    else:
        order = jnp.bitwise_xor(place_of(me[0]), jnp.arange(levels))
        stacked = jnp.concatenate(chunks)[:, :rows * q_heads][order].reshape(steps, rows, heads, per, width)

        def by_pair(x):
            x = x.reshape(levels, per, LANES)[order][:, :, :pairs].reshape(steps, per, rows, heads)
            return jnp.transpose(x, (0, 2, 3, 1))

        peak, total = by_pair(stats[0]), by_pair(stats[1])
        factor = jnp.exp(peak - lax.pmax(peak, "ctx"))
        denominator, summed = lax.psum((total * factor, stacked * factor[..., None]), "ctx")
        attn_out = (summed / denominator[..., None]).astype(BF16).reshape(queries.shape)
        tile_mass = jnp.sum(total * factor / denominator, axis=(0, 3))[:, :, None]

    moved_keys = pl.pallas_call(
        functools.partial(place_keys_kernel, devices, group),
        out_shape=jax.ShapeDtypeStruct(key_cache.shape, BF16),
        in_specs=[SMEM, SMEM, HBM],
        out_specs=HBM,
        scratch_shapes=[
            pltpu.VMEM(keys_in.shape, BF16),
            pltpu.SemaphoreType.DMA,
            pltpu.SemaphoreType.DMA((devices,)),
        ],
        compiler_params=WHOLE,
        cost_estimate=COST,
        name="place_keys",
    )(me, table, keys_in)
    moved_values = pl.pallas_call(
        functools.partial(place_values_kernel, devices, group),
        out_shape=jax.ShapeDtypeStruct(value_cache.shape, BF16),
        in_specs=[SMEM] + [HBM] * devices,
        out_specs=HBM,
        scratch_shapes=[
            pltpu.VMEM(keys_in.shape, BF16),
            pltpu.SemaphoreType.DMA,
            pltpu.SemaphoreType.DMA((devices + group,)),
        ],
        compiler_params=WHOLE,
        cost_estimate=COST,
        name="place_values",
    )(table, value_cache, *values_in)
    return attn_out, tile_mass, moved_keys, moved_values


def solution(mesh):
    in_specs = (
        P(None, "grp", None, None),
        P("grp", None, "ctx", None),
        P("grp", None, "ctx", None),
        P("grp"),
        P(None, "grp", None),
        P("grp", None, None),
    )
    out_specs = (
        P(None, "grp", None, None),
        P("grp", None, "ctx"),
        P("grp", None, "ctx", None),
        P("grp", None, "ctx", None),
    )
    return jax.shard_map(local, mesh=mesh, in_specs=in_specs, out_specs=out_specs, check_vma=False)
```

```python
import functools

import jax
import jax.numpy as jnp
from jax import lax
from jax.experimental import pallas as pl
from jax.experimental.pallas import tpu as pltpu
from jax.sharding import PartitionSpec as P

absent_score = -1e30
LANES = 128
F32 = jnp.float32
BF16 = jnp.bfloat16
VMEM = pl.BlockSpec(memory_space=pltpu.VMEM)
SMEM = pl.BlockSpec(memory_space=pltpu.SMEM)
HBM = pl.BlockSpec(memory_space=pltpu.HBM)
PARAMS = pltpu.CompilerParams(vmem_limit_bytes=16 * 1024 * 1024)
WHOLE = pltpu.CompilerParams(vmem_limit_bytes=62 * 1024 * 1024)


COST = pl.CostEstimate(flops=1000, bytes_accessed=1000, transcendentals=0)


def stage_kernel(devices, group, me_ref, dest_hbm, k_ref, v_ref, buf, table, k_vm, v_vm, dest, counts, sem, load_sem):
    rows, heads = k_ref.shape[:2]
    small = pltpu.make_async_copy(dest_hbm, dest, sem.at[0])
    small.start()
    loads = []
    for row in range(rows):
        for which, (src, dst) in enumerate(((k_ref, k_vm), (v_ref, v_vm))):
            copy = pltpu.make_async_copy(src.at[row], dst.at[row], load_sem.at[which, row])
            copy.start()
            loads.append(copy)
    me = me_ref[0]

    def clear(i, carry):
        counts[i] = 0
        for k in range(group):
            table[i * group + k] = -1
        return carry

    lax.fori_loop(0, devices, clear, 0)
    small.wait()
    for row in range(rows):
        loads[2 * row].wait()
        loads[2 * row + 1].wait()

        def send(head, carry):
            offset = lax.rem(dest[row, head, 0], devices)
            rank = jnp.minimum(counts[offset], group - 1)
            counts[offset] = rank + 1
            table[offset * group + rank] = row * heads + head
            slot = lax.rem(me + offset, devices) * group + rank
            pltpu.make_async_copy(k_vm.at[row, head], buf.at[slot, 0], sem.at[1]).start()
            pltpu.make_async_copy(v_vm.at[row, head], buf.at[slot, 1], sem.at[2]).start()
            return carry

        lax.fori_loop(0, heads, send, 0)
    pltpu.make_async_copy(k_ref, k_vm, sem.at[1]).wait()
    pltpu.make_async_copy(v_ref, v_vm, sem.at[2]).wait()


def attend_kernel(
    levels,
    me_ref, table, len_hbm, kept_hbm, q_hbm, k_ref, v_ref,
    stats_ref, *rest,
):
    chunks = rest[:levels // 2]
    q_vm, k_vm, v_vm, work, len_ref, kept_ref, load_sem, small_sem, out_sem = rest[levels // 2:]
    rows, heads, tile, width = k_ref.shape
    steps, _, q_heads, _ = q_hbm.shape
    per = q_heads // heads
    me = me_ref[0]

    small = [
        pltpu.make_async_copy(len_hbm, len_ref, small_sem.at[0]),
        pltpu.make_async_copy(kept_hbm, kept_ref, small_sem.at[1]),
    ]
    for copy in small:
        copy.start()
    loads = []
    for row in range(rows):
        copies = [
            pltpu.make_async_copy(q_hbm.at[:, row], q_vm.at[row], load_sem.at[0, row]),
            pltpu.make_async_copy(k_ref.at[row], k_vm.at[row], load_sem.at[1, row]),
            pltpu.make_async_copy(v_ref.at[row], v_vm.at[row], load_sem.at[2, row]),
        ]
        for copy in copies:
            copy.start()
        loads.append(copies)
    for copy in small:
        copy.wait()

    lane = lax.broadcasted_iota(jnp.int32, (per, tile), 1)
    pair_lane = lax.broadcasted_iota(jnp.int32, (steps * per, LANES), 1)
    peaks = jnp.full((steps * per, LANES), absent_score, F32)
    totals = jnp.zeros((steps * per, LANES), F32)
    order = [jnp.bitwise_xor(place_of(me), level) for level in range(levels)]
    scale = width ** -0.5
    block = steps * per
    for row in range(rows):
        for copy in loads[row]:
            copy.wait()
        queries = [q_vm[row, step].astype(F32) for step in order]
        live = []
        for step in order:
            limit = jnp.where(kept_ref[row, step, me] > 0, len_ref[row] - me * tile, 0)
            live.append(lane < limit)
        live = jnp.concatenate(live * heads, axis=0)
        scores = []
        for head in range(heads):
            q = jnp.concatenate([x[head * per:(head + 1) * per] for x in queries], axis=0).astype(BF16)
            scores.append(lax.dot_general(
                q, k_vm[row, head], (((1,), (1,)), ((), ())), preferred_element_type=F32
            ))
        scores = jnp.concatenate(scores, axis=0) * scale
        peak = jnp.max(jnp.where(live, scores, absent_score), axis=1, keepdims=True)
        weights = jnp.where(live, jnp.exp(scores - peak), 0.0)
        total = jnp.sum(weights, axis=1, keepdims=True)
        rounded = weights.astype(BF16)
        for head in range(heads):
            out = jnp.dot(
                rounded[head * block:(head + 1) * block], v_vm[row, head], preferred_element_type=F32
            )
            pair = row * heads + head
            for i in range(levels):
                work[i, pair * per:(pair + 1) * per, :] = out[i * per:(i + 1) * per]
            here = pair_lane == pair
            peaks = jnp.where(here, peak[head * block:(head + 1) * block], peaks)
            totals = jnp.where(here, total[head * block:(head + 1) * block], totals)
    base = rows * q_heads
    for i in range(levels):
        work[i, base:base + per, :] = peaks[i * per:(i + 1) * per]
        work[i, base + per:base + 2 * per, :] = totals[i * per:(i + 1) * per]
    stats_ref[0] = peaks
    stats_ref[1] = totals
    copies = [
        pltpu.make_async_copy(work.at[pl.ds(2 * i, 2)], chunks[i], out_sem.at[i]) for i in range(levels // 2)
    ]
    for copy in copies:
        copy.start()
    for copy in copies:
        copy.wait()


def place_of(me):
    return lax.rem(me, 2) * 2 + lax.rem(me // 2, 2)


def merge(swap, own, got, pairs, per):
    def both(rows):
        x, y = own[rows, :], got[rows, :]
        return jnp.where(swap, y, x), jnp.where(swap, x, y)

    base = pairs * per
    peaks = both(slice(base, base + per))
    totals = both(slice(base + per, base + 2 * per))
    peak = jnp.maximum(*peaks)
    factors = [jnp.exp(x - peak) for x in peaks]
    total = factors[0] * totals[0] + factors[1] * totals[1]

    def summed(pair):
        first, second = [jnp.broadcast_to(f[:, pair:pair + 1], (per, LANES)) for f in factors]
        x, y = both(slice(pair * per, (pair + 1) * per))
        return first * x + second * y

    return peak, total, summed


def merge_kernel(bit, pairs, per, me_ref, own, got, *outs):
    swap = lax.rem(me_ref[0] // bit, 2) == 1
    base = pairs * per
    for i, out in enumerate(outs):
        x, y = (own, got) if len(outs) == 1 else (own.at[i], got.at[i])
        peak, total, summed = merge(swap, x, y, pairs, per)
        for pair in range(pairs):
            out[pair * per:(pair + 1) * per, :] = summed(pair)
        out[base:base + per, :] = peak
        out[base + per:base + 2 * per, :] = total


def last_kernel(bit, pairs, per, me_ref, own, got, out):
    swap = lax.rem(me_ref[0] // bit, 2) == 1
    base = pairs * per
    peak, total, summed = merge(swap, own, got, pairs, per)
    lane = lax.broadcasted_iota(jnp.int32, peak.shape, 1)
    total = jnp.where(lane < pairs, total, 1.0)
    peak = jnp.where(lane < pairs, peak, 0.0)

    def result(pair):
        return summed(pair) / jnp.broadcast_to(total[:, pair:pair + 1], (per, LANES))

    for pair in range(0, pairs, 2):
        both = jnp.concatenate([result(pair), result(pair + 1)], axis=0)
        out[pair * per:(pair + 2) * per, :] = both.astype(BF16)
    rest = jnp.concatenate([peak, total], axis=0)
    lane = lax.broadcasted_iota(jnp.int32, rest.shape, 1)
    parts = []
    for i in range(3):
        parts.append(rest.astype(BF16).astype(F32))
        rest = rest - parts[i]
    half = LANES // 2
    packed = jnp.where(lane < half, parts[0], pltpu.roll(parts[1], half, 1))
    out[base:base + 2 * per, :] = packed.astype(BF16)
    out[base + 2 * per:base + 4 * per, :] = parts[2].astype(BF16)


def finish_kernel(pairs, per, heads, levels, me_ref, stats_ref, *refs):
    ins, out, mass_ref = refs[:levels], refs[levels], refs[levels + 1]
    base = pairs * per
    lane = lax.broadcasted_iota(jnp.int32, (2 * per, LANES), 1)
    mass = jnp.zeros((per, LANES), F32)
    for level in range(levels):
        step = jnp.bitwise_xor(place_of(me_ref[0]), level)
        out[step] = ins[level][:base, :]
        packed = ins[level][base:base + 2 * per, :].astype(F32)
        third = ins[level][base + 2 * per:base + 4 * per, :].astype(F32)
        both = third + pltpu.roll(packed, LANES // 2, 1) + packed
        both = jnp.where(lane < pairs, both, 1.0)
        at = level * per
        coefficient = jnp.exp(jnp.minimum(stats_ref[0, at:at + per, :] - both[:per], 0.0)) / both[per:]
        mass = mass + stats_ref[1, at:at + per, :] * coefficient
    mass = jnp.sum(mass, axis=0, keepdims=True)
    for row in range(pairs // heads):
        mass_ref[row] = mass[:, row * heads:(row + 1) * heads]


def place_kernel(devices, group, me_ref, table, got_ref, k_ref, v_ref, me_out, got_vm, sem, load_sem):
    heads = k_ref.shape[1]
    me = me_ref[0]
    me_out[0] = me
    loads = []
    for offset in range(devices):
        source = lax.rem(me + devices - offset, devices)
        part = got_ref.at[pl.ds(source * group, group)]
        copy = pltpu.make_async_copy(part, got_vm.at[pl.ds(offset * group, group)], load_sem.at[offset])
        copy.start()
        loads.append(copy)
    for offset in range(devices):
        loads[offset].wait()
        for slot in range(offset * group, (offset + 1) * group):
            pair = table[slot]

            @pl.when(pair >= 0)
            def _():
                row, head = pair // heads, lax.rem(pair, heads)
                for which, ref in enumerate((k_ref, v_ref)):
                    pltpu.make_async_copy(got_vm.at[slot, which], ref.at[row, head], sem.at[which]).start()
    pltpu.make_async_copy(k_ref, k_ref, sem.at[0]).wait()
    pltpu.make_async_copy(v_ref, v_ref, sem.at[1]).wait()


def local(queries, key_cache, value_cache, row_lengths, kept_tiles, tile_dest):
    devices = lax.axis_size("ctx")
    rows, heads, span, width = key_cache.shape
    steps, _, q_heads, _ = queries.shape
    per = q_heads // heads
    pairs = rows * heads
    group = -(-pairs // devices)
    levels = 4
    assert steps == levels and tile_dest.shape[2] == devices and pairs % 2 == 0 and pairs <= LANES // 2
    assert devices > levels and devices & (devices - 1) == 0 and width == LANES

    me = lax.axis_index("ctx").astype(jnp.int32).reshape(1)
    kept = jnp.transpose(kept_tiles, (1, 0, 2))
    block_rows = rows * q_heads + 2 * per
    block_type = jax.ShapeDtypeStruct((block_rows, width), F32)
    message_type = jax.ShapeDtypeStruct((rows * q_heads + 4 * per, width), BF16)
    tiles_type = jax.ShapeDtypeStruct((devices * group, 2, span, width), BF16)

    tiles_out, table = pl.pallas_call(
        functools.partial(stage_kernel, devices, group),
        out_shape=[tiles_type, jax.ShapeDtypeStruct((devices * group,), jnp.int32)],
        in_specs=[SMEM, HBM, HBM, HBM],
        out_specs=[HBM, SMEM],
        scratch_shapes=[
            pltpu.VMEM(key_cache.shape, BF16),
            pltpu.VMEM(value_cache.shape, BF16),
            pltpu.SMEM(tile_dest.shape, jnp.int32),
            pltpu.SMEM((devices,), jnp.int32),
            pltpu.SemaphoreType.DMA((3,)),
            pltpu.SemaphoreType.DMA((2, rows)),
        ],
        compiler_params=WHOLE,
        cost_estimate=COST,
        name="stage",
    )(me, tile_dest, key_cache, value_cache)
    tiles_in = lax.all_to_all(tiles_out, "ctx", split_axis=0, concat_axis=0, tiled=True)

    stats, *chunks = pl.pallas_call(
        functools.partial(attend_kernel, levels),
        out_shape=[
            jax.ShapeDtypeStruct((2, steps * per, LANES), F32),
        ] + [jax.ShapeDtypeStruct((2, block_rows, width), F32)] * 2,
        in_specs=[SMEM, SMEM, HBM, HBM, HBM, HBM, HBM],
        out_specs=[VMEM] + [HBM] * 2,
        scratch_shapes=[
            pltpu.VMEM((rows, steps, q_heads, width), BF16),
            pltpu.VMEM(key_cache.shape, BF16),
            pltpu.VMEM(value_cache.shape, BF16),
            pltpu.VMEM((levels, block_rows, width), F32),
            pltpu.SMEM(row_lengths.shape, jnp.int32),
            pltpu.SMEM(kept.shape, jnp.int32),
            pltpu.SemaphoreType.DMA((3, rows)),
            pltpu.SemaphoreType.DMA((2,)),
            pltpu.SemaphoreType.DMA((2,)),
        ],
        compiler_params=WHOLE,
        cost_estimate=COST,
        name="attend",
    )(me, table, row_lengths, kept, queries, key_cache, value_cache)

    def flip(x, bit):
        return lax.ppermute(x, "ctx", [(i, i ^ bit) for i in range(devices)])

    def merged(kernel, name, bit, own, got, out_shape):
        return pl.pallas_call(
            functools.partial(kernel, bit, pairs, per),
            out_shape=out_shape,
            in_specs=[SMEM, VMEM, VMEM],
            out_specs=[VMEM] * len(out_shape),
            compiler_params=PARAMS,
            cost_estimate=COST,
            name=name,
        )(me, own, got)

    block, sent = merged(merge_kernel, "core", 1, chunks[0], flip(chunks[1], 1), [block_type] * 2)
    block, = merged(merge_kernel, "near", 2, block, flip(sent, 2), [block_type])
    bit = levels
    while 2 * bit < devices:
        block, = merged(merge_kernel, "far", bit, block, flip(block, bit), [block_type])
        bit *= 2
    message, = merged(last_kernel, "last", bit, block, flip(block, bit), [message_type])
    other = flip(message, 2)

    moved_keys, moved_values, me_next = pl.pallas_call(
        functools.partial(place_kernel, devices, group),
        out_shape=[
            jax.ShapeDtypeStruct(key_cache.shape, BF16),
            jax.ShapeDtypeStruct(value_cache.shape, BF16),
            jax.ShapeDtypeStruct((1,), jnp.int32),
        ],
        in_specs=[SMEM, SMEM, HBM],
        out_specs=[HBM, HBM, SMEM],
        scratch_shapes=[
            pltpu.VMEM(tiles_type.shape, BF16),
            pltpu.SemaphoreType.DMA((2,)),
            pltpu.SemaphoreType.DMA((devices,)),
        ],
        compiler_params=WHOLE,
        cost_estimate=COST,
        name="place",
    )(me, table, tiles_in)

    attn_out, mass = pl.pallas_call(
        functools.partial(finish_kernel, pairs, per, heads, levels),
        out_shape=[
            jax.ShapeDtypeStruct((steps, rows * q_heads, width), BF16),
            jax.ShapeDtypeStruct((rows, 1, heads), F32),
        ],
        in_specs=[SMEM, VMEM] + [VMEM] * levels,
        out_specs=[VMEM, VMEM],
        compiler_params=PARAMS,
        cost_estimate=COST,
        name="finish",
    )(me_next, stats, message, other, flip(message, 1), flip(other, 1))
    return attn_out.reshape(queries.shape), jnp.transpose(mass, (0, 2, 1)), moved_keys, moved_values


def solution(mesh):
    in_specs = (
        P(None, "grp", None, None),
        P("grp", None, "ctx", None),
        P("grp", None, "ctx", None),
        P("grp"),
        P(None, "grp", None),
        P("grp", None, None),
    )
    out_specs = (
        P(None, "grp", None, None),
        P("grp", None, "ctx"),
        P("grp", None, "ctx", None),
        P("grp", None, "ctx", None),
    )
    return jax.shard_map(local, mesh=mesh, in_specs=in_specs, out_specs=out_specs, check_vma=False)
```

```python
import functools

import jax
import jax.numpy as jnp
from jax import lax
from jax.experimental import pallas as pl
from jax.experimental.pallas import tpu as pltpu
from jax.sharding import PartitionSpec as P

absent_score = -1e30
LANES = 128
F32 = jnp.float32
BF16 = jnp.bfloat16
VMEM = pl.BlockSpec(memory_space=pltpu.VMEM)
SMEM = pl.BlockSpec(memory_space=pltpu.SMEM)
HBM = pl.BlockSpec(memory_space=pltpu.HBM)
ANY = pl.BlockSpec(memory_space=pl.ANY)
PARAMS = pltpu.CompilerParams(vmem_limit_bytes=16 * 1024 * 1024)
WHOLE = pltpu.CompilerParams(vmem_limit_bytes=62 * 1024 * 1024)


COST = pl.CostEstimate(flops=1000, bytes_accessed=1000, transcendentals=0)


def stage_kernel(devices, group, me_ref, dest_hbm, k_ref, v_ref, buf, table, k_vm, v_vm, dest, counts, sem, load_sem):
    rows, heads = k_ref.shape[:2]
    small = pltpu.make_async_copy(dest_hbm, dest, sem.at[0])
    small.start()
    loads = []
    for row in range(rows):
        for which, (src, dst) in enumerate(((k_ref, k_vm), (v_ref, v_vm))):
            copy = pltpu.make_async_copy(src.at[row], dst.at[row], load_sem.at[which, row])
            copy.start()
            loads.append(copy)
    me = me_ref[0]

    def clear(i, carry):
        counts[i] = 0
        for k in range(group):
            table[i * group + k] = -1
        return carry

    lax.fori_loop(0, devices, clear, 0)
    small.wait()
    for row in range(rows):
        loads[2 * row].wait()
        loads[2 * row + 1].wait()

        def send(head, carry):
            offset = lax.rem(dest[row, head, 0], devices)
            rank = jnp.minimum(counts[offset], group - 1)
            counts[offset] = rank + 1
            table[offset * group + rank] = row * heads + head
            slot = lax.rem(me + offset, devices) * group + rank
            pltpu.make_async_copy(k_vm.at[row, head], buf.at[slot, 0], sem.at[1]).start()
            pltpu.make_async_copy(v_vm.at[row, head], buf.at[slot, 1], sem.at[2]).start()
            return carry

        lax.fori_loop(0, heads, send, 0)
    pltpu.make_async_copy(k_ref, k_vm, sem.at[1]).wait()
    pltpu.make_async_copy(v_ref, v_vm, sem.at[2]).wait()


def attend_kernel(
    levels,
    me_ref, table, len_hbm, kept_hbm, q_ref, k_ref, v_ref,
    stats_ref, *rest,
):
    chunks = rest[:levels // 2]
    len_ref, kept_ref, small_sem = rest[levels // 2:]
    rows, heads, tile, width = k_ref.shape
    steps, _, q_heads, _ = q_ref.shape
    per = q_heads // heads
    me = me_ref[0]

    small = [
        pltpu.make_async_copy(len_hbm, len_ref, small_sem.at[0]),
        pltpu.make_async_copy(kept_hbm, kept_ref, small_sem.at[1]),
    ]
    for copy in small:
        copy.start()
    for copy in small:
        copy.wait()

    lane = lax.broadcasted_iota(jnp.int32, (per, tile), 1)
    pair_lane = lax.broadcasted_iota(jnp.int32, (steps * per, LANES), 1)
    peaks = jnp.full((steps * per, LANES), absent_score, F32)
    totals = jnp.zeros((steps * per, LANES), F32)
    order = [jnp.bitwise_xor(place_of(me), level) for level in range(levels)]
    scale = width ** -0.5
    block = steps * per
    for row in range(rows):
        queries = [q_ref[step, row].astype(F32) for step in order]
        live = []
        for step in order:
            limit = jnp.where(kept_ref[row, step, me] > 0, len_ref[row] - me * tile, 0)
            live.append(lane < limit)
        live = jnp.concatenate(live * heads, axis=0)
        scores = []
        for head in range(heads):
            q = jnp.concatenate([x[head * per:(head + 1) * per] for x in queries], axis=0).astype(BF16)
            scores.append(lax.dot_general(
                q, k_ref[row, head], (((1,), (1,)), ((), ())), preferred_element_type=F32
            ))
        scores = jnp.concatenate(scores, axis=0) * scale
        peak = jnp.max(jnp.where(live, scores, absent_score), axis=1, keepdims=True)
        weights = jnp.where(live, jnp.exp(scores - peak), 0.0)
        total = jnp.sum(weights, axis=1, keepdims=True)
        rounded = weights.astype(BF16)
        for head in range(heads):
            out = jnp.dot(
                rounded[head * block:(head + 1) * block], v_ref[row, head], preferred_element_type=F32
            )
            pair = row * heads + head
            for i in range(levels):
                chunks[i // 2][i % 2, pair * per:(pair + 1) * per, :] = out[i * per:(i + 1) * per]
            here = pair_lane == pair
            peaks = jnp.where(here, peak[head * block:(head + 1) * block], peaks)
            totals = jnp.where(here, total[head * block:(head + 1) * block], totals)
    base = rows * q_heads
    for i in range(levels):
        chunks[i // 2][i % 2, base:base + per, :] = peaks[i * per:(i + 1) * per]
        chunks[i // 2][i % 2, base + per:base + 2 * per, :] = totals[i * per:(i + 1) * per]
    stats_ref[0] = peaks
    stats_ref[1] = totals


def place_of(me):
    return lax.rem(me, 2) * 2 + lax.rem(me // 2, 2)


def merge(swap, own, got, pairs, per):
    def both(rows):
        x, y = own[rows, :], got[rows, :]
        return jnp.where(swap, y, x), jnp.where(swap, x, y)

    base = pairs * per
    peaks = both(slice(base, base + per))
    totals = both(slice(base + per, base + 2 * per))
    peak = jnp.maximum(*peaks)
    factors = [jnp.exp(x - peak) for x in peaks]
    total = factors[0] * totals[0] + factors[1] * totals[1]

    def summed(pair):
        first, second = [jnp.broadcast_to(f[:, pair:pair + 1], (per, LANES)) for f in factors]
        x, y = both(slice(pair * per, (pair + 1) * per))
        return first * x + second * y

    return peak, total, summed


def merge_kernel(bit, pairs, per, me_ref, own, got, *outs):
    swap = lax.rem(me_ref[0] // bit, 2) == 1
    base = pairs * per
    for i, out in enumerate(outs):
        x, y = (own, got) if len(outs) == 1 else (own.at[i], got.at[i])
        peak, total, summed = merge(swap, x, y, pairs, per)
        for pair in range(pairs):
            out[pair * per:(pair + 1) * per, :] = summed(pair)
        out[base:base + per, :] = peak
        out[base + per:base + 2 * per, :] = total


def last_kernel(bit, pairs, per, me_ref, own, got, out):
    swap = lax.rem(me_ref[0] // bit, 2) == 1
    base = pairs * per
    peak, total, summed = merge(swap, own, got, pairs, per)
    lane = lax.broadcasted_iota(jnp.int32, peak.shape, 1)
    total = jnp.where(lane < pairs, total, 1.0)
    peak = jnp.where(lane < pairs, peak, 0.0)

    def result(pair):
        return summed(pair) / jnp.broadcast_to(total[:, pair:pair + 1], (per, LANES))

    for pair in range(0, pairs, 2):
        both = jnp.concatenate([result(pair), result(pair + 1)], axis=0)
        out[pair * per:(pair + 2) * per, :] = both.astype(BF16)
    rest = jnp.concatenate([peak, total], axis=0)
    lane = lax.broadcasted_iota(jnp.int32, rest.shape, 1)
    parts = []
    for i in range(3):
        parts.append(rest.astype(BF16).astype(F32))
        rest = rest - parts[i]
    half = LANES // 2
    packed = jnp.where(lane < half, parts[0], pltpu.roll(parts[1], half, 1))
    out[base:base + 2 * per, :] = packed.astype(BF16)
    out[base + 2 * per:base + 4 * per, :] = parts[2].astype(BF16)


def finish_kernel(pairs, per, heads, levels, me_ref, stats_ref, *refs):
    ins, out, mass_ref = refs[:levels], refs[levels], refs[levels + 1]
    base = pairs * per
    lane = lax.broadcasted_iota(jnp.int32, (2 * per, LANES), 1)
    mass = jnp.zeros((per, LANES), F32)
    for level in range(levels):
        step = jnp.bitwise_xor(place_of(me_ref[0]), level)
        out[step] = ins[level][:base, :]
        packed = ins[level][base:base + 2 * per, :].astype(F32)
        third = ins[level][base + 2 * per:base + 4 * per, :].astype(F32)
        both = third + pltpu.roll(packed, LANES // 2, 1) + packed
        both = jnp.where(lane < pairs, both, 1.0)
        at = level * per
        coefficient = jnp.exp(jnp.minimum(stats_ref[0, at:at + per, :] - both[:per], 0.0)) / both[per:]
        mass = mass + stats_ref[1, at:at + per, :] * coefficient
    mass = jnp.sum(mass, axis=0, keepdims=True)
    for row in range(pairs // heads):
        mass_ref[row] = mass[:, row * heads:(row + 1) * heads]


def place_kernel(devices, group, me_ref, table, got_ref, k_ref, v_ref, me_out, sem):
    heads = k_ref.shape[1]
    me = me_ref[0]
    me_out[0] = me
    for offset in range(devices):
        source = lax.rem(me + devices - offset, devices)
        for k in range(group):
            pair = table[offset * group + k]

            @pl.when(pair >= 0)
            def _():
                row, head = pair // heads, lax.rem(pair, heads)
                for which, ref in enumerate((k_ref, v_ref)):
                    src = got_ref.at[source * group + k, which]
                    pltpu.make_async_copy(src, ref.at[row, head], sem.at[which]).start()
    pltpu.make_async_copy(k_ref, k_ref, sem.at[0]).wait()
    pltpu.make_async_copy(v_ref, v_ref, sem.at[1]).wait()


def local(queries, key_cache, value_cache, row_lengths, kept_tiles, tile_dest):
    devices = lax.axis_size("ctx")
    rows, heads, span, width = key_cache.shape
    steps, _, q_heads, _ = queries.shape
    per = q_heads // heads
    pairs = rows * heads
    group = -(-pairs // devices)
    levels = 4
    assert steps == levels and tile_dest.shape[2] == devices and pairs % 2 == 0 and pairs <= LANES // 2
    assert devices > levels and devices & (devices - 1) == 0 and width == LANES

    me = lax.axis_index("ctx").astype(jnp.int32).reshape(1)
    kept = jnp.transpose(kept_tiles, (1, 0, 2))
    block_rows = rows * q_heads + 2 * per
    block_type = jax.ShapeDtypeStruct((block_rows, width), F32)
    message_type = jax.ShapeDtypeStruct((rows * q_heads + 4 * per, width), BF16)
    tiles_type = jax.ShapeDtypeStruct((devices * group, 2, span, width), BF16)

    tiles_out, table = pl.pallas_call(
        functools.partial(stage_kernel, devices, group),
        out_shape=[tiles_type, jax.ShapeDtypeStruct((devices * group,), jnp.int32)],
        in_specs=[SMEM, HBM, HBM, HBM],
        out_specs=[HBM, SMEM],
        scratch_shapes=[
            pltpu.VMEM(key_cache.shape, BF16),
            pltpu.VMEM(value_cache.shape, BF16),
            pltpu.SMEM(tile_dest.shape, jnp.int32),
            pltpu.SMEM((devices,), jnp.int32),
            pltpu.SemaphoreType.DMA((3,)),
            pltpu.SemaphoreType.DMA((2, rows)),
        ],
        compiler_params=WHOLE,
        cost_estimate=COST,
        name="stage",
    )(me, tile_dest, key_cache, value_cache)
    tiles_in = lax.all_to_all(tiles_out, "ctx", split_axis=0, concat_axis=0, tiled=True)

    stats, *chunks = pl.pallas_call(
        functools.partial(attend_kernel, levels),
        out_shape=[
            jax.ShapeDtypeStruct((2, steps * per, LANES), F32),
        ] + [jax.ShapeDtypeStruct((2, block_rows, width), F32)] * 2,
        in_specs=[SMEM, SMEM, HBM, HBM, VMEM, VMEM, VMEM],
        out_specs=[VMEM] * 3,
        scratch_shapes=[
            pltpu.SMEM(row_lengths.shape, jnp.int32),
            pltpu.SMEM(kept.shape, jnp.int32),
            pltpu.SemaphoreType.DMA((2,)),
        ],
        compiler_params=PARAMS,
        cost_estimate=COST,
        name="attend",
    )(me, table, row_lengths, kept, queries, key_cache, value_cache)

    def flip(x, bit):
        return lax.ppermute(x, "ctx", [(i, i ^ bit) for i in range(devices)])

    def merged(kernel, name, bit, own, got, out_shape):
        return pl.pallas_call(
            functools.partial(kernel, bit, pairs, per),
            out_shape=out_shape,
            in_specs=[SMEM, VMEM, VMEM],
            out_specs=[VMEM] * len(out_shape),
            compiler_params=PARAMS,
            cost_estimate=COST,
            name=name,
        )(me, own, got)

    block, sent = merged(merge_kernel, "core", 1, chunks[0], flip(chunks[1], 1), [block_type] * 2)
    block, = merged(merge_kernel, "near", 2, block, flip(sent, 2), [block_type])
    bit = levels
    while 2 * bit < devices:
        block, = merged(merge_kernel, "far", bit, block, flip(block, bit), [block_type])
        bit *= 2
    message, = merged(last_kernel, "last", bit, block, flip(block, bit), [message_type])
    arrived = [message] + [flip(message, i) for i in (2, 1, 3)]

    moved_keys, moved_values, me_next = pl.pallas_call(
        functools.partial(place_kernel, devices, group),
        out_shape=[
            jax.ShapeDtypeStruct(key_cache.shape, BF16),
            jax.ShapeDtypeStruct(value_cache.shape, BF16),
            jax.ShapeDtypeStruct((1,), jnp.int32),
        ],
        in_specs=[SMEM, SMEM, ANY],
        out_specs=[HBM, HBM, SMEM],
        scratch_shapes=[pltpu.SemaphoreType.DMA((2,))],
        compiler_params=PARAMS,
        cost_estimate=COST,
        name="place",
    )(me, table, tiles_in)

    attn_out, mass = pl.pallas_call(
        functools.partial(finish_kernel, pairs, per, heads, levels),
        out_shape=[
            jax.ShapeDtypeStruct((steps, rows * q_heads, width), BF16),
            jax.ShapeDtypeStruct((rows, 1, heads), F32),
        ],
        in_specs=[SMEM, VMEM] + [VMEM] * levels,
        out_specs=[VMEM, VMEM],
        compiler_params=PARAMS,
        cost_estimate=COST,
        name="finish",
    )(me_next, stats, *arrived)
    return attn_out.reshape(queries.shape), jnp.transpose(mass, (0, 2, 1)), moved_keys, moved_values


def solution(mesh):
    in_specs = (
        P(None, "grp", None, None),
        P("grp", None, "ctx", None),
        P("grp", None, "ctx", None),
        P("grp"),
        P(None, "grp", None),
        P("grp", None, None),
    )
    out_specs = (
        P(None, "grp", None, None),
        P("grp", None, "ctx"),
        P("grp", None, "ctx", None),
        P("grp", None, "ctx", None),
    )
    return jax.shard_map(local, mesh=mesh, in_specs=in_specs, out_specs=out_specs, check_vma=False)
```

```python
import functools

import jax
import jax.numpy as jnp
from jax import lax
from jax.experimental import pallas as pl
from jax.experimental.pallas import tpu as pltpu
from jax.sharding import PartitionSpec as P

absent_score = -1e30
LANES = 128
F32 = jnp.float32
BF16 = jnp.bfloat16
VMEM = pl.BlockSpec(memory_space=pltpu.VMEM)
SMEM = pl.BlockSpec(memory_space=pltpu.SMEM)
HBM = pl.BlockSpec(memory_space=pltpu.HBM)
ANY = pl.BlockSpec(memory_space=pl.ANY)
PARAMS = pltpu.CompilerParams(vmem_limit_bytes=16 * 1024 * 1024)
WHOLE = pltpu.CompilerParams(vmem_limit_bytes=62 * 1024 * 1024)


COST = pl.CostEstimate(flops=1000, bytes_accessed=1000, transcendentals=0)


def stage_kernel(devices, group, me_ref, dest_hbm, k_ref, v_ref, buf, table, k_vm, v_vm, dest, counts, sem, load_sem):
    rows, heads = k_ref.shape[:2]
    small = pltpu.make_async_copy(dest_hbm, dest, sem.at[0])
    small.start()
    loads = []
    for row in range(rows):
        for which, (src, dst) in enumerate(((k_ref, k_vm), (v_ref, v_vm))):
            copy = pltpu.make_async_copy(src.at[row], dst.at[row], load_sem.at[which, row])
            copy.start()
            loads.append(copy)
    me = me_ref[0]

    def clear(i, carry):
        counts[i] = 0
        for k in range(group):
            table[i * group + k] = -1
        return carry

    lax.fori_loop(0, devices, clear, 0)
    small.wait()
    for row in range(rows):
        loads[2 * row].wait()
        loads[2 * row + 1].wait()

        def send(head, carry):
            offset = lax.rem(dest[row, head, 0], devices)
            rank = jnp.minimum(counts[offset], group - 1)
            counts[offset] = rank + 1
            table[offset * group + rank] = row * heads + head
            slot = lax.rem(me + offset, devices) * group + rank
            pltpu.make_async_copy(k_vm.at[row, head], buf.at[slot, 0], sem.at[1]).start()
            pltpu.make_async_copy(v_vm.at[row, head], buf.at[slot, 1], sem.at[2]).start()
            return carry

        lax.fori_loop(0, heads, send, 0)
    pltpu.make_async_copy(k_ref, k_vm, sem.at[1]).wait()
    pltpu.make_async_copy(v_ref, v_vm, sem.at[2]).wait()


def attend_kernel(
    levels,
    me_ref, table, len_hbm, kept_hbm, q_ref, k_ref, v_ref,
    stats_ref, *rest,
):
    chunks = rest[:levels // 2]
    len_ref, kept_ref, small_sem = rest[levels // 2:]
    rows, heads, tile, width = k_ref.shape
    steps, _, q_heads, _ = q_ref.shape
    per = q_heads // heads
    me = me_ref[0]

    small = [
        pltpu.make_async_copy(len_hbm, len_ref, small_sem.at[0]),
        pltpu.make_async_copy(kept_hbm, kept_ref, small_sem.at[1]),
    ]
    for copy in small:
        copy.start()
    for copy in small:
        copy.wait()

    lane = lax.broadcasted_iota(jnp.int32, (per, tile), 1)
    pair_lane = lax.broadcasted_iota(jnp.int32, (steps * per, LANES), 1)
    peaks = jnp.full((steps * per, LANES), absent_score, F32)
    totals = jnp.zeros((steps * per, LANES), F32)
    order = [jnp.bitwise_xor(place_of(me), level) for level in range(levels)]
    scale = width ** -0.5
    block = steps * per
    for row in range(rows):
        queries = [q_ref[step, row].astype(F32) for step in order]
        live = []
        for step in order:
            limit = jnp.where(kept_ref[row, step, me] > 0, len_ref[row] - me * tile, 0)
            live.append(lane < limit)
        live = jnp.concatenate(live * heads, axis=0)
        scores = []
        for head in range(heads):
            q = jnp.concatenate([x[head * per:(head + 1) * per] for x in queries], axis=0).astype(BF16)
            scores.append(lax.dot_general(
                q, k_ref[row, head], (((1,), (1,)), ((), ())), preferred_element_type=F32
            ))
        scores = jnp.concatenate(scores, axis=0) * scale
        peak = jnp.max(jnp.where(live, scores, absent_score), axis=1, keepdims=True)
        weights = jnp.where(live, jnp.exp(scores - peak), 0.0)
        total = jnp.sum(weights, axis=1, keepdims=True)
        rounded = weights.astype(BF16)
        for head in range(heads):
            out = jnp.dot(
                rounded[head * block:(head + 1) * block], v_ref[row, head], preferred_element_type=F32
            )
            pair = row * heads + head
            for i in range(levels):
                chunks[i // 2][i % 2, pair * per:(pair + 1) * per, :] = out[i * per:(i + 1) * per]
            here = pair_lane == pair
            peaks = jnp.where(here, peak[head * block:(head + 1) * block], peaks)
            totals = jnp.where(here, total[head * block:(head + 1) * block], totals)
    base = rows * q_heads
    for i in range(levels):
        chunks[i // 2][i % 2, base:base + per, :] = peaks[i * per:(i + 1) * per]
        chunks[i // 2][i % 2, base + per:base + 2 * per, :] = totals[i * per:(i + 1) * per]
    stats_ref[0] = peaks
    stats_ref[1] = totals


def place_of(me):
    return lax.rem(me, 2) * 2 + lax.rem(me // 2, 2)


def merge(swap, own, got, pairs, per, own_stats=None, got_stats=None):
    def both(rows, own=own, got=got):
        x, y = own[rows, :], got[rows, :]
        return jnp.where(swap, y, x), jnp.where(swap, x, y)

    scaled = own_stats is not None
    base = 0 if scaled else pairs * per
    stats = (own_stats, got_stats) if scaled else (own, got)
    peaks = both(slice(base, base + per), *stats)
    totals = both(slice(base + per, base + 2 * per), *stats)
    peak = jnp.maximum(*peaks)
    factors = [jnp.exp(x - peak) for x in peaks]
    total = factors[0] * totals[0] + factors[1] * totals[1]
    if scaled:
        scales = both(slice(2 * per, 3 * per), *stats)
        factors = [f * x for f, x in zip(factors, scales)]

    def summed(pair):
        first, second = [jnp.broadcast_to(f[:, pair:pair + 1], (per, LANES)) for f in factors]
        x, y = both(slice(pair * per, (pair + 1) * per))
        return first * x + second * y

    return peak, total, summed


def merge_kernel(bit, pairs, per, me_ref, own, got, *outs):
    swap = lax.rem(me_ref[0] // bit, 2) == 1
    base = pairs * per
    for i, out in enumerate(outs):
        x, y = (own, got) if len(outs) == 1 else (own.at[i], got.at[i])
        peak, total, summed = merge(swap, x, y, pairs, per)
        for pair in range(pairs):
            out[pair * per:(pair + 1) * per, :] = summed(pair)
        out[base:base + per, :] = peak
        out[base + per:base + 2 * per, :] = total


def scale_kernel(pairs, per, block, sums, stats):
    lane = lax.broadcasted_iota(jnp.int32, (per, LANES), 1)
    base = pairs * per
    scales = jnp.ones((per, LANES), F32)
    for pair in range(pairs):
        x = block[pair * per:(pair + 1) * per, :]
        largest = jnp.max(jnp.abs(x), axis=1, keepdims=True)
        largest = jnp.where(largest > 0.0, largest, 1.0)
        sums[pair * per:(pair + 1) * per, :] = x / largest
        scales = jnp.where(lane == pair, largest, scales)
    stats[:2 * per, :] = block[base:base + 2 * per, :]
    stats[2 * per:, :] = scales


def last_kernel(bit, pairs, per, me_ref, own, got, own_stats, got_stats, out):
    swap = lax.rem(me_ref[0] // bit, 2) == 1
    base = pairs * per
    peak, total, summed = merge(swap, own, got, pairs, per, own_stats, got_stats)
    lane = lax.broadcasted_iota(jnp.int32, peak.shape, 1)
    total = jnp.where(lane < pairs, total, 1.0)
    peak = jnp.where(lane < pairs, peak, 0.0)

    def result(pair):
        return summed(pair) / jnp.broadcast_to(total[:, pair:pair + 1], (per, LANES))

    for pair in range(0, pairs, 2):
        both = jnp.concatenate([result(pair), result(pair + 1)], axis=0)
        out[pair * per:(pair + 2) * per, :] = both.astype(BF16)
    rest = jnp.concatenate([peak, total], axis=0)
    lane = lax.broadcasted_iota(jnp.int32, rest.shape, 1)
    parts = []
    for i in range(3):
        parts.append(rest.astype(BF16).astype(F32))
        rest = rest - parts[i]
    half = LANES // 2
    packed = jnp.where(lane < half, parts[0], pltpu.roll(parts[1], half, 1))
    out[base:base + 2 * per, :] = packed.astype(BF16)
    out[base + 2 * per:base + 4 * per, :] = parts[2].astype(BF16)


def pass_kernel(me_ref, x, out):
    out[...] = x[...]


def finish_kernel(pairs, per, heads, levels, me_ref, stats_ref, *refs):
    ins, out, mass_ref = refs[:levels], refs[levels], refs[levels + 1]
    base = pairs * per
    lane = lax.broadcasted_iota(jnp.int32, (2 * per, LANES), 1)
    mass = jnp.zeros((per, LANES), F32)
    for level in range(levels):
        step = jnp.bitwise_xor(place_of(me_ref[0]), level)
        out[step] = ins[level][:base, :]
        packed = ins[level][base:base + 2 * per, :].astype(F32)
        third = ins[level][base + 2 * per:base + 4 * per, :].astype(F32)
        both = third + pltpu.roll(packed, LANES // 2, 1) + packed
        both = jnp.where(lane < pairs, both, 1.0)
        at = level * per
        coefficient = jnp.exp(jnp.minimum(stats_ref[0, at:at + per, :] - both[:per], 0.0)) / both[per:]
        mass = mass + stats_ref[1, at:at + per, :] * coefficient
    mass = jnp.sum(mass, axis=0, keepdims=True)
    for row in range(pairs // heads):
        mass_ref[row] = mass[:, row * heads:(row + 1) * heads]


def place_kernel(devices, group, me_ref, table, got_ref, k_ref, v_ref, me_out, sem):
    heads = k_ref.shape[1]
    me = me_ref[0]
    me_out[0] = me
    for offset in range(devices):
        source = lax.rem(me + devices - offset, devices)
        for k in range(group):
            pair = table[offset * group + k]

            @pl.when(pair >= 0)
            def _():
                row, head = pair // heads, lax.rem(pair, heads)
                for which, ref in enumerate((k_ref, v_ref)):
                    src = got_ref.at[source * group + k, which]
                    pltpu.make_async_copy(src, ref.at[row, head], sem.at[which]).start()
    pltpu.make_async_copy(k_ref, k_ref, sem.at[0]).wait()
    pltpu.make_async_copy(v_ref, v_ref, sem.at[1]).wait()


def local(queries, key_cache, value_cache, row_lengths, kept_tiles, tile_dest):
    devices = lax.axis_size("ctx")
    rows, heads, span, width = key_cache.shape
    steps, _, q_heads, _ = queries.shape
    per = q_heads // heads
    pairs = rows * heads
    group = -(-pairs // devices)
    levels = 4
    assert steps == levels and tile_dest.shape[2] == devices and pairs % 2 == 0 and pairs <= LANES // 2
    assert devices > levels and devices & (devices - 1) == 0 and width == LANES

    me = lax.axis_index("ctx").astype(jnp.int32).reshape(1)
    kept = jnp.transpose(kept_tiles, (1, 0, 2))
    block_rows = rows * q_heads + 2 * per
    block_type = jax.ShapeDtypeStruct((block_rows, width), F32)
    message_type = jax.ShapeDtypeStruct((rows * q_heads + 4 * per, width), BF16)
    tiles_type = jax.ShapeDtypeStruct((devices * group, 2, span, width), BF16)

    tiles_out, table = pl.pallas_call(
        functools.partial(stage_kernel, devices, group),
        out_shape=[tiles_type, jax.ShapeDtypeStruct((devices * group,), jnp.int32)],
        in_specs=[SMEM, HBM, HBM, HBM],
        out_specs=[HBM, SMEM],
        scratch_shapes=[
            pltpu.VMEM(key_cache.shape, BF16),
            pltpu.VMEM(value_cache.shape, BF16),
            pltpu.SMEM(tile_dest.shape, jnp.int32),
            pltpu.SMEM((devices,), jnp.int32),
            pltpu.SemaphoreType.DMA((3,)),
            pltpu.SemaphoreType.DMA((2, rows)),
        ],
        compiler_params=WHOLE,
        cost_estimate=COST,
        name="stage",
    )(me, tile_dest, key_cache, value_cache)
    tiles_in = lax.all_to_all(tiles_out, "ctx", split_axis=0, concat_axis=0, tiled=True)

    stats, *chunks = pl.pallas_call(
        functools.partial(attend_kernel, levels),
        out_shape=[
            jax.ShapeDtypeStruct((2, steps * per, LANES), F32),
        ] + [jax.ShapeDtypeStruct((2, block_rows, width), F32)] * 2,
        in_specs=[SMEM, SMEM, HBM, HBM, VMEM, VMEM, VMEM],
        out_specs=[VMEM] * 3,
        scratch_shapes=[
            pltpu.SMEM(row_lengths.shape, jnp.int32),
            pltpu.SMEM(kept.shape, jnp.int32),
            pltpu.SemaphoreType.DMA((2,)),
        ],
        compiler_params=PARAMS,
        cost_estimate=COST,
        name="attend",
    )(me, table, row_lengths, kept, queries, key_cache, value_cache)

    def flip(x, bit):
        return lax.ppermute(x, "ctx", [(i, i ^ bit) for i in range(devices)])

    def local_call(kernel, name, out_shape, *operands):
        return pl.pallas_call(
            kernel,
            out_shape=out_shape,
            in_specs=[SMEM if x is me or x.shape == (1,) else VMEM for x in operands],
            out_specs=[VMEM] * len(out_shape),
            compiler_params=PARAMS,
            cost_estimate=COST,
            name=name,
        )(*operands)

    def merged(name, bit, own, got, out_shape):
        return local_call(functools.partial(merge_kernel, bit, pairs, per), name, out_shape, me, own, got)

    block, sent = merged("core", 1, chunks[0], flip(chunks[1], 1), [block_type] * 2)
    block, = merged("near", 2, block, flip(sent, 2), [block_type])
    bit = levels
    while 2 * bit < devices:
        block, = merged("far", bit, block, flip(block, bit), [block_type])
        bit *= 2
    sums_type = jax.ShapeDtypeStruct((rows * q_heads, width), F32)
    stats_type = jax.ShapeDtypeStruct((3 * per, width), F32)
    sums, sum_stats = local_call(functools.partial(scale_kernel, pairs, per), "scale", [sums_type, stats_type], block)
    sums = lax.reduce_precision(sums, 5, 10)
    got = flip(sums.astype(jnp.float16), bit).astype(F32)
    message, = local_call(
        functools.partial(last_kernel, bit, pairs, per), "last", [message_type],
        me, sums, got, sum_stats, flip(sum_stats, bit),
    )
    other = flip(message, 2)

    moved_keys, moved_values, me_next = pl.pallas_call(
        functools.partial(place_kernel, devices, group),
        out_shape=[
            jax.ShapeDtypeStruct(key_cache.shape, BF16),
            jax.ShapeDtypeStruct(value_cache.shape, BF16),
            jax.ShapeDtypeStruct((1,), jnp.int32),
        ],
        in_specs=[SMEM, SMEM, ANY],
        out_specs=[HBM, HBM, SMEM],
        scratch_shapes=[pltpu.SemaphoreType.DMA((2,))],
        compiler_params=PARAMS,
        cost_estimate=COST,
        name="place",
    )(me, table, tiles_in)

    other_next, = local_call(pass_kernel, "pass", [message_type], me_next, other)
    arrived = [message, other, flip(message, 1), flip(other_next, 1)]

    attn_out, mass = pl.pallas_call(
        functools.partial(finish_kernel, pairs, per, heads, levels),
        out_shape=[
            jax.ShapeDtypeStruct((steps, rows * q_heads, width), BF16),
            jax.ShapeDtypeStruct((rows, 1, heads), F32),
        ],
        in_specs=[SMEM, VMEM] + [VMEM] * levels,
        out_specs=[VMEM, VMEM],
        compiler_params=PARAMS,
        cost_estimate=COST,
        name="finish",
    )(me_next, stats, *arrived)
    return attn_out.reshape(queries.shape), jnp.transpose(mass, (0, 2, 1)), moved_keys, moved_values


def solution(mesh):
    in_specs = (
        P(None, "grp", None, None),
        P("grp", None, "ctx", None),
        P("grp", None, "ctx", None),
        P("grp"),
        P(None, "grp", None),
        P("grp", None, None),
    )
    out_specs = (
        P(None, "grp", None, None),
        P("grp", None, "ctx"),
        P("grp", None, "ctx", None),
        P("grp", None, "ctx", None),
    )
    return jax.shard_map(local, mesh=mesh, in_specs=in_specs, out_specs=out_specs, check_vma=False)
```

```python
import functools

import jax
import jax.numpy as jnp
from jax import lax
from jax.experimental import pallas as pl
from jax.experimental.pallas import tpu as pltpu
from jax.sharding import PartitionSpec as P

absent_score = -1e30
LANES = 128
F32 = jnp.float32
BF16 = jnp.bfloat16
VMEM = pl.BlockSpec(memory_space=pltpu.VMEM)
SMEM = pl.BlockSpec(memory_space=pltpu.SMEM)
HBM = pl.BlockSpec(memory_space=pltpu.HBM)
ANY = pl.BlockSpec(memory_space=pl.ANY)
PARAMS = pltpu.CompilerParams(vmem_limit_bytes=16 * 1024 * 1024)
WHOLE = pltpu.CompilerParams(vmem_limit_bytes=62 * 1024 * 1024)


COST = pl.CostEstimate(flops=1000, bytes_accessed=1000, transcendentals=0)


def stage_kernel(devices, group, me_ref, dest_hbm, x_ref, buf, table, me_out, x_vm, dest, counts, sem, load_sem):
    rows, heads = x_ref.shape[:2]
    small = pltpu.make_async_copy(dest_hbm, dest, sem.at[0])
    small.start()
    loads = []
    for row in range(rows):
        copy = pltpu.make_async_copy(x_ref.at[row], x_vm.at[row], load_sem.at[row])
        copy.start()
        loads.append(copy)
    me = me_ref[0]
    me_out[0] = me

    def clear(i, carry):
        counts[i] = 0
        for k in range(group):
            table[i * group + k] = -1
        return carry

    lax.fori_loop(0, devices, clear, 0)
    small.wait()
    for row in range(rows):
        loads[row].wait()
        for head in range(heads):
            offset = dest[row, head, 0]
            rank = counts[offset]
            counts[offset] = rank + 1
            table[offset * group + rank] = row * heads + head
            slot = jnp.bitwise_and(me + offset, devices - 1) * group + rank
            pltpu.make_async_copy(x_vm.at[row, head], buf.at[slot], sem.at[1]).start()
    pltpu.make_async_copy(x_ref, x_vm, sem.at[1]).wait()


def attend_kernel(
    levels,
    me_ref, table, len_hbm, kept_hbm, q_ref, k_ref, v_ref,
    stats_ref, *rest,
):
    chunks = rest[:levels // 2]
    len_ref, kept_ref, small_sem = rest[levels // 2:]
    rows, heads, tile, width = k_ref.shape
    steps, _, q_heads, _ = q_ref.shape
    per = q_heads // heads
    me = me_ref[0]

    small = [
        pltpu.make_async_copy(len_hbm, len_ref, small_sem.at[0]),
        pltpu.make_async_copy(kept_hbm, kept_ref, small_sem.at[1]),
    ]
    for copy in small:
        copy.start()
    for copy in small:
        copy.wait()

    lane = lax.broadcasted_iota(jnp.int32, (per, tile), 1)
    pair_lane = lax.broadcasted_iota(jnp.int32, (steps * per, LANES), 1)
    peaks = jnp.full((steps * per, LANES), absent_score, F32)
    totals = jnp.zeros((steps * per, LANES), F32)
    order = [jnp.bitwise_xor(place_of(me), level) for level in range(levels)]
    scale = width ** -0.5
    block = steps * per
    for row in range(rows):
        queries = [q_ref[step, row].astype(F32) for step in order]
        live = []
        for step in order:
            limit = jnp.where(kept_ref[row, step, me] > 0, len_ref[row] - me * tile, 0)
            live.append(lane < limit)
        live = jnp.concatenate(live * heads, axis=0)
        scores = []
        for head in range(heads):
            q = jnp.concatenate([x[head * per:(head + 1) * per] for x in queries], axis=0).astype(BF16)
            scores.append(lax.dot_general(
                q, k_ref[row, head], (((1,), (1,)), ((), ())), preferred_element_type=F32
            ))
        scores = jnp.concatenate(scores, axis=0) * scale
        peak = jnp.max(jnp.where(live, scores, absent_score), axis=1, keepdims=True)
        weights = jnp.where(live, jnp.exp(scores - peak), 0.0)
        total = jnp.sum(weights, axis=1, keepdims=True)
        rounded = weights.astype(BF16)
        for head in range(heads):
            out = jnp.dot(
                rounded[head * block:(head + 1) * block], v_ref[row, head], preferred_element_type=F32
            )
            pair = row * heads + head
            for i in range(levels):
                chunks[i // 2][i % 2, pair * per:(pair + 1) * per, :] = out[i * per:(i + 1) * per]
            here = pair_lane == pair
            peaks = jnp.where(here, peak[head * block:(head + 1) * block], peaks)
            totals = jnp.where(here, total[head * block:(head + 1) * block], totals)
    base = rows * q_heads
    for i in range(levels):
        chunks[i // 2][i % 2, base:base + per, :] = peaks[i * per:(i + 1) * per]
        chunks[i // 2][i % 2, base + per:base + 2 * per, :] = totals[i * per:(i + 1) * per]
    stats_ref[0] = peaks
    stats_ref[1] = totals


def place_of(me):
    return lax.rem(me, 2) * 2 + lax.rem(me // 2, 2)


def merge(swap, own, got, pairs, per, own_stats=None, got_stats=None):
    def both(rows, own=own, got=got):
        x, y = own[rows, :], got[rows, :]
        return jnp.where(swap, y, x), jnp.where(swap, x, y)

    scaled = own_stats is not None
    base = 0 if scaled else pairs * per
    stats = (own_stats, got_stats) if scaled else (own, got)
    peaks = both(slice(base, base + per), *stats)
    totals = both(slice(base + per, base + 2 * per), *stats)
    peak = jnp.maximum(*peaks)
    factors = [jnp.exp(x - peak) for x in peaks]
    total = factors[0] * totals[0] + factors[1] * totals[1]
    if scaled:
        scales = both(slice(2 * per, 3 * per), *stats)
        factors = [f * x for f, x in zip(factors, scales)]

    def summed(pair):
        first, second = [jnp.broadcast_to(f[:, pair:pair + 1], (per, LANES)) for f in factors]
        x, y = both(slice(pair * per, (pair + 1) * per))
        return first * x + second * y

    return peak, total, summed


def merge_kernel(bit, pairs, per, me_ref, own, got, *outs):
    swap = lax.rem(me_ref[0] // bit, 2) == 1
    base = pairs * per
    for i, out in enumerate(outs):
        x, y = (own, got) if len(outs) == 1 else (own.at[i], got.at[i])
        peak, total, summed = merge(swap, x, y, pairs, per)
        for pair in range(pairs):
            out[pair * per:(pair + 1) * per, :] = summed(pair)
        out[base:base + per, :] = peak
        out[base + per:base + 2 * per, :] = total


def scale_kernel(pairs, per, block, sums, stats):
    lane = lax.broadcasted_iota(jnp.int32, (per, LANES), 1)
    base = pairs * per
    scales = jnp.ones((per, LANES), F32)
    for pair in range(pairs):
        x = block[pair * per:(pair + 1) * per, :]
        largest = jnp.max(jnp.abs(x), axis=1, keepdims=True)
        largest = jnp.where(largest > 0.0, largest, 1.0)
        sums[pair * per:(pair + 1) * per, :] = x / largest
        scales = jnp.where(lane == pair, largest, scales)
    stats[:2 * per, :] = block[base:base + 2 * per, :]
    stats[2 * per:, :] = scales


def last_kernel(bit, pairs, per, me_ref, own, got, own_stats, got_stats, out):
    swap = lax.rem(me_ref[0] // bit, 2) == 1
    base = pairs * per
    peak, total, summed = merge(swap, own, got, pairs, per, own_stats, got_stats)
    lane = lax.broadcasted_iota(jnp.int32, peak.shape, 1)
    total = jnp.where(lane < pairs, total, 1.0)
    peak = jnp.where(lane < pairs, peak, 0.0)

    def result(pair):
        return summed(pair) / jnp.broadcast_to(total[:, pair:pair + 1], (per, LANES))

    for pair in range(0, pairs, 2):
        both = jnp.concatenate([result(pair), result(pair + 1)], axis=0)
        out[pair * per:(pair + 2) * per, :] = both.astype(BF16)
    rest = jnp.concatenate([peak, total], axis=0)
    lane = lax.broadcasted_iota(jnp.int32, rest.shape, 1)
    parts = []
    for i in range(3):
        parts.append(rest.astype(BF16).astype(F32))
        rest = rest - parts[i]
    half = LANES // 2
    packed = jnp.where(lane < half, parts[0], pltpu.roll(parts[1], half, 1))
    out[base:base + 2 * per, :] = packed.astype(BF16)
    out[base + 2 * per:base + 4 * per, :] = parts[2].astype(BF16)


def finish_kernel(pairs, per, heads, levels, me_ref, stats_ref, *refs):
    ins, out, mass_ref = refs[:levels], refs[levels], refs[levels + 1]
    base = pairs * per
    lane = lax.broadcasted_iota(jnp.int32, (2 * per, LANES), 1)
    mass = jnp.zeros((per, LANES), F32)
    for level in range(levels):
        step = jnp.bitwise_xor(place_of(me_ref[0]), level)
        out[step] = ins[level][:base, :]
        packed = ins[level][base:base + 2 * per, :].astype(F32)
        third = ins[level][base + 2 * per:base + 4 * per, :].astype(F32)
        both = third + pltpu.roll(packed, LANES // 2, 1) + packed
        both = jnp.where(lane < pairs, both, 1.0)
        at = level * per
        coefficient = jnp.exp(jnp.minimum(stats_ref[0, at:at + per, :] - both[:per], 0.0)) / both[per:]
        mass = mass + stats_ref[1, at:at + per, :] * coefficient
    mass = jnp.sum(mass, axis=0, keepdims=True)
    for row in range(pairs // heads):
        mass_ref[row] = mass[:, row * heads:(row + 1) * heads]


def place_kernel(devices, group, me_ref, table, got_ref, out_ref, sem):
    heads = out_ref.shape[1]
    me = me_ref[0]
    for offset in range(devices):
        source = jnp.bitwise_and(me + devices - offset, devices - 1)
        for k in range(group):
            pair = table[offset * group + k]

            @pl.when(pair >= 0)
            def _():
                dst = out_ref.at[pair // heads, lax.rem(pair, heads)]
                pltpu.make_async_copy(got_ref.at[source * group + k], dst, sem).start()
    pltpu.make_async_copy(out_ref, out_ref, sem).wait()


def local(queries, key_cache, value_cache, row_lengths, kept_tiles, tile_dest):
    devices = lax.axis_size("ctx")
    rows, heads, span, width = key_cache.shape
    steps, _, q_heads, _ = queries.shape
    per = q_heads // heads
    pairs = rows * heads
    group = -(-pairs // devices)
    levels = 4
    assert steps == levels and tile_dest.shape[2] == devices and pairs % 2 == 0 and pairs <= LANES // 2
    assert devices > levels and devices & (devices - 1) == 0 and width == LANES

    me = lax.axis_index("ctx").astype(jnp.int32).reshape(1)
    kept = jnp.transpose(kept_tiles, (1, 0, 2))
    block_rows = rows * q_heads + 2 * per
    block_type = jax.ShapeDtypeStruct((block_rows, width), F32)
    message_type = jax.ShapeDtypeStruct((rows * q_heads + 4 * per, width), BF16)
    tiles_type = jax.ShapeDtypeStruct((devices * group, span, width), BF16)

    def stage(name, params, me, dest, x):
        return pl.pallas_call(
            functools.partial(stage_kernel, devices, group),
            out_shape=[
                tiles_type,
                jax.ShapeDtypeStruct((devices * group,), jnp.int32),
                jax.ShapeDtypeStruct((1,), jnp.int32),
            ],
            in_specs=[SMEM, HBM, HBM],
            out_specs=[HBM, SMEM, SMEM],
            scratch_shapes=[
                pltpu.VMEM(x.shape, BF16),
                pltpu.SMEM(dest.shape, jnp.int32),
                pltpu.SMEM((devices,), jnp.int32),
                pltpu.SemaphoreType.DMA((2,)),
                pltpu.SemaphoreType.DMA((rows,)),
            ],
            compiler_params=params,
            cost_estimate=COST,
            name=name,
        )(me, dest, x)

    def exchange(x):
        return lax.all_to_all(x, "ctx", split_axis=0, concat_axis=0, tiled=True)

    keys_out, table, me_next = stage("stage_keys", WHOLE, me, tile_dest, key_cache)
    keys_in = exchange(keys_out)

    stats, *chunks = pl.pallas_call(
        functools.partial(attend_kernel, levels),
        out_shape=[
            jax.ShapeDtypeStruct((2, steps * per, LANES), F32),
        ] + [jax.ShapeDtypeStruct((2, block_rows, width), F32)] * 2,
        in_specs=[SMEM, SMEM, HBM, HBM, VMEM, VMEM, VMEM],
        out_specs=[VMEM] * 3,
        scratch_shapes=[
            pltpu.SMEM(row_lengths.shape, jnp.int32),
            pltpu.SMEM(kept.shape, jnp.int32),
            pltpu.SemaphoreType.DMA((2,)),
        ],
        compiler_params=PARAMS,
        cost_estimate=COST,
        name="attend",
    )(me, table, row_lengths, kept, queries, key_cache, value_cache)

    values_out, _, _ = stage("stage_values", PARAMS, me_next, tile_dest, value_cache)
    values_in = exchange(values_out)

    def flip(x, bit):
        return lax.ppermute(x, "ctx", [(i, i ^ bit) for i in range(devices)])

    def local_call(kernel, name, out_shape, *operands):
        return pl.pallas_call(
            kernel,
            out_shape=out_shape,
            in_specs=[SMEM if x is me or x.shape == (1,) else VMEM for x in operands],
            out_specs=[VMEM] * len(out_shape),
            compiler_params=PARAMS,
            cost_estimate=COST,
            name=name,
        )(*operands)

    def merged(name, bit, own, got, out_shape):
        return local_call(functools.partial(merge_kernel, bit, pairs, per), name, out_shape, me, own, got)

    block, sent = merged("core", 1, chunks[0], flip(chunks[1], 1), [block_type] * 2)
    block, = merged("near", 2, block, flip(sent, 2), [block_type])
    bit = levels
    while 2 * bit < devices:
        block, = merged("far", bit, block, flip(block, bit), [block_type])
        bit *= 2
    sums_type = jax.ShapeDtypeStruct((rows * q_heads, width), F32)
    stats_type = jax.ShapeDtypeStruct((3 * per, width), F32)
    sums, sum_stats = local_call(functools.partial(scale_kernel, pairs, per), "scale", [sums_type, stats_type], block)
    sums = lax.reduce_precision(sums, 5, 10)
    got = flip(sums.astype(jnp.float16), bit).astype(F32)
    message, = local_call(
        functools.partial(last_kernel, bit, pairs, per), "last", [message_type],
        me, sums, got, sum_stats, flip(sum_stats, bit),
    )
    other = flip(message, 2)

    def place(name, got):
        return pl.pallas_call(
            functools.partial(place_kernel, devices, group),
            out_shape=jax.ShapeDtypeStruct(key_cache.shape, BF16),
            in_specs=[SMEM, SMEM, ANY],
            out_specs=HBM,
            scratch_shapes=[pltpu.SemaphoreType.DMA],
            compiler_params=PARAMS,
            cost_estimate=COST,
            name=name,
        )(me, table, got)

    moved_keys = place("place_keys", keys_in)
    moved_values = place("place_values", values_in)
    arrived = [message, other, flip(message, 1), flip(other, 1)]
    attn_out, mass = pl.pallas_call(
        functools.partial(finish_kernel, pairs, per, heads, levels),
        out_shape=[
            jax.ShapeDtypeStruct((steps, rows * q_heads, width), BF16),
            jax.ShapeDtypeStruct((rows, 1, heads), F32),
        ],
        in_specs=[SMEM, VMEM] + [VMEM] * levels,
        out_specs=[VMEM, VMEM],
        compiler_params=PARAMS,
        cost_estimate=COST,
        name="finish",
    )(me, stats, *arrived)
    return attn_out.reshape(queries.shape), jnp.transpose(mass, (0, 2, 1)), moved_keys, moved_values


def solution(mesh):
    in_specs = (
        P(None, "grp", None, None),
        P("grp", None, "ctx", None),
        P("grp", None, "ctx", None),
        P("grp"),
        P(None, "grp", None),
        P("grp", None, None),
    )
    out_specs = (
        P(None, "grp", None, None),
        P("grp", None, "ctx"),
        P("grp", None, "ctx", None),
        P("grp", None, "ctx", None),
    )
    return jax.shard_map(local, mesh=mesh, in_specs=in_specs, out_specs=out_specs, check_vma=False)
```

```python
import functools

import jax
import jax.numpy as jnp
from jax import lax
from jax.experimental import pallas as pl
from jax.experimental.pallas import tpu as pltpu
from jax.sharding import PartitionSpec as P

absent_score = -1e30
LANES = 128
F32 = jnp.float32
BF16 = jnp.bfloat16
VMEM = pl.BlockSpec(memory_space=pltpu.VMEM)
SMEM = pl.BlockSpec(memory_space=pltpu.SMEM)
HBM = pl.BlockSpec(memory_space=pltpu.HBM)
ANY = pl.BlockSpec(memory_space=pl.ANY)
PARAMS = pltpu.CompilerParams(vmem_limit_bytes=16 * 1024 * 1024)
WHOLE = pltpu.CompilerParams(vmem_limit_bytes=62 * 1024 * 1024)


COST = pl.CostEstimate(flops=1000, bytes_accessed=1000, transcendentals=0)


def stage_kernel(devices, group, me_ref, dest_hbm, k_ref, v_ref, buf, table, k_vm, v_vm, dest, counts, sem, load_sem):
    rows, heads = k_ref.shape[:2]
    small = pltpu.make_async_copy(dest_hbm, dest, sem.at[0])
    small.start()
    loads = []
    for row in range(rows):
        for which, (src, dst) in enumerate(((k_ref, k_vm), (v_ref, v_vm))):
            copy = pltpu.make_async_copy(src.at[row], dst.at[row], load_sem.at[which, row])
            copy.start()
            loads.append(copy)
    me = me_ref[0]

    def clear(i, carry):
        counts[i] = 0
        for k in range(group):
            table[i * group + k] = -1
        return carry

    lax.fori_loop(0, devices, clear, 0)
    small.wait()
    for row in range(rows):
        loads[2 * row].wait()
        loads[2 * row + 1].wait()

        for head in range(heads):
            offset = dest[row, head, 0]
            rank = counts[offset]
            counts[offset] = rank + 1
            table[offset * group + rank] = row * heads + head
            slot = jnp.bitwise_and(me + offset, devices - 1) * group + rank
            pltpu.make_async_copy(k_vm.at[row, head], buf.at[slot, 0], sem.at[1]).start()
            pltpu.make_async_copy(v_vm.at[row, head], buf.at[slot, 1], sem.at[2]).start()
    pltpu.make_async_copy(k_ref, k_vm, sem.at[1]).wait()
    pltpu.make_async_copy(v_ref, v_vm, sem.at[2]).wait()


def attend_kernel(
    levels,
    me_ref, table, len_hbm, kept_hbm, q_ref, k_ref, v_ref,
    stats_ref, *rest,
):
    chunks = rest[:levels // 2]
    len_ref, kept_ref, small_sem = rest[levels // 2:]
    rows, heads, tile, width = k_ref.shape
    steps, _, q_heads, _ = q_ref.shape
    per = q_heads // heads
    me = me_ref[0]

    small = [
        pltpu.make_async_copy(len_hbm, len_ref, small_sem.at[0]),
        pltpu.make_async_copy(kept_hbm, kept_ref, small_sem.at[1]),
    ]
    for copy in small:
        copy.start()
    for copy in small:
        copy.wait()

    lane = lax.broadcasted_iota(jnp.int32, (per, tile), 1)
    pair_lane = lax.broadcasted_iota(jnp.int32, (steps * per, LANES), 1)
    peaks = jnp.full((steps * per, LANES), absent_score, F32)
    totals = jnp.zeros((steps * per, LANES), F32)
    order = [jnp.bitwise_xor(place_of(me), level) for level in range(levels)]
    scale = width ** -0.5
    block = steps * per
    for row in range(rows):
        queries = [q_ref[step, row].astype(F32) for step in order]
        live = []
        for step in order:
            limit = jnp.where(kept_ref[row, step, me] > 0, len_ref[row] - me * tile, 0)
            live.append(lane < limit)
        live = jnp.concatenate(live * heads, axis=0)
        scores = []
        for head in range(heads):
            q = jnp.concatenate([x[head * per:(head + 1) * per] for x in queries], axis=0).astype(BF16)
            scores.append(lax.dot_general(
                q, k_ref[row, head], (((1,), (1,)), ((), ())), preferred_element_type=F32
            ))
        scores = jnp.concatenate(scores, axis=0) * scale
        peak = jnp.max(jnp.where(live, scores, absent_score), axis=1, keepdims=True)
        weights = jnp.where(live, jnp.exp(scores - peak), 0.0)
        total = jnp.sum(weights, axis=1, keepdims=True)
        rounded = weights.astype(BF16)
        for head in range(heads):
            out = jnp.dot(
                rounded[head * block:(head + 1) * block], v_ref[row, head], preferred_element_type=F32
            )
            pair = row * heads + head
            for i in range(levels):
                chunks[i // 2][i % 2, pair * per:(pair + 1) * per, :] = out[i * per:(i + 1) * per]
            here = pair_lane == pair
            peaks = jnp.where(here, peak[head * block:(head + 1) * block], peaks)
            totals = jnp.where(here, total[head * block:(head + 1) * block], totals)
    base = rows * q_heads
    for i in range(levels):
        chunks[i // 2][i % 2, base:base + per, :] = peaks[i * per:(i + 1) * per]
        chunks[i // 2][i % 2, base + per:base + 2 * per, :] = totals[i * per:(i + 1) * per]
    stats_ref[0] = peaks
    stats_ref[1] = totals


def place_of(me):
    return lax.rem(me, 2) * 2 + lax.rem(me // 2, 2)


def merge(swap, own, got, pairs, per, own_stats=None, got_stats=None):
    def both(rows, own=own, got=got):
        x, y = own[rows, :], got[rows, :]
        return jnp.where(swap, y, x), jnp.where(swap, x, y)

    scaled = own_stats is not None
    base = 0 if scaled else pairs * per
    stats = (own_stats, got_stats) if scaled else (own, got)
    peaks = both(slice(base, base + per), *stats)
    totals = both(slice(base + per, base + 2 * per), *stats)
    peak = jnp.maximum(*peaks)
    factors = [jnp.exp(x - peak) for x in peaks]
    total = factors[0] * totals[0] + factors[1] * totals[1]
    if scaled:
        scales = both(slice(2 * per, 3 * per), *stats)
        factors = [f * x for f, x in zip(factors, scales)]

    def summed(pair):
        first, second = [jnp.broadcast_to(f[:, pair:pair + 1], (per, LANES)) for f in factors]
        x, y = both(slice(pair * per, (pair + 1) * per))
        return first * x + second * y

    return peak, total, summed


def merge_kernel(bit, pairs, per, me_ref, own, got, *outs):
    swap = lax.rem(me_ref[0] // bit, 2) == 1
    base = pairs * per
    for i, out in enumerate(outs):
        x, y = (own, got) if len(outs) == 1 else (own.at[i], got.at[i])
        peak, total, summed = merge(swap, x, y, pairs, per)
        for pair in range(pairs):
            out[pair * per:(pair + 1) * per, :] = summed(pair)
        out[base:base + per, :] = peak
        out[base + per:base + 2 * per, :] = total


def scale_kernel(pairs, per, block, sums, stats):
    lane = lax.broadcasted_iota(jnp.int32, (per, LANES), 1)
    base = pairs * per
    scales = jnp.ones((per, LANES), F32)
    for pair in range(pairs):
        x = block[pair * per:(pair + 1) * per, :]
        largest = jnp.max(jnp.abs(x), axis=1, keepdims=True)
        largest = jnp.where(largest > 0.0, largest, 1.0)
        sums[pair * per:(pair + 1) * per, :] = x / largest
        scales = jnp.where(lane == pair, largest, scales)
    stats[:2 * per, :] = block[base:base + 2 * per, :]
    stats[2 * per:, :] = scales


def last_kernel(bit, pairs, per, me_ref, own, got, own_stats, got_stats, out):
    swap = lax.rem(me_ref[0] // bit, 2) == 1
    base = pairs * per
    peak, total, summed = merge(swap, own, got, pairs, per, own_stats, got_stats)
    lane = lax.broadcasted_iota(jnp.int32, peak.shape, 1)
    total = jnp.where(lane < pairs, total, 1.0)
    peak = jnp.where(lane < pairs, peak, 0.0)

    def result(pair):
        return summed(pair) / jnp.broadcast_to(total[:, pair:pair + 1], (per, LANES))

    for pair in range(0, pairs, 2):
        both = jnp.concatenate([result(pair), result(pair + 1)], axis=0)
        out[pair * per:(pair + 2) * per, :] = both.astype(BF16)
    rest = jnp.concatenate([peak, total], axis=0)
    lane = lax.broadcasted_iota(jnp.int32, rest.shape, 1)
    parts = []
    for i in range(3):
        parts.append(rest.astype(BF16).astype(F32))
        rest = rest - parts[i]
    half = LANES // 2
    packed = jnp.where(lane < half, parts[0], pltpu.roll(parts[1], half, 1))
    out[base:base + 2 * per, :] = packed.astype(BF16)
    out[base + 2 * per:base + 4 * per, :] = parts[2].astype(BF16)


def finish_kernel(pairs, per, heads, levels, me_ref, stats_ref, *refs):
    ins, (out, mass_ref, sem) = refs[:levels], refs[levels:]
    base = pairs * per
    copies = [
        pltpu.make_async_copy(
            ins[level].at[:base], out.at[jnp.bitwise_xor(place_of(me_ref[0]), level)], sem.at[level]
        )
        for level in range(levels)
    ]
    for copy in copies:
        copy.start()
    lane = lax.broadcasted_iota(jnp.int32, (2 * per, LANES), 1)
    mass = jnp.zeros((per, LANES), F32)
    for level in range(levels):
        packed = ins[level][base:base + 2 * per, :].astype(F32)
        third = ins[level][base + 2 * per:base + 4 * per, :].astype(F32)
        both = third + pltpu.roll(packed, LANES // 2, 1) + packed
        both = jnp.where(lane < pairs, both, 1.0)
        at = level * per
        coefficient = jnp.exp(jnp.minimum(stats_ref[0, at:at + per, :] - both[:per], 0.0)) / both[per:]
        mass = mass + stats_ref[1, at:at + per, :] * coefficient
    mass = jnp.sum(mass, axis=0, keepdims=True)
    for row in range(pairs // heads):
        mass_ref[row] = mass[:, row * heads:(row + 1) * heads]
    for copy in copies:
        copy.wait()


def place_kernel(devices, group, me_ref, table, got_ref, k_ref, v_ref, me_out, sem):
    heads = k_ref.shape[1]
    me = me_ref[0]
    me_out[0] = me
    for offset in range(devices):
        source = jnp.bitwise_and(me + devices - offset, devices - 1)
        for k in range(group):
            pair = table[offset * group + k]

            @pl.when(pair >= 0)
            def _():
                row, head = pair // heads, lax.rem(pair, heads)
                for which, ref in enumerate((k_ref, v_ref)):
                    src = got_ref.at[source * group + k, which]
                    pltpu.make_async_copy(src, ref.at[row, head], sem.at[which]).start()
    pltpu.make_async_copy(k_ref, k_ref, sem.at[0]).wait()
    pltpu.make_async_copy(v_ref, v_ref, sem.at[1]).wait()


def local(queries, key_cache, value_cache, row_lengths, kept_tiles, tile_dest):
    devices = lax.axis_size("ctx")
    rows, heads, span, width = key_cache.shape
    steps, _, q_heads, _ = queries.shape
    per = q_heads // heads
    pairs = rows * heads
    group = -(-pairs // devices)
    levels = 4
    assert steps == levels and tile_dest.shape[2] == devices and pairs % 2 == 0 and pairs <= LANES // 2
    assert devices > levels and devices & (devices - 1) == 0 and width == LANES

    me = lax.axis_index("ctx").astype(jnp.int32).reshape(1)
    kept = jnp.transpose(kept_tiles, (1, 0, 2))
    block_rows = rows * q_heads + 2 * per
    block_type = jax.ShapeDtypeStruct((block_rows, width), F32)
    message_type = jax.ShapeDtypeStruct((rows * q_heads + 4 * per, width), BF16)
    tiles_type = jax.ShapeDtypeStruct((devices * group, 2, span, width), BF16)

    tiles_out, table = pl.pallas_call(
        functools.partial(stage_kernel, devices, group),
        out_shape=[tiles_type, jax.ShapeDtypeStruct((devices * group,), jnp.int32)],
        in_specs=[SMEM, HBM, HBM, HBM],
        out_specs=[HBM, SMEM],
        scratch_shapes=[
            pltpu.VMEM(key_cache.shape, BF16),
            pltpu.VMEM(value_cache.shape, BF16),
            pltpu.SMEM(tile_dest.shape, jnp.int32),
            pltpu.SMEM((devices,), jnp.int32),
            pltpu.SemaphoreType.DMA((3,)),
            pltpu.SemaphoreType.DMA((2, rows)),
        ],
        compiler_params=WHOLE,
        cost_estimate=COST,
        name="stage",
    )(me, tile_dest, key_cache, value_cache)
    tiles_in = lax.all_to_all(tiles_out, "ctx", split_axis=0, concat_axis=0, tiled=True)

    stats, *chunks = pl.pallas_call(
        functools.partial(attend_kernel, levels),
        out_shape=[
            jax.ShapeDtypeStruct((2, steps * per, LANES), F32),
        ] + [jax.ShapeDtypeStruct((2, block_rows, width), F32)] * 2,
        in_specs=[SMEM, SMEM, HBM, HBM, VMEM, VMEM, VMEM],
        out_specs=[VMEM] * 3,
        scratch_shapes=[
            pltpu.SMEM(row_lengths.shape, jnp.int32),
            pltpu.SMEM(kept.shape, jnp.int32),
            pltpu.SemaphoreType.DMA((2,)),
        ],
        compiler_params=PARAMS,
        cost_estimate=COST,
        name="attend",
    )(me, table, row_lengths, kept, queries, key_cache, value_cache)

    def flip(x, bit):
        return lax.ppermute(x, "ctx", [(i, i ^ bit) for i in range(devices)])

    def local_call(kernel, name, out_shape, *operands):
        return pl.pallas_call(
            kernel,
            out_shape=out_shape,
            in_specs=[SMEM if x is me or x.shape == (1,) else VMEM for x in operands],
            out_specs=[VMEM] * len(out_shape),
            compiler_params=PARAMS,
            cost_estimate=COST,
            name=name,
        )(*operands)

    def merged(name, bit, own, got, out_shape):
        return local_call(functools.partial(merge_kernel, bit, pairs, per), name, out_shape, me, own, got)

    block, sent = merged("core", 1, chunks[0], flip(chunks[1], 1), [block_type] * 2)
    block, = merged("near", 2, block, flip(sent, 2), [block_type])
    bit = levels
    while 2 * bit < devices:
        block, = merged("far", bit, block, flip(block, bit), [block_type])
        bit *= 2
    sums_type = jax.ShapeDtypeStruct((rows * q_heads, width), F32)
    stats_type = jax.ShapeDtypeStruct((3 * per, width), F32)
    sums, sum_stats = local_call(functools.partial(scale_kernel, pairs, per), "scale", [sums_type, stats_type], block)
    sums = lax.reduce_precision(sums, 5, 10)
    got = flip(sums.astype(jnp.float16), bit).astype(F32)
    moved_keys, moved_values, me_next = pl.pallas_call(
        functools.partial(place_kernel, devices, group),
        out_shape=[
            jax.ShapeDtypeStruct(key_cache.shape, BF16),
            jax.ShapeDtypeStruct(value_cache.shape, BF16),
            jax.ShapeDtypeStruct((1,), jnp.int32),
        ],
        in_specs=[SMEM, SMEM, ANY],
        out_specs=[HBM, HBM, SMEM],
        scratch_shapes=[pltpu.SemaphoreType.DMA((2,))],
        compiler_params=PARAMS,
        cost_estimate=COST,
        name="place",
    )(me, table, tiles_in)


    message, = local_call(
        functools.partial(last_kernel, bit, pairs, per), "last", [message_type],
        me_next, sums, got, sum_stats, flip(sum_stats, bit),
    )
    other = flip(message, 2)
    arrived = [message, other, flip(message, 1), flip(other, 1)]

    attn_out, mass = pl.pallas_call(
        functools.partial(finish_kernel, pairs, per, heads, levels),
        out_shape=[
            jax.ShapeDtypeStruct((steps, rows * q_heads, width), BF16),
            jax.ShapeDtypeStruct((rows, 1, heads), F32),
        ],
        in_specs=[SMEM, VMEM] + [VMEM] * levels,
        out_specs=[HBM, VMEM],
        scratch_shapes=[pltpu.SemaphoreType.DMA((levels,))],
        compiler_params=PARAMS,
        cost_estimate=COST,
        name="finish",
    )(me, stats, *arrived)
    return attn_out.reshape(queries.shape), jnp.transpose(mass, (0, 2, 1)), moved_keys, moved_values


def solution(mesh):
    in_specs = (
        P(None, "grp", None, None),
        P("grp", None, "ctx", None),
        P("grp", None, "ctx", None),
        P("grp"),
        P(None, "grp", None),
        P("grp", None, None),
    )
    out_specs = (
        P(None, "grp", None, None),
        P("grp", None, "ctx"),
        P("grp", None, "ctx", None),
        P("grp", None, "ctx", None),
    )
    return jax.shard_map(local, mesh=mesh, in_specs=in_specs, out_specs=out_specs, check_vma=False)
```

```python
import functools

import jax
import jax.numpy as jnp
from jax import lax
from jax.experimental import pallas as pl
from jax.experimental.pallas import tpu as pltpu
from jax.sharding import PartitionSpec as P

absent_score = -1e30
LANES = 128
F32 = jnp.float32
BF16 = jnp.bfloat16
VMEM = pl.BlockSpec(memory_space=pltpu.VMEM)
SMEM = pl.BlockSpec(memory_space=pltpu.SMEM)
HBM = pl.BlockSpec(memory_space=pltpu.HBM)
ANY = pl.BlockSpec(memory_space=pl.ANY)
PARAMS = pltpu.CompilerParams(vmem_limit_bytes=16 * 1024 * 1024)
WHOLE = pltpu.CompilerParams(vmem_limit_bytes=62 * 1024 * 1024)


COST = pl.CostEstimate(flops=1000, bytes_accessed=1000, transcendentals=0)


def stage_kernel(devices, group, me_ref, dest_hbm, k_ref, v_ref, buf, table, k_vm, v_vm, dest, counts, sem, load_sem):
    rows, heads = k_ref.shape[:2]
    small = pltpu.make_async_copy(dest_hbm, dest, sem.at[0])
    small.start()
    loads = []
    for row in range(rows):
        for which, (src, dst) in enumerate(((k_ref, k_vm), (v_ref, v_vm))):
            copy = pltpu.make_async_copy(src.at[row], dst.at[row], load_sem.at[which, row])
            copy.start()
            loads.append(copy)
    me = me_ref[0]

    def clear(i, carry):
        counts[i] = 0
        for k in range(group):
            table[i * group + k] = -1
        return carry

    lax.fori_loop(0, devices, clear, 0)
    small.wait()
    for row in range(rows):
        loads[2 * row].wait()
        loads[2 * row + 1].wait()

        for head in range(heads):
            offset = dest[row, head, 0]
            rank = counts[offset]
            counts[offset] = rank + 1
            table[offset * group + rank] = row * heads + head
            slot = jnp.bitwise_and(me + offset, devices - 1) * group + rank
            pltpu.make_async_copy(k_vm.at[row, head], buf.at[slot, 0], sem.at[1]).start()
            pltpu.make_async_copy(v_vm.at[row, head], buf.at[slot, 1], sem.at[2]).start()
    pltpu.make_async_copy(k_ref, k_vm, sem.at[1]).wait()
    pltpu.make_async_copy(v_ref, v_vm, sem.at[2]).wait()


def attend_kernel(
    levels,
    me_ref, table, len_hbm, kept_hbm, q_ref, k_ref, v_ref,
    stats_ref, *rest,
):
    chunks = rest[:levels // 2]
    len_ref, kept_ref, small_sem = rest[levels // 2:]
    rows, heads, tile, width = k_ref.shape
    steps, _, q_heads, _ = q_ref.shape
    per = q_heads // heads
    me = me_ref[0]

    small = [
        pltpu.make_async_copy(len_hbm, len_ref, small_sem.at[0]),
        pltpu.make_async_copy(kept_hbm, kept_ref, small_sem.at[1]),
    ]
    for copy in small:
        copy.start()
    for copy in small:
        copy.wait()

    lane = lax.broadcasted_iota(jnp.int32, (per, tile), 1)
    pair_lane = lax.broadcasted_iota(jnp.int32, (steps * per, LANES), 1)
    peaks = jnp.full((steps * per, LANES), absent_score, F32)
    totals = jnp.zeros((steps * per, LANES), F32)
    order = [jnp.bitwise_xor(place_of(me), level) for level in range(levels)]
    scale = width ** -0.5
    block = steps * per
    for row in range(rows):
        queries = [q_ref[step, row].astype(F32) for step in order]
        live = []
        for step in order:
            limit = jnp.where(kept_ref[row, step, me] > 0, len_ref[row] - me * tile, 0)
            live.append(lane < limit)
        live = jnp.concatenate(live * heads, axis=0)
        scores = []
        for head in range(heads):
            q = jnp.concatenate([x[head * per:(head + 1) * per] for x in queries], axis=0).astype(BF16)
            scores.append(lax.dot_general(
                q, k_ref[row, head], (((1,), (1,)), ((), ())), preferred_element_type=F32
            ))
        scores = jnp.concatenate(scores, axis=0) * scale
        peak = jnp.max(jnp.where(live, scores, absent_score), axis=1, keepdims=True)
        weights = jnp.where(live, jnp.exp(scores - peak), 0.0)
        total = jnp.sum(weights, axis=1, keepdims=True)
        rounded = weights.astype(BF16)
        for head in range(heads):
            out = jnp.dot(
                rounded[head * block:(head + 1) * block], v_ref[row, head], preferred_element_type=F32
            )
            pair = row * heads + head
            for i in range(levels):
                chunks[i // 2][i % 2, pair * per:(pair + 1) * per, :] = out[i * per:(i + 1) * per]
            here = pair_lane == pair
            peaks = jnp.where(here, peak[head * block:(head + 1) * block], peaks)
            totals = jnp.where(here, total[head * block:(head + 1) * block], totals)
    base = rows * q_heads
    for i in range(levels):
        chunks[i // 2][i % 2, base:base + per, :] = peaks[i * per:(i + 1) * per]
        chunks[i // 2][i % 2, base + per:base + 2 * per, :] = totals[i * per:(i + 1) * per]
    stats_ref[0] = peaks
    stats_ref[1] = totals


def place_of(me):
    return lax.rem(me, 2) * 2 + lax.rem(me // 2, 2)


def merge(swap, own, got, own_stats, got_stats, pairs, per, scaled):
    def both(x, y, rows):
        x, y = x[rows, :], y[rows, :]
        return jnp.where(swap, y, x), jnp.where(swap, x, y)

    peaks = both(own_stats, got_stats, slice(0, per))
    totals = both(own_stats, got_stats, slice(per, 2 * per))
    peak = jnp.maximum(*peaks)
    factors = [jnp.exp(x - peak) for x in peaks]
    total = factors[0] * totals[0] + factors[1] * totals[1]
    if scaled:
        factors = [f * x for f, x in zip(factors, both(own_stats, got_stats, slice(2 * per, 3 * per)))]

    def summed(pair):
        first, second = [jnp.broadcast_to(f[:, pair:pair + 1], (per, LANES)) for f in factors]
        x, y = both(own, got, slice(pair * per, (pair + 1) * per))
        return first * x + second * y

    return peak, total, summed


def put_scaled(peak, total, summed, pairs, per, sums, stats):
    lane = lax.broadcasted_iota(jnp.int32, (per, LANES), 1)
    scales = jnp.ones((per, LANES), F32)
    for pair in range(pairs):
        x = summed(pair)
        largest = jnp.max(jnp.abs(x), axis=1, keepdims=True)
        largest = jnp.where(largest > 0.0, largest, 1.0)
        sums[pair * per:(pair + 1) * per, :] = x / largest
        scales = jnp.where(lane == pair, largest, scales)
    stats[:per, :] = peak
    stats[per:2 * per, :] = total
    stats[2 * per:, :] = scales


def core_kernel(pairs, per, me_ref, own, got, *outs):
    base = pairs * per
    swap = lax.rem(me_ref[0], 2) == 1
    for i in range(2):
        x, y = own.at[i], got.at[i]
        merged = merge(swap, x, y, x.at[pl.ds(base, 2 * per)], y.at[pl.ds(base, 2 * per)], pairs, per, False)
        put_scaled(*merged, pairs, per, outs[2 * i], outs[2 * i + 1])


def merge_kernel(bit, pairs, per, me_ref, own, own_stats, got, got_stats, sums, stats):
    swap = lax.rem(me_ref[0] // bit, 2) == 1
    put_scaled(*merge(swap, own, got, own_stats, got_stats, pairs, per, True), pairs, per, sums, stats)


def last_kernel(bit, pairs, per, me_ref, own, own_stats, got, got_stats, out):
    swap = lax.rem(me_ref[0] // bit, 2) == 1
    base = pairs * per
    peak, total, summed = merge(swap, own, got, own_stats, got_stats, pairs, per, True)
    lane = lax.broadcasted_iota(jnp.int32, peak.shape, 1)
    total = jnp.where(lane < pairs, total, 1.0)
    peak = jnp.where(lane < pairs, peak, 0.0)

    def result(pair):
        return summed(pair) / jnp.broadcast_to(total[:, pair:pair + 1], (per, LANES))

    for pair in range(0, pairs, 2):
        both = jnp.concatenate([result(pair), result(pair + 1)], axis=0)
        out[pair * per:(pair + 2) * per, :] = both.astype(BF16)
    rest = jnp.concatenate([peak, total], axis=0)
    lane = lax.broadcasted_iota(jnp.int32, rest.shape, 1)
    parts = []
    for i in range(3):
        parts.append(rest.astype(BF16).astype(F32))
        rest = rest - parts[i]
    half = LANES // 2
    packed = jnp.where(lane < half, parts[0], pltpu.roll(parts[1], half, 1))
    out[base:base + 2 * per, :] = packed.astype(BF16)
    out[base + 2 * per:base + 4 * per, :] = parts[2].astype(BF16)


def pass_kernel(me_ref, x, out):
    out[...] = x[...]


def finish_kernel(pairs, per, heads, levels, me_ref, stats_ref, *refs):
    ins, (out, mass_ref, sem) = refs[:levels], refs[levels:]
    base = pairs * per
    copies = [
        pltpu.make_async_copy(
            ins[level].at[:base], out.at[jnp.bitwise_xor(place_of(me_ref[0]), level)], sem.at[level]
        )
        for level in range(levels)
    ]
    for copy in copies:
        copy.start()
    lane = lax.broadcasted_iota(jnp.int32, (2 * per, LANES), 1)
    mass = jnp.zeros((per, LANES), F32)
    for level in range(levels):
        packed = ins[level][base:base + 2 * per, :].astype(F32)
        third = ins[level][base + 2 * per:base + 4 * per, :].astype(F32)
        both = third + pltpu.roll(packed, LANES // 2, 1) + packed
        both = jnp.where(lane < pairs, both, 1.0)
        at = level * per
        coefficient = jnp.exp(jnp.minimum(stats_ref[0, at:at + per, :] - both[:per], 0.0)) / both[per:]
        mass = mass + stats_ref[1, at:at + per, :] * coefficient
    mass = jnp.sum(mass, axis=0, keepdims=True)
    for row in range(pairs // heads):
        mass_ref[row] = mass[:, row * heads:(row + 1) * heads]
    for copy in copies:
        copy.wait()


def place_kernel(devices, group, me_ref, table, got_ref, k_ref, v_ref, me_out, sem):
    heads = k_ref.shape[1]
    me = me_ref[0]
    me_out[0] = me
    for offset in range(devices):
        source = jnp.bitwise_and(me + devices - offset, devices - 1)
        for k in range(group):
            pair = table[offset * group + k]

            @pl.when(pair >= 0)
            def _():
                row, head = pair // heads, lax.rem(pair, heads)
                for which, ref in enumerate((k_ref, v_ref)):
                    src = got_ref.at[source * group + k, which]
                    pltpu.make_async_copy(src, ref.at[row, head], sem.at[which]).start()
    pltpu.make_async_copy(k_ref, k_ref, sem.at[0]).wait()
    pltpu.make_async_copy(v_ref, v_ref, sem.at[1]).wait()


def local(queries, key_cache, value_cache, row_lengths, kept_tiles, tile_dest):
    devices = lax.axis_size("ctx")
    rows, heads, span, width = key_cache.shape
    steps, _, q_heads, _ = queries.shape
    per = q_heads // heads
    pairs = rows * heads
    group = -(-pairs // devices)
    levels = 4
    assert steps == levels and tile_dest.shape[2] == devices and pairs % 2 == 0 and pairs <= LANES // 2
    assert devices > levels and devices & (devices - 1) == 0 and width == LANES

    me = lax.axis_index("ctx").astype(jnp.int32).reshape(1)
    kept = jnp.transpose(kept_tiles, (1, 0, 2))
    block_rows = rows * q_heads + 2 * per
    block_type = jax.ShapeDtypeStruct((block_rows, width), F32)
    message_type = jax.ShapeDtypeStruct((rows * q_heads + 4 * per, width), BF16)
    tiles_type = jax.ShapeDtypeStruct((devices * group, 2, span, width), BF16)

    tiles_out, table = pl.pallas_call(
        functools.partial(stage_kernel, devices, group),
        out_shape=[tiles_type, jax.ShapeDtypeStruct((devices * group,), jnp.int32)],
        in_specs=[SMEM, HBM, HBM, HBM],
        out_specs=[HBM, SMEM],
        scratch_shapes=[
            pltpu.VMEM(key_cache.shape, BF16),
            pltpu.VMEM(value_cache.shape, BF16),
            pltpu.SMEM(tile_dest.shape, jnp.int32),
            pltpu.SMEM((devices,), jnp.int32),
            pltpu.SemaphoreType.DMA((3,)),
            pltpu.SemaphoreType.DMA((2, rows)),
        ],
        compiler_params=WHOLE,
        cost_estimate=COST,
        name="stage",
    )(me, tile_dest, key_cache, value_cache)
    tiles_in = lax.all_to_all(tiles_out, "ctx", split_axis=0, concat_axis=0, tiled=True)

    stats, *chunks = pl.pallas_call(
        functools.partial(attend_kernel, levels),
        out_shape=[
            jax.ShapeDtypeStruct((2, steps * per, LANES), F32),
        ] + [jax.ShapeDtypeStruct((2, block_rows, width), F32)] * 2,
        in_specs=[SMEM, SMEM, HBM, HBM, VMEM, VMEM, VMEM],
        out_specs=[VMEM] * 3,
        scratch_shapes=[
            pltpu.SMEM(row_lengths.shape, jnp.int32),
            pltpu.SMEM(kept.shape, jnp.int32),
            pltpu.SemaphoreType.DMA((2,)),
        ],
        compiler_params=PARAMS,
        cost_estimate=COST,
        name="attend",
    )(me, table, row_lengths, kept, queries, key_cache, value_cache)

    def flip(x, bit):
        return lax.ppermute(x, "ctx", [(i, i ^ bit) for i in range(devices)])

    def local_call(kernel, name, out_shape, *operands):
        return pl.pallas_call(
            kernel,
            out_shape=out_shape,
            in_specs=[SMEM if x is me or x.shape == (1,) else VMEM for x in operands],
            out_specs=[VMEM] * len(out_shape),
            compiler_params=PARAMS,
            cost_estimate=COST,
            name=name,
        )(*operands)

    sums_type = jax.ShapeDtypeStruct((rows * q_heads, width), F32)
    stats_type = jax.ShapeDtypeStruct((3 * per, width), F32)

    def flip_sums(sums, stats, bit):
        return flip(sums.astype(jnp.float16), bit).astype(F32), flip(stats, bit)

    def rounded(x):
        return lax.reduce_precision(x, 5, 10)

    sums, stats_own, sent, sent_stats = local_call(
        functools.partial(core_kernel, pairs, per), "core", [sums_type, stats_type] * 2,
        me, chunks[0], flip(chunks[1], 1),
    )
    bit, other = 2, flip_sums(rounded(sent), sent_stats, 2)
    while 2 * bit < devices:
        sums, stats_own = local_call(
            functools.partial(merge_kernel, bit, pairs, per), "merge", [sums_type, stats_type],
            me, sums, stats_own, *other,
        )
        sums, bit = rounded(sums), 2 * bit
        other = flip_sums(sums, stats_own, bit)
    message, = local_call(
        functools.partial(last_kernel, bit, pairs, per), "last", [message_type], me, sums, stats_own, *other,
    )
    other = flip(message, 2)

    moved_keys, moved_values, me_next = pl.pallas_call(
        functools.partial(place_kernel, devices, group),
        out_shape=[
            jax.ShapeDtypeStruct(key_cache.shape, BF16),
            jax.ShapeDtypeStruct(value_cache.shape, BF16),
            jax.ShapeDtypeStruct((1,), jnp.int32),
        ],
        in_specs=[SMEM, SMEM, ANY],
        out_specs=[HBM, HBM, SMEM],
        scratch_shapes=[pltpu.SemaphoreType.DMA((2,))],
        compiler_params=PARAMS,
        cost_estimate=COST,
        name="place",
    )(me, table, tiles_in)


    other_next, = local_call(pass_kernel, "pass", [message_type], me_next, other)
    arrived = [message, other, flip(message, 1), flip(other_next, 1)]

    attn_out, mass = pl.pallas_call(
        functools.partial(finish_kernel, pairs, per, heads, levels),
        out_shape=[
            jax.ShapeDtypeStruct((steps, rows * q_heads, width), BF16),
            jax.ShapeDtypeStruct((rows, 1, heads), F32),
        ],
        in_specs=[SMEM, VMEM] + [VMEM] * levels,
        out_specs=[HBM, VMEM],
        scratch_shapes=[pltpu.SemaphoreType.DMA((levels,))],
        compiler_params=PARAMS,
        cost_estimate=COST,
        name="finish",
    )(me, stats, *arrived)
    return attn_out.reshape(queries.shape), jnp.transpose(mass, (0, 2, 1)), moved_keys, moved_values


def solution(mesh):
    in_specs = (
        P(None, "grp", None, None),
        P("grp", None, "ctx", None),
        P("grp", None, "ctx", None),
        P("grp"),
        P(None, "grp", None),
        P("grp", None, None),
    )
    out_specs = (
        P(None, "grp", None, None),
        P("grp", None, "ctx"),
        P("grp", None, "ctx", None),
        P("grp", None, "ctx", None),
    )
    return jax.shard_map(local, mesh=mesh, in_specs=in_specs, out_specs=out_specs, check_vma=False)
```

```python
import functools

import jax
import jax.numpy as jnp
from jax import lax
from jax.experimental import pallas as pl
from jax.experimental.pallas import tpu as pltpu
from jax.sharding import PartitionSpec as P

absent_score = -1e30
LANES = 128
F32 = jnp.float32
BF16 = jnp.bfloat16
VMEM = pl.BlockSpec(memory_space=pltpu.VMEM)
SMEM = pl.BlockSpec(memory_space=pltpu.SMEM)
HBM = pl.BlockSpec(memory_space=pltpu.HBM)
ANY = pl.BlockSpec(memory_space=pl.ANY)
PARAMS = pltpu.CompilerParams(vmem_limit_bytes=16 * 1024 * 1024)
WHOLE = pltpu.CompilerParams(vmem_limit_bytes=62 * 1024 * 1024)


COST = pl.CostEstimate(flops=1000, bytes_accessed=1000, transcendentals=0)


def stage_kernel(
    devices, group, first, me_ref, dest_hbm, k_ref, v_ref, buf, buf_rest, table, k_vm, v_vm, dest, counts, sem, load_sem
):
    rows, heads = k_ref.shape[:2]
    small = pltpu.make_async_copy(dest_hbm, dest, sem.at[0])
    small.start()
    loads = []
    for row in range(rows):
        for which, (src, dst) in enumerate(((k_ref, k_vm), (v_ref, v_vm))):
            copy = pltpu.make_async_copy(src.at[row], dst.at[row], load_sem.at[which, row])
            copy.start()
            loads.append(copy)
    me = me_ref[0]

    def clear(i, carry):
        counts[i] = 0
        for k in range(group):
            table[i * group + k] = -1
        return carry

    lax.fori_loop(0, devices, clear, 0)
    small.wait()
    for row in range(rows):
        loads[2 * row].wait()
        loads[2 * row + 1].wait()

        def send(head, carry):
            offset = dest[row, head, 0]
            rank = counts[offset]
            counts[offset] = rank + 1
            table[offset * group + rank] = row * heads + head
            target = jnp.bitwise_and(me + offset, devices - 1)
            pltpu.make_async_copy(k_vm.at[row, head], buf.at[target * first + rank], sem.at[1]).start()

            @pl.when(rank < first - group)
            def _():
                at = target * first + group + rank
                pltpu.make_async_copy(v_vm.at[row, head], buf.at[at], sem.at[2]).start()

            @pl.when(rank >= first - group)
            def _():
                at = target * (2 * group - first) + rank + group - first
                pltpu.make_async_copy(v_vm.at[row, head], buf_rest.at[at], sem.at[2]).start()
            return carry

        lax.fori_loop(0, heads, send, 0)
    pltpu.make_async_copy(k_ref, k_vm, sem.at[1]).wait()
    pltpu.make_async_copy(v_ref, v_vm, sem.at[2]).wait()


def attend_kernel(
    levels,
    me_ref, table, len_hbm, kept_hbm, q_ref, k_ref, v_ref,
    stats_ref, *rest,
):
    chunks = rest[:levels // 2]
    len_ref, kept_ref, small_sem = rest[levels // 2:]
    rows, heads, tile, width = k_ref.shape
    steps, _, q_heads, _ = q_ref.shape
    per = q_heads // heads
    me = me_ref[0]

    small = [
        pltpu.make_async_copy(len_hbm, len_ref, small_sem.at[0]),
        pltpu.make_async_copy(kept_hbm, kept_ref, small_sem.at[1]),
    ]
    for copy in small:
        copy.start()
    for copy in small:
        copy.wait()

    lane = lax.broadcasted_iota(jnp.int32, (per, tile), 1)
    pair_lane = lax.broadcasted_iota(jnp.int32, (steps * per, LANES), 1)
    peaks = jnp.full((steps * per, LANES), absent_score, F32)
    totals = jnp.zeros((steps * per, LANES), F32)
    order = [jnp.bitwise_xor(place_of(me), level) for level in range(levels)]
    scale = width ** -0.5
    block = steps * per
    for row in range(rows):
        queries = [q_ref[step, row].astype(F32) for step in order]
        live = []
        for step in order:
            limit = jnp.where(kept_ref[row, step, me] > 0, len_ref[row] - me * tile, 0)
            live.append(lane < limit)
        live = jnp.concatenate(live * heads, axis=0)
        scores = []
        for head in range(heads):
            q = jnp.concatenate([x[head * per:(head + 1) * per] for x in queries], axis=0).astype(BF16)
            scores.append(lax.dot_general(
                q, k_ref[row, head], (((1,), (1,)), ((), ())), preferred_element_type=F32
            ))
        scores = jnp.concatenate(scores, axis=0) * scale
        peak = jnp.max(jnp.where(live, scores, absent_score), axis=1, keepdims=True)
        weights = jnp.where(live, jnp.exp(scores - peak), 0.0)
        total = jnp.sum(weights, axis=1, keepdims=True)
        rounded = weights.astype(BF16)
        for head in range(heads):
            out = jnp.dot(
                rounded[head * block:(head + 1) * block], v_ref[row, head], preferred_element_type=F32
            )
            pair = row * heads + head
            for i in range(levels):
                chunks[i // 2][i % 2, pair * per:(pair + 1) * per, :] = out[i * per:(i + 1) * per]
            here = pair_lane == pair
            peaks = jnp.where(here, peak[head * block:(head + 1) * block], peaks)
            totals = jnp.where(here, total[head * block:(head + 1) * block], totals)
    base = rows * q_heads
    for i in range(levels):
        chunks[i // 2][i % 2, base:base + per, :] = peaks[i * per:(i + 1) * per]
        chunks[i // 2][i % 2, base + per:base + 2 * per, :] = totals[i * per:(i + 1) * per]
    stats_ref[0] = peaks
    stats_ref[1] = totals


def place_of(me):
    return lax.rem(me, 2) * 2 + lax.rem(me // 2, 2)


def merge(swap, own, got, pairs, per, own_stats=None, got_stats=None):
    def both(rows, own=own, got=got):
        x, y = own[rows, :], got[rows, :]
        return jnp.where(swap, y, x), jnp.where(swap, x, y)

    scaled = own_stats is not None
    base = 0 if scaled else pairs * per
    stats = (own_stats, got_stats) if scaled else (own, got)
    peaks = both(slice(base, base + per), *stats)
    totals = both(slice(base + per, base + 2 * per), *stats)
    peak = jnp.maximum(*peaks)
    factors = [jnp.exp(x - peak) for x in peaks]
    total = factors[0] * totals[0] + factors[1] * totals[1]
    if scaled:
        scales = both(slice(2 * per, 3 * per), *stats)
        factors = [f * x for f, x in zip(factors, scales)]

    def summed(pair):
        first, second = [jnp.broadcast_to(f[:, pair:pair + 1], (per, LANES)) for f in factors]
        x, y = both(slice(pair * per, (pair + 1) * per))
        return first * x + second * y

    return peak, total, summed


def merge_kernel(bit, pairs, per, me_ref, own, got, *outs):
    swap = lax.rem(me_ref[0] // bit, 2) == 1
    base = pairs * per
    for i, out in enumerate(outs):
        x, y = (own, got) if len(outs) == 1 else (own.at[i], got.at[i])
        peak, total, summed = merge(swap, x, y, pairs, per)
        for pair in range(pairs):
            out[pair * per:(pair + 1) * per, :] = summed(pair)
        out[base:base + per, :] = peak
        out[base + per:base + 2 * per, :] = total


def scale_kernel(pairs, per, block, sums, stats):
    lane = lax.broadcasted_iota(jnp.int32, (per, LANES), 1)
    base = pairs * per
    scales = jnp.ones((per, LANES), F32)
    for pair in range(pairs):
        x = block[pair * per:(pair + 1) * per, :]
        largest = jnp.max(jnp.abs(x), axis=1, keepdims=True)
        largest = jnp.where(largest > 0.0, largest, 1.0)
        sums[pair * per:(pair + 1) * per, :] = x / largest
        scales = jnp.where(lane == pair, largest, scales)
    stats[:2 * per, :] = block[base:base + 2 * per, :]
    stats[2 * per:, :] = scales


def last_kernel(bit, pairs, per, me_ref, own, got, own_stats, got_stats, out):
    swap = lax.rem(me_ref[0] // bit, 2) == 1
    base = pairs * per
    peak, total, summed = merge(swap, own, got, pairs, per, own_stats, got_stats)
    lane = lax.broadcasted_iota(jnp.int32, peak.shape, 1)
    total = jnp.where(lane < pairs, total, 1.0)
    peak = jnp.where(lane < pairs, peak, 0.0)

    def result(pair):
        return summed(pair) / jnp.broadcast_to(total[:, pair:pair + 1], (per, LANES))

    for pair in range(0, pairs, 2):
        both = jnp.concatenate([result(pair), result(pair + 1)], axis=0)
        out[pair * per:(pair + 2) * per, :] = both.astype(BF16)
    rest = jnp.concatenate([peak, total], axis=0)
    lane = lax.broadcasted_iota(jnp.int32, rest.shape, 1)
    parts = []
    for i in range(3):
        parts.append(rest.astype(BF16).astype(F32))
        rest = rest - parts[i]
    half = LANES // 2
    packed = jnp.where(lane < half, parts[0], pltpu.roll(parts[1], half, 1))
    out[base:base + 2 * per, :] = packed.astype(BF16)
    out[base + 2 * per:base + 4 * per, :] = parts[2].astype(BF16)


def finish_kernel(pairs, per, heads, levels, me_ref, stats_ref, *refs):
    ins, (out, mass_ref, sem) = refs[:levels], refs[levels:]
    base = pairs * per
    copies = [
        pltpu.make_async_copy(
            ins[level].at[:base], out.at[jnp.bitwise_xor(place_of(me_ref[0]), level)], sem.at[level]
        )
        for level in range(levels)
    ]
    for copy in copies:
        copy.start()
    lane = lax.broadcasted_iota(jnp.int32, (2 * per, LANES), 1)
    mass = jnp.zeros((per, LANES), F32)
    for level in range(levels):
        packed = ins[level][base:base + 2 * per, :].astype(F32)
        third = ins[level][base + 2 * per:base + 4 * per, :].astype(F32)
        both = third + pltpu.roll(packed, LANES // 2, 1) + packed
        both = jnp.where(lane < pairs, both, 1.0)
        at = level * per
        coefficient = jnp.exp(jnp.minimum(stats_ref[0, at:at + per, :] - both[:per], 0.0)) / both[per:]
        mass = mass + stats_ref[1, at:at + per, :] * coefficient
    mass = jnp.sum(mass, axis=0, keepdims=True)
    for row in range(pairs // heads):
        mass_ref[row] = mass[:, row * heads:(row + 1) * heads]
    for copy in copies:
        copy.wait()


def place_keys_kernel(devices, group, first, me_ref, table, got, out, sem):
    heads = out.shape[1]
    me = me_ref[0]
    for offset in range(devices):
        source = jnp.bitwise_and(me + devices - offset, devices - 1)
        for k in range(group):
            put(got.at[source * first + k], table[offset * group + k], heads, out, sem)
    pltpu.make_async_copy(out, out, sem).wait()


def place_values_kernel(devices, group, first, me_ref, table, got, got_rest, out, sem):
    heads = out.shape[1]
    me = me_ref[0]
    rest = 2 * group - first
    for offset in range(devices):
        source = jnp.bitwise_and(me + devices - offset, devices - 1)
        for k in range(group):
            at = group + k
            src = got.at[source * first + at] if at < first else got_rest.at[source * rest + at - first]
            put(src, table[offset * group + k], heads, out, sem)
    pltpu.make_async_copy(out, out, sem).wait()


def put(src, pair, heads, out, sem):
    @pl.when(pair >= 0)
    def _():
        pltpu.make_async_copy(src, out.at[pair // heads, lax.rem(pair, heads)], sem).start()


def local(queries, key_cache, value_cache, row_lengths, kept_tiles, tile_dest):
    devices = lax.axis_size("ctx")
    rows, heads, span, width = key_cache.shape
    steps, _, q_heads, _ = queries.shape
    per = q_heads // heads
    pairs = rows * heads
    group = -(-pairs // devices)
    levels = 4
    assert steps == levels and tile_dest.shape[2] == devices and pairs % 2 == 0 and pairs <= LANES // 2
    assert devices > levels and devices & (devices - 1) == 0 and width == LANES

    me = lax.axis_index("ctx").astype(jnp.int32).reshape(1)
    kept = jnp.transpose(kept_tiles, (1, 0, 2))
    block_rows = rows * q_heads + 2 * per
    block_type = jax.ShapeDtypeStruct((block_rows, width), F32)
    message_type = jax.ShapeDtypeStruct((rows * q_heads + 4 * per, width), BF16)
    first = 2 * group - max(1, 2 * group // 3)

    def tiles_type(count):
        return jax.ShapeDtypeStruct((devices * count, span, width), BF16)

    def exchange(x):
        return lax.all_to_all(x, "ctx", split_axis=0, concat_axis=0, tiled=True)


    tiles_out, rest_out, table = pl.pallas_call(
        functools.partial(stage_kernel, devices, group, first),
        out_shape=[
            tiles_type(first), tiles_type(2 * group - first),
            jax.ShapeDtypeStruct((devices * group,), jnp.int32),
        ],
        in_specs=[SMEM, HBM, HBM, HBM],
        out_specs=[HBM, HBM, SMEM],
        scratch_shapes=[
            pltpu.VMEM(key_cache.shape, BF16),
            pltpu.VMEM(value_cache.shape, BF16),
            pltpu.SMEM(tile_dest.shape, jnp.int32),
            pltpu.SMEM((devices,), jnp.int32),
            pltpu.SemaphoreType.DMA((3,)),
            pltpu.SemaphoreType.DMA((2, rows)),
        ],
        compiler_params=WHOLE,
        cost_estimate=COST,
        name="stage",
    )(me, tile_dest, key_cache, value_cache)
    tiles_in = exchange(tiles_out)

    stats, *chunks = pl.pallas_call(
        functools.partial(attend_kernel, levels),
        out_shape=[
            jax.ShapeDtypeStruct((2, steps * per, LANES), F32),
        ] + [jax.ShapeDtypeStruct((2, block_rows, width), F32)] * 2,
        in_specs=[SMEM, SMEM, HBM, HBM, VMEM, VMEM, VMEM],
        out_specs=[VMEM] * 3,
        scratch_shapes=[
            pltpu.SMEM(row_lengths.shape, jnp.int32),
            pltpu.SMEM(kept.shape, jnp.int32),
            pltpu.SemaphoreType.DMA((2,)),
        ],
        compiler_params=PARAMS,
        cost_estimate=COST,
        name="attend",
    )(me, table, row_lengths, kept, queries, key_cache, value_cache)

    def flip(x, bit):
        return lax.ppermute(x, "ctx", [(i, i ^ bit) for i in range(devices)])

    def local_call(kernel, name, out_shape, *operands):
        return pl.pallas_call(
            kernel,
            out_shape=out_shape,
            in_specs=[SMEM if x is me or x.shape == (1,) else VMEM for x in operands],
            out_specs=[VMEM] * len(out_shape),
            compiler_params=PARAMS,
            cost_estimate=COST,
            name=name,
        )(*operands)

    def merged(name, bit, own, got, out_shape):
        return local_call(functools.partial(merge_kernel, bit, pairs, per), name, out_shape, me, own, got)

    block, sent = merged("core", 1, chunks[0], flip(chunks[1], 1), [block_type] * 2)
    block, = merged("near", 2, block, flip(sent, 2), [block_type])
    bit = levels
    while 2 * bit < devices:
        block, = merged("far", bit, block, flip(block, bit), [block_type])
        bit *= 2
    sums_type = jax.ShapeDtypeStruct((rows * q_heads, width), F32)
    stats_type = jax.ShapeDtypeStruct((3 * per, width), F32)
    sums, sum_stats = local_call(functools.partial(scale_kernel, pairs, per), "scale", [sums_type, stats_type], block)
    sums = lax.reduce_precision(sums, 5, 10)
    got = flip(sums.astype(jnp.float16), bit).astype(F32)
    got, rest_out = lax.optimization_barrier((got, rest_out))
    rest_in = exchange(rest_out)
    message, = local_call(
        functools.partial(last_kernel, bit, pairs, per), "last", [message_type],
        me, sums, got, sum_stats, flip(sum_stats, bit),
    )
    other = flip(message, 2)

    def place(kernel, name, *got):
        return pl.pallas_call(
            functools.partial(kernel, devices, group, first),
            out_shape=jax.ShapeDtypeStruct(key_cache.shape, BF16),
            in_specs=[SMEM, SMEM] + [ANY] * len(got),
            out_specs=HBM,
            scratch_shapes=[pltpu.SemaphoreType.DMA],
            compiler_params=PARAMS,
            cost_estimate=COST,
            name=name,
        )(me, table, *got)

    moved_keys = place(place_keys_kernel, "place_keys", tiles_in)
    moved_values = place(place_values_kernel, "place_values", tiles_in, rest_in)
    arrived = [message, other, flip(message, 1), flip(other, 1)]

    attn_out, mass = pl.pallas_call(
        functools.partial(finish_kernel, pairs, per, heads, levels),
        out_shape=[
            jax.ShapeDtypeStruct((steps, rows * q_heads, width), BF16),
            jax.ShapeDtypeStruct((rows, 1, heads), F32),
        ],
        in_specs=[SMEM, VMEM] + [VMEM] * levels,
        out_specs=[HBM, VMEM],
        scratch_shapes=[pltpu.SemaphoreType.DMA((levels,))],
        compiler_params=PARAMS,
        cost_estimate=COST,
        name="finish",
    )(me, stats, *arrived)
    return attn_out.reshape(queries.shape), jnp.transpose(mass, (0, 2, 1)), moved_keys, moved_values


def solution(mesh):
    in_specs = (
        P(None, "grp", None, None),
        P("grp", None, "ctx", None),
        P("grp", None, "ctx", None),
        P("grp"),
        P(None, "grp", None),
        P("grp", None, None),
    )
    out_specs = (
        P(None, "grp", None, None),
        P("grp", None, "ctx"),
        P("grp", None, "ctx", None),
        P("grp", None, "ctx", None),
    )
    return jax.shard_map(local, mesh=mesh, in_specs=in_specs, out_specs=out_specs, check_vma=False)
```

```python
import functools

import jax
import jax.numpy as jnp
from jax import lax
from jax.experimental import pallas as pl
from jax.experimental.pallas import tpu as pltpu
from jax.sharding import PartitionSpec as P

absent_score = -1e30
LANES = 128
F32 = jnp.float32
BF16 = jnp.bfloat16
VMEM = pl.BlockSpec(memory_space=pltpu.VMEM)
SMEM = pl.BlockSpec(memory_space=pltpu.SMEM)
HBM = pl.BlockSpec(memory_space=pltpu.HBM)
ANY = pl.BlockSpec(memory_space=pl.ANY)
PARAMS = pltpu.CompilerParams(vmem_limit_bytes=16 * 1024 * 1024)
WHOLE = pltpu.CompilerParams(vmem_limit_bytes=62 * 1024 * 1024)


COST = pl.CostEstimate(flops=1000, bytes_accessed=1000, transcendentals=0)


def stage_kernel(
    devices, group, first, me_ref, dest_hbm, k_ref, v_ref, buf, buf_rest, table, k_vm, v_vm, dest, counts, sem, load_sem
):
    rows, heads = k_ref.shape[:2]
    small = pltpu.make_async_copy(dest_hbm, dest, sem.at[0])
    small.start()
    loads = []
    for row in range(rows):
        for which, (src, dst) in enumerate(((k_ref, k_vm), (v_ref, v_vm))):
            copy = pltpu.make_async_copy(src.at[row], dst.at[row], load_sem.at[which, row])
            copy.start()
            loads.append(copy)
    me = me_ref[0]

    def clear(i, carry):
        counts[i] = 0
        for k in range(group):
            table[i * group + k] = -1
        return carry

    lax.fori_loop(0, devices, clear, 0)
    small.wait()
    for row in range(rows):
        loads[2 * row].wait()
        loads[2 * row + 1].wait()

        def send(head, carry):
            offset = dest[row, head, 0]
            rank = counts[offset]
            counts[offset] = rank + 1
            table[offset * group + rank] = row * heads + head
            target = jnp.bitwise_and(me + offset, devices - 1)
            pltpu.make_async_copy(k_vm.at[row, head], buf.at[target * first + rank], sem.at[1]).start()

            @pl.when(rank < first - group)
            def _():
                at = target * first + group + rank
                pltpu.make_async_copy(v_vm.at[row, head], buf.at[at], sem.at[2]).start()

            @pl.when(rank >= first - group)
            def _():
                at = target * (2 * group - first) + rank + group - first
                pltpu.make_async_copy(v_vm.at[row, head], buf_rest.at[at], sem.at[2]).start()
            return carry

        lax.fori_loop(0, heads, send, 0)
    pltpu.make_async_copy(k_ref, k_vm, sem.at[1]).wait()
    pltpu.make_async_copy(v_ref, v_vm, sem.at[2]).wait()


def attend_kernel(
    levels,
    me_ref, table, len_hbm, kept_hbm, q_ref, k_ref, v_ref,
    stats_ref, *rest,
):
    chunks = rest[:levels // 2]
    len_ref, kept_ref, small_sem = rest[levels // 2:]
    rows, heads, tile, width = k_ref.shape
    steps, _, q_heads, _ = q_ref.shape
    per = q_heads // heads
    me = me_ref[0]

    small = [
        pltpu.make_async_copy(len_hbm, len_ref, small_sem.at[0]),
        pltpu.make_async_copy(kept_hbm, kept_ref, small_sem.at[1]),
    ]
    for copy in small:
        copy.start()
    for copy in small:
        copy.wait()

    lane = lax.broadcasted_iota(jnp.int32, (per, tile), 1)
    pair_lane = lax.broadcasted_iota(jnp.int32, (steps * per, LANES), 1)
    peaks = jnp.full((steps * per, LANES), absent_score, F32)
    totals = jnp.zeros((steps * per, LANES), F32)
    order = [jnp.bitwise_xor(place_of(me), level) for level in range(levels)]
    scale = width ** -0.5
    block = steps * per
    for row in range(rows):
        queries = [q_ref[step, row].astype(F32) for step in order]
        live = []
        for step in order:
            limit = jnp.where(kept_ref[row, step, me] > 0, len_ref[row] - me * tile, 0)
            live.append(lane < limit)
        live = jnp.concatenate(live * heads, axis=0)
        scores = []
        for head in range(heads):
            q = jnp.concatenate([x[head * per:(head + 1) * per] for x in queries], axis=0).astype(BF16)
            scores.append(lax.dot_general(
                q, k_ref[row, head], (((1,), (1,)), ((), ())), preferred_element_type=F32
            ))
        scores = jnp.concatenate(scores, axis=0) * scale
        peak = jnp.max(jnp.where(live, scores, absent_score), axis=1, keepdims=True)
        weights = jnp.where(live, jnp.exp(scores - peak), 0.0)
        total = jnp.sum(weights, axis=1, keepdims=True)
        rounded = weights.astype(BF16)
        for head in range(heads):
            out = jnp.dot(
                rounded[head * block:(head + 1) * block], v_ref[row, head], preferred_element_type=F32
            )
            pair = row * heads + head
            for i in range(levels):
                chunks[i // 2][i % 2, pair * per:(pair + 1) * per, :] = out[i * per:(i + 1) * per]
            here = pair_lane == pair
            peaks = jnp.where(here, peak[head * block:(head + 1) * block], peaks)
            totals = jnp.where(here, total[head * block:(head + 1) * block], totals)
    base = rows * q_heads
    for i in range(levels):
        chunks[i // 2][i % 2, base:base + per, :] = peaks[i * per:(i + 1) * per]
        chunks[i // 2][i % 2, base + per:base + 2 * per, :] = totals[i * per:(i + 1) * per]
    stats_ref[0] = peaks
    stats_ref[1] = totals


def place_of(me):
    return lax.rem(me, 2) * 2 + lax.rem(me // 2, 2)


def merge(swap, own, got, pairs, per, own_stats=None, got_stats=None):
    def both(rows, own=own, got=got):
        x, y = own[rows, :], got[rows, :]
        return jnp.where(swap, y, x), jnp.where(swap, x, y)

    scaled = own_stats is not None
    base = 0 if scaled else pairs * per
    stats = (own_stats, got_stats) if scaled else (own, got)
    peaks = both(slice(base, base + per), *stats)
    totals = both(slice(base + per, base + 2 * per), *stats)
    peak = jnp.maximum(*peaks)
    factors = [jnp.exp(x - peak) for x in peaks]
    total = factors[0] * totals[0] + factors[1] * totals[1]
    if scaled:
        scales = both(slice(2 * per, 3 * per), *stats)
        factors = [f * x for f, x in zip(factors, scales)]

    def summed(pair):
        first, second = [jnp.broadcast_to(f[:, pair:pair + 1], (per, LANES)) for f in factors]
        x, y = both(slice(pair * per, (pair + 1) * per))
        return first * x + second * y

    return peak, total, summed


def merge_kernel(bit, pairs, per, me_ref, own, got, *outs):
    swap = lax.rem(me_ref[0] // bit, 2) == 1
    base = pairs * per
    for i, out in enumerate(outs):
        x, y = (own, got) if len(outs) == 1 else (own.at[i], got.at[i])
        peak, total, summed = merge(swap, x, y, pairs, per)
        for pair in range(pairs):
            out[pair * per:(pair + 1) * per, :] = summed(pair)
        out[base:base + per, :] = peak
        out[base + per:base + 2 * per, :] = total


def scale_kernel(pairs, per, block, sums, stats):
    lane = lax.broadcasted_iota(jnp.int32, (per, LANES), 1)
    base = pairs * per
    scales = jnp.ones((per, LANES), F32)
    for pair in range(pairs):
        x = block[pair * per:(pair + 1) * per, :]
        largest = jnp.max(jnp.abs(x), axis=1, keepdims=True)
        largest = jnp.where(largest > 0.0, largest, 1.0)
        sums[pair * per:(pair + 1) * per, :] = x / largest
        scales = jnp.where(lane == pair, largest, scales)
    stats[:2 * per, :] = block[base:base + 2 * per, :]
    stats[2 * per:, :] = scales


def last_kernel(bit, pairs, per, me_ref, own, got, own_stats, got_stats, out):
    swap = lax.rem(me_ref[0] // bit, 2) == 1
    base = pairs * per
    peak, total, summed = merge(swap, own, got, pairs, per, own_stats, got_stats)
    lane = lax.broadcasted_iota(jnp.int32, peak.shape, 1)
    total = jnp.where(lane < pairs, total, 1.0)
    peak = jnp.where(lane < pairs, peak, 0.0)

    def result(pair):
        return summed(pair) / jnp.broadcast_to(total[:, pair:pair + 1], (per, LANES))

    for pair in range(0, pairs, 2):
        both = jnp.concatenate([result(pair), result(pair + 1)], axis=0)
        out[pair * per:(pair + 2) * per, :] = both.astype(BF16)
    rest = jnp.concatenate([peak, total], axis=0)
    lane = lax.broadcasted_iota(jnp.int32, rest.shape, 1)
    parts = []
    for i in range(3):
        parts.append(rest.astype(BF16).astype(F32))
        rest = rest - parts[i]
    half = LANES // 2
    packed = jnp.where(lane < half, parts[0], pltpu.roll(parts[1], half, 1))
    out[base:base + 2 * per, :] = packed.astype(BF16)
    out[base + 2 * per:base + 4 * per, :] = parts[2].astype(BF16)


def finish_kernel(pairs, per, heads, levels, me_ref, stats_ref, *refs):
    ins, (out, mass_ref, sem) = refs[:levels], refs[levels:]
    base = pairs * per
    copies = [
        pltpu.make_async_copy(
            ins[level].at[:base], out.at[jnp.bitwise_xor(place_of(me_ref[0]), level)], sem.at[level]
        )
        for level in range(levels)
    ]
    for copy in copies:
        copy.start()
    lane = lax.broadcasted_iota(jnp.int32, (2 * per, LANES), 1)
    mass = jnp.zeros((per, LANES), F32)
    for level in range(levels):
        packed = ins[level][base:base + 2 * per, :].astype(F32)
        third = ins[level][base + 2 * per:base + 4 * per, :].astype(F32)
        both = third + pltpu.roll(packed, LANES // 2, 1) + packed
        both = jnp.where(lane < pairs, both, 1.0)
        at = level * per
        coefficient = jnp.exp(jnp.minimum(stats_ref[0, at:at + per, :] - both[:per], 0.0)) / both[per:]
        mass = mass + stats_ref[1, at:at + per, :] * coefficient
    mass = jnp.sum(mass, axis=0, keepdims=True)
    for row in range(pairs // heads):
        mass_ref[row] = mass[:, row * heads:(row + 1) * heads]
    for copy in copies:
        copy.wait()


def place_keys_kernel(devices, group, first, me_ref, table, got, out, sem):
    heads = out.shape[1]
    me = me_ref[0]
    for offset in range(devices):
        source = jnp.bitwise_and(me + devices - offset, devices - 1)
        for k in range(group):
            put(got.at[source * first + k], table[offset * group + k], heads, out, sem)
    pltpu.make_async_copy(out, out, sem).wait()


def place_values_kernel(devices, group, first, me_ref, table, got, got_rest, out, sem):
    heads = out.shape[1]
    me = me_ref[0]
    rest = 2 * group - first
    for offset in range(devices):
        source = jnp.bitwise_and(me + devices - offset, devices - 1)
        for k in range(group):
            at = group + k
            src = got.at[source * first + at] if at < first else got_rest.at[source * rest + at - first]
            put(src, table[offset * group + k], heads, out, sem)
    pltpu.make_async_copy(out, out, sem).wait()


def put(src, pair, heads, out, sem):
    @pl.when(pair >= 0)
    def _():
        pltpu.make_async_copy(src, out.at[pair // heads, lax.rem(pair, heads)], sem).start()


def local(queries, key_cache, value_cache, row_lengths, kept_tiles, tile_dest):
    devices = lax.axis_size("ctx")
    rows, heads, span, width = key_cache.shape
    steps, _, q_heads, _ = queries.shape
    per = q_heads // heads
    pairs = rows * heads
    group = -(-pairs // devices)
    levels = 4
    assert steps == levels and tile_dest.shape[2] == devices and pairs % 2 == 0 and pairs <= LANES // 2
    assert devices > levels and devices & (devices - 1) == 0 and width == LANES

    me = lax.axis_index("ctx").astype(jnp.int32).reshape(1)
    kept = jnp.transpose(kept_tiles, (1, 0, 2))
    block_rows = rows * q_heads + 2 * per
    block_type = jax.ShapeDtypeStruct((block_rows, width), F32)
    message_type = jax.ShapeDtypeStruct((rows * q_heads + 4 * per, width), BF16)
    first = 2 * group - max(1, 2 * group // 3)

    def tiles_type(count):
        return jax.ShapeDtypeStruct((devices * count, span, width), BF16)

    def exchange(x):
        return lax.all_to_all(x, "ctx", split_axis=0, concat_axis=0, tiled=True)


    tiles_out, rest_out, table = pl.pallas_call(
        functools.partial(stage_kernel, devices, group, first),
        out_shape=[
            tiles_type(first), tiles_type(2 * group - first),
            jax.ShapeDtypeStruct((devices * group,), jnp.int32),
        ],
        in_specs=[SMEM, HBM, HBM, HBM],
        out_specs=[HBM, HBM, SMEM],
        scratch_shapes=[
            pltpu.VMEM(key_cache.shape, BF16),
            pltpu.VMEM(value_cache.shape, BF16),
            pltpu.SMEM(tile_dest.shape, jnp.int32),
            pltpu.SMEM((devices,), jnp.int32),
            pltpu.SemaphoreType.DMA((3,)),
            pltpu.SemaphoreType.DMA((2, rows)),
        ],
        compiler_params=WHOLE,
        cost_estimate=COST,
        name="stage",
    )(me, tile_dest, key_cache, value_cache)
    tiles_in = exchange(tiles_out)

    stats, *chunks = pl.pallas_call(
        functools.partial(attend_kernel, levels),
        out_shape=[
            jax.ShapeDtypeStruct((2, steps * per, LANES), F32),
        ] + [jax.ShapeDtypeStruct((2, block_rows, width), F32)] * 2,
        in_specs=[SMEM, SMEM, HBM, HBM, VMEM, VMEM, VMEM],
        out_specs=[VMEM] * 3,
        scratch_shapes=[
            pltpu.SMEM(row_lengths.shape, jnp.int32),
            pltpu.SMEM(kept.shape, jnp.int32),
            pltpu.SemaphoreType.DMA((2,)),
        ],
        compiler_params=PARAMS,
        cost_estimate=COST,
        name="attend",
    )(me, table, row_lengths, kept, queries, key_cache, value_cache)

    def flip(x, bit):
        return lax.ppermute(x, "ctx", [(i, i ^ bit) for i in range(devices)])

    def local_call(kernel, name, out_shape, *operands):
        return pl.pallas_call(
            kernel,
            out_shape=out_shape,
            in_specs=[SMEM if x is me or x.shape == (1,) else VMEM for x in operands],
            out_specs=[VMEM] * len(out_shape),
            compiler_params=PARAMS,
            cost_estimate=COST,
            name=name,
        )(*operands)

    def merged(name, bit, own, got, out_shape):
        return local_call(functools.partial(merge_kernel, bit, pairs, per), name, out_shape, me, own, got)

    block, sent = merged("core", 1, chunks[0], flip(chunks[1], 1), [block_type] * 2)
    block, = merged("near", 2, block, flip(sent, 2), [block_type])
    bit = levels
    while 2 * bit < devices:
        block, = merged("far", bit, block, flip(block, bit), [block_type])
        bit *= 2
    sums_type = jax.ShapeDtypeStruct((rows * q_heads, width), F32)
    stats_type = jax.ShapeDtypeStruct((3 * per, width), F32)
    sums, sum_stats = local_call(functools.partial(scale_kernel, pairs, per), "scale", [sums_type, stats_type], block)
    sums = lax.reduce_precision(sums, 5, 10)
    got = flip(sums.astype(jnp.float16), bit).astype(F32)
    got, got_stats, rest_out = lax.optimization_barrier((got, flip(sum_stats, bit), rest_out))
    rest_in = exchange(rest_out)
    message, = local_call(
        functools.partial(last_kernel, bit, pairs, per), "last", [message_type],
        me, sums, got, sum_stats, got_stats,
    )
    other = flip(message, 2)

    def place(kernel, name, *got):
        return pl.pallas_call(
            functools.partial(kernel, devices, group, first),
            out_shape=jax.ShapeDtypeStruct(key_cache.shape, BF16),
            in_specs=[SMEM, SMEM] + [ANY] * len(got),
            out_specs=HBM,
            scratch_shapes=[pltpu.SemaphoreType.DMA],
            compiler_params=PARAMS,
            cost_estimate=COST,
            name=name,
        )(me, table, *got)

    moved_keys = place(place_keys_kernel, "place_keys", tiles_in)
    moved_values = place(place_values_kernel, "place_values", tiles_in, rest_in)
    arrived = [message, other, flip(message, 1), flip(other, 1)]

    attn_out, mass = pl.pallas_call(
        functools.partial(finish_kernel, pairs, per, heads, levels),
        out_shape=[
            jax.ShapeDtypeStruct((steps, rows * q_heads, width), BF16),
            jax.ShapeDtypeStruct((rows, 1, heads), F32),
        ],
        in_specs=[SMEM, VMEM] + [VMEM] * levels,
        out_specs=[HBM, VMEM],
        scratch_shapes=[pltpu.SemaphoreType.DMA((levels,))],
        compiler_params=PARAMS,
        cost_estimate=COST,
        name="finish",
    )(me, stats, *arrived)
    return attn_out.reshape(queries.shape), jnp.transpose(mass, (0, 2, 1)), moved_keys, moved_values


def solution(mesh):
    in_specs = (
        P(None, "grp", None, None),
        P("grp", None, "ctx", None),
        P("grp", None, "ctx", None),
        P("grp"),
        P(None, "grp", None),
        P("grp", None, None),
    )
    out_specs = (
        P(None, "grp", None, None),
        P("grp", None, "ctx"),
        P("grp", None, "ctx", None),
        P("grp", None, "ctx", None),
    )
    return jax.shard_map(local, mesh=mesh, in_specs=in_specs, out_specs=out_specs, check_vma=False)
```

```python
import functools

import jax
import jax.numpy as jnp
from jax import lax
from jax.experimental import pallas as pl
from jax.experimental.pallas import tpu as pltpu
from jax.sharding import PartitionSpec as P

absent_score = -1e30
LANES = 128
F32 = jnp.float32
BF16 = jnp.bfloat16
VMEM = pl.BlockSpec(memory_space=pltpu.VMEM)
SMEM = pl.BlockSpec(memory_space=pltpu.SMEM)
HBM = pl.BlockSpec(memory_space=pltpu.HBM)
ANY = pl.BlockSpec(memory_space=pl.ANY)
PARAMS = pltpu.CompilerParams(vmem_limit_bytes=16 * 1024 * 1024)
WHOLE = pltpu.CompilerParams(vmem_limit_bytes=62 * 1024 * 1024)


COST = pl.CostEstimate(flops=1000, bytes_accessed=1000, transcendentals=0)


def stage_kernel(
    devices, group, first, me_ref, dest_hbm, k_ref, v_ref, buf, buf_rest, table, k_vm, v_vm, dest, counts, sem, load_sem
):
    rows, heads = k_ref.shape[:2]
    small = pltpu.make_async_copy(dest_hbm, dest, sem.at[0])
    small.start()
    loads = []
    for row in range(rows):
        for which, (src, dst) in enumerate(((k_ref, k_vm), (v_ref, v_vm))):
            copy = pltpu.make_async_copy(src.at[row], dst.at[row], load_sem.at[which, row])
            copy.start()
            loads.append(copy)
    me = me_ref[0]

    def clear(i, carry):
        counts[i] = 0
        for k in range(group):
            table[i * group + k] = -1
        return carry

    lax.fori_loop(0, devices, clear, 0)
    small.wait()
    for row in range(rows):
        loads[2 * row].wait()
        loads[2 * row + 1].wait()

        def send(head, carry):
            offset = dest[row, head, 0]
            rank = counts[offset]
            counts[offset] = rank + 1
            table[offset * group + rank] = row * heads + head
            target = turn_of(jnp.bitwise_and(me + offset, devices - 1), devices)
            pltpu.make_async_copy(k_vm.at[row, head], buf.at[target * first + rank], sem.at[1]).start()

            @pl.when(rank < first - group)
            def _():
                at = target * first + group + rank
                pltpu.make_async_copy(v_vm.at[row, head], buf.at[at], sem.at[2]).start()

            @pl.when(rank >= first - group)
            def _():
                at = target * (2 * group - first) + rank + group - first
                pltpu.make_async_copy(v_vm.at[row, head], buf_rest.at[at], sem.at[2]).start()
            return carry

        lax.fori_loop(0, heads, send, 0)
    pltpu.make_async_copy(k_ref, k_vm, sem.at[1]).wait()
    pltpu.make_async_copy(v_ref, v_vm, sem.at[2]).wait()


def attend_kernel(
    levels,
    me_ref, table, len_hbm, kept_hbm, q_ref, k_ref, v_ref,
    stats_ref, *rest,
):
    chunks = rest[:levels // 2]
    len_ref, kept_ref, small_sem = rest[levels // 2:]
    rows, heads, tile, width = k_ref.shape
    steps, _, q_heads, _ = q_ref.shape
    per = q_heads // heads
    me = me_ref[0]

    small = [
        pltpu.make_async_copy(len_hbm, len_ref, small_sem.at[0]),
        pltpu.make_async_copy(kept_hbm, kept_ref, small_sem.at[1]),
    ]
    for copy in small:
        copy.start()
    for copy in small:
        copy.wait()

    lane = lax.broadcasted_iota(jnp.int32, (per, tile), 1)
    pair_lane = lax.broadcasted_iota(jnp.int32, (steps * per, LANES), 1)
    peaks = jnp.full((steps * per, LANES), absent_score, F32)
    totals = jnp.zeros((steps * per, LANES), F32)
    order = [jnp.bitwise_xor(place_of(me), level) for level in range(levels)]
    scale = width ** -0.5
    block = steps * per
    for row in range(rows):
        queries = [q_ref[step, row].astype(F32) for step in order]
        live = []
        for step in order:
            limit = jnp.where(kept_ref[row, step, me] > 0, len_ref[row] - me * tile, 0)
            live.append(lane < limit)
        live = jnp.concatenate(live * heads, axis=0)
        scores = []
        for head in range(heads):
            q = jnp.concatenate([x[head * per:(head + 1) * per] for x in queries], axis=0).astype(BF16)
            scores.append(lax.dot_general(
                q, k_ref[row, head], (((1,), (1,)), ((), ())), preferred_element_type=F32
            ))
        scores = jnp.concatenate(scores, axis=0) * scale
        peak = jnp.max(jnp.where(live, scores, absent_score), axis=1, keepdims=True)
        weights = jnp.where(live, jnp.exp(scores - peak), 0.0)
        total = jnp.sum(weights, axis=1, keepdims=True)
        rounded = weights.astype(BF16)
        for head in range(heads):
            out = jnp.dot(
                rounded[head * block:(head + 1) * block], v_ref[row, head], preferred_element_type=F32
            )
            pair = row * heads + head
            for i in range(levels):
                chunks[i // 2][i % 2, pair * per:(pair + 1) * per, :] = out[i * per:(i + 1) * per]
            here = pair_lane == pair
            peaks = jnp.where(here, peak[head * block:(head + 1) * block], peaks)
            totals = jnp.where(here, total[head * block:(head + 1) * block], totals)
    base = rows * q_heads
    for i in range(levels):
        chunks[i // 2][i % 2, base:base + per, :] = peaks[i * per:(i + 1) * per]
        chunks[i // 2][i % 2, base + per:base + 2 * per, :] = totals[i * per:(i + 1) * per]
    stats_ref[0] = peaks
    stats_ref[1] = totals


def place_of(me):
    return lax.rem(me, 2) * 2 + lax.rem(me // 2, 2)


def merge(swap, own, got, pairs, per, own_stats=None, got_stats=None):
    def both(rows, own=own, got=got):
        x, y = own[rows, :], got[rows, :]
        return jnp.where(swap, y, x), jnp.where(swap, x, y)

    scaled = own_stats is not None
    base = 0 if scaled else pairs * per
    stats = (own_stats, got_stats) if scaled else (own, got)
    peaks = both(slice(base, base + per), *stats)
    totals = both(slice(base + per, base + 2 * per), *stats)
    peak = jnp.maximum(*peaks)
    factors = [jnp.exp(x - peak) for x in peaks]
    total = factors[0] * totals[0] + factors[1] * totals[1]
    if scaled:
        scales = both(slice(2 * per, 3 * per), *stats)
        factors = [f * x for f, x in zip(factors, scales)]

    def summed(pair):
        first, second = [jnp.broadcast_to(f[:, pair:pair + 1], (per, LANES)) for f in factors]
        x, y = both(slice(pair * per, (pair + 1) * per))
        return first * x + second * y

    return peak, total, summed


def merge_kernel(bit, pairs, per, me_ref, own, got, *outs):
    swap = lax.rem(me_ref[0] // bit, 2) == 1
    base = pairs * per
    for i, out in enumerate(outs):
        x, y = (own, got) if len(outs) == 1 else (own.at[i], got.at[i])
        peak, total, summed = merge(swap, x, y, pairs, per)
        for pair in range(pairs):
            out[pair * per:(pair + 1) * per, :] = summed(pair)
        out[base:base + per, :] = peak
        out[base + per:base + 2 * per, :] = total


def scale_kernel(pairs, per, block, sums, stats):
    lane = lax.broadcasted_iota(jnp.int32, (per, LANES), 1)
    base = pairs * per
    scales = jnp.ones((per, LANES), F32)
    for pair in range(pairs):
        x = block[pair * per:(pair + 1) * per, :]
        largest = jnp.max(jnp.abs(x), axis=1, keepdims=True)
        largest = jnp.where(largest > 0.0, largest, 1.0)
        sums[pair * per:(pair + 1) * per, :] = x / largest
        scales = jnp.where(lane == pair, largest, scales)
    stats[:2 * per, :] = block[base:base + 2 * per, :]
    stats[2 * per:, :] = scales


def last_kernel(bit, pairs, per, me_ref, own, got, own_stats, got_stats, out):
    swap = lax.rem(me_ref[0] // bit, 2) == 1
    base = pairs * per
    peak, total, summed = merge(swap, own, got, pairs, per, own_stats, got_stats)
    lane = lax.broadcasted_iota(jnp.int32, peak.shape, 1)
    total = jnp.where(lane < pairs, total, 1.0)
    peak = jnp.where(lane < pairs, peak, 0.0)

    def result(pair):
        return summed(pair) / jnp.broadcast_to(total[:, pair:pair + 1], (per, LANES))

    for pair in range(0, pairs, 2):
        both = jnp.concatenate([result(pair), result(pair + 1)], axis=0)
        out[pair * per:(pair + 2) * per, :] = both.astype(BF16)
    rest = jnp.concatenate([peak, total], axis=0)
    lane = lax.broadcasted_iota(jnp.int32, rest.shape, 1)
    parts = []
    for i in range(3):
        parts.append(rest.astype(BF16).astype(F32))
        rest = rest - parts[i]
    half = LANES // 2
    packed = jnp.where(lane < half, parts[0], pltpu.roll(parts[1], half, 1))
    out[base:base + 2 * per, :] = packed.astype(BF16)
    out[base + 2 * per:base + 4 * per, :] = parts[2].astype(BF16)


def finish_kernel(pairs, per, heads, levels, me_ref, stats_ref, *refs):
    ins, (out, mass_ref, sem) = refs[:levels], refs[levels:]
    base = pairs * per
    copies = [
        pltpu.make_async_copy(
            ins[level].at[:base], out.at[jnp.bitwise_xor(place_of(me_ref[0]), level)], sem.at[level]
        )
        for level in range(levels)
    ]
    for copy in copies:
        copy.start()
    lane = lax.broadcasted_iota(jnp.int32, (2 * per, LANES), 1)
    mass = jnp.zeros((per, LANES), F32)
    for level in range(levels):
        packed = ins[level][base:base + 2 * per, :].astype(F32)
        third = ins[level][base + 2 * per:base + 4 * per, :].astype(F32)
        both = third + pltpu.roll(packed, LANES // 2, 1) + packed
        both = jnp.where(lane < pairs, both, 1.0)
        at = level * per
        coefficient = jnp.exp(jnp.minimum(stats_ref[0, at:at + per, :] - both[:per], 0.0)) / both[per:]
        mass = mass + stats_ref[1, at:at + per, :] * coefficient
    mass = jnp.sum(mass, axis=0, keepdims=True)
    for row in range(pairs // heads):
        mass_ref[row] = mass[:, row * heads:(row + 1) * heads]
    for copy in copies:
        copy.wait()


def place_keys_kernel(devices, group, first, me_ref, table, got, out, sem):
    heads = out.shape[1]
    me = me_ref[0]
    for offset in range(devices):
        source = turn_of(jnp.bitwise_and(me + devices - offset, devices - 1), devices)
        for k in range(group):
            put(got.at[source * first + k], table[offset * group + k], heads, out, sem)
    pltpu.make_async_copy(out, out, sem).wait()


def place_values_kernel(devices, group, first, me_ref, table, got, got_rest, out, sem):
    heads = out.shape[1]
    me = me_ref[0]
    rest = 2 * group - first
    for offset in range(devices):
        source = turn_of(jnp.bitwise_and(me + devices - offset, devices - 1), devices)
        for k in range(group):
            at = group + k
            src = got.at[source * first + at] if at < first else got_rest.at[source * rest + at - first]
            put(src, table[offset * group + k], heads, out, sem)
    pltpu.make_async_copy(out, out, sem).wait()


def turn_of(index, devices):
    return lax.rem(index, devices // 2) * 2 + index // (devices // 2)


def put(src, pair, heads, out, sem):
    @pl.when(pair >= 0)
    def _():
        pltpu.make_async_copy(src, out.at[pair // heads, lax.rem(pair, heads)], sem).start()


def local(queries, key_cache, value_cache, row_lengths, kept_tiles, tile_dest):
    devices = lax.axis_size("ctx")
    rows, heads, span, width = key_cache.shape
    steps, _, q_heads, _ = queries.shape
    per = q_heads // heads
    pairs = rows * heads
    group = -(-pairs // devices)
    levels = 4
    assert steps == levels and tile_dest.shape[2] == devices and pairs % 2 == 0 and pairs <= LANES // 2
    assert devices > levels and devices & (devices - 1) == 0 and width == LANES

    me = lax.axis_index("ctx").astype(jnp.int32).reshape(1)
    kept = jnp.transpose(kept_tiles, (1, 0, 2))
    block_rows = rows * q_heads + 2 * per
    block_type = jax.ShapeDtypeStruct((block_rows, width), F32)
    message_type = jax.ShapeDtypeStruct((rows * q_heads + 4 * per, width), BF16)
    first = 2 * group - max(1, 2 * group // 3)

    def tiles_type(count):
        return jax.ShapeDtypeStruct((devices * count, span, width), BF16)

    order = [turn // 2 + turn % 2 * (devices // 2) for turn in range(devices)]

    def exchange(x):
        return lax.all_to_all(x, "ctx", split_axis=0, concat_axis=0, axis_index_groups=[order], tiled=True)


    tiles_out, rest_out, table = pl.pallas_call(
        functools.partial(stage_kernel, devices, group, first),
        out_shape=[
            tiles_type(first), tiles_type(2 * group - first),
            jax.ShapeDtypeStruct((devices * group,), jnp.int32),
        ],
        in_specs=[SMEM, HBM, HBM, HBM],
        out_specs=[HBM, HBM, SMEM],
        scratch_shapes=[
            pltpu.VMEM(key_cache.shape, BF16),
            pltpu.VMEM(value_cache.shape, BF16),
            pltpu.SMEM(tile_dest.shape, jnp.int32),
            pltpu.SMEM((devices,), jnp.int32),
            pltpu.SemaphoreType.DMA((3,)),
            pltpu.SemaphoreType.DMA((2, rows)),
        ],
        compiler_params=WHOLE,
        cost_estimate=COST,
        name="stage",
    )(me, tile_dest, key_cache, value_cache)
    tiles_in = exchange(tiles_out)

    stats, *chunks = pl.pallas_call(
        functools.partial(attend_kernel, levels),
        out_shape=[
            jax.ShapeDtypeStruct((2, steps * per, LANES), F32),
        ] + [jax.ShapeDtypeStruct((2, block_rows, width), F32)] * 2,
        in_specs=[SMEM, SMEM, HBM, HBM, VMEM, VMEM, VMEM],
        out_specs=[VMEM] * 3,
        scratch_shapes=[
            pltpu.SMEM(row_lengths.shape, jnp.int32),
            pltpu.SMEM(kept.shape, jnp.int32),
            pltpu.SemaphoreType.DMA((2,)),
        ],
        compiler_params=PARAMS,
        cost_estimate=COST,
        name="attend",
    )(me, table, row_lengths, kept, queries, key_cache, value_cache)

    def flip(x, bit):
        return lax.ppermute(x, "ctx", [(i, i ^ bit) for i in range(devices)])

    def local_call(kernel, name, out_shape, *operands):
        return pl.pallas_call(
            kernel,
            out_shape=out_shape,
            in_specs=[SMEM if x is me or x.shape == (1,) else VMEM for x in operands],
            out_specs=[VMEM] * len(out_shape),
            compiler_params=PARAMS,
            cost_estimate=COST,
            name=name,
        )(*operands)

    def merged(name, bit, own, got, out_shape):
        return local_call(functools.partial(merge_kernel, bit, pairs, per), name, out_shape, me, own, got)

    block, sent = merged("core", 1, chunks[0], flip(chunks[1], 1), [block_type] * 2)
    block, = merged("near", 2, block, flip(sent, 2), [block_type])
    bit = levels
    while 2 * bit < devices:
        block, = merged("far", bit, block, flip(block, bit), [block_type])
        bit *= 2
    sums_type = jax.ShapeDtypeStruct((rows * q_heads, width), F32)
    stats_type = jax.ShapeDtypeStruct((3 * per, width), F32)
    sums, sum_stats = local_call(functools.partial(scale_kernel, pairs, per), "scale", [sums_type, stats_type], block)
    sums = lax.reduce_precision(sums, 5, 10)
    got = flip(sums.astype(jnp.float16), bit).astype(F32)
    got, got_stats, rest_out = lax.optimization_barrier((got, flip(sum_stats, bit), rest_out))
    rest_in = exchange(rest_out)
    message, = local_call(
        functools.partial(last_kernel, bit, pairs, per), "last", [message_type],
        me, sums, got, sum_stats, got_stats,
    )
    other = flip(message, 2)

    def place(kernel, name, *got):
        return pl.pallas_call(
            functools.partial(kernel, devices, group, first),
            out_shape=jax.ShapeDtypeStruct(key_cache.shape, BF16),
            in_specs=[SMEM, SMEM] + [ANY] * len(got),
            out_specs=HBM,
            scratch_shapes=[pltpu.SemaphoreType.DMA],
            compiler_params=PARAMS,
            cost_estimate=COST,
            name=name,
        )(me, table, *got)

    moved_keys = place(place_keys_kernel, "place_keys", tiles_in)
    moved_values = place(place_values_kernel, "place_values", tiles_in, rest_in)
    arrived = [message, other, flip(message, 1), flip(other, 1)]

    attn_out, mass = pl.pallas_call(
        functools.partial(finish_kernel, pairs, per, heads, levels),
        out_shape=[
            jax.ShapeDtypeStruct((steps, rows * q_heads, width), BF16),
            jax.ShapeDtypeStruct((rows, 1, heads), F32),
        ],
        in_specs=[SMEM, VMEM] + [VMEM] * levels,
        out_specs=[HBM, VMEM],
        scratch_shapes=[pltpu.SemaphoreType.DMA((levels,))],
        compiler_params=PARAMS,
        cost_estimate=COST,
        name="finish",
    )(me, stats, *arrived)
    return attn_out.reshape(queries.shape), jnp.transpose(mass, (0, 2, 1)), moved_keys, moved_values


def solution(mesh):
    in_specs = (
        P(None, "grp", None, None),
        P("grp", None, "ctx", None),
        P("grp", None, "ctx", None),
        P("grp"),
        P(None, "grp", None),
        P("grp", None, None),
    )
    out_specs = (
        P(None, "grp", None, None),
        P("grp", None, "ctx"),
        P("grp", None, "ctx", None),
        P("grp", None, "ctx", None),
    )
    return jax.shard_map(local, mesh=mesh, in_specs=in_specs, out_specs=out_specs, check_vma=False)
```

```python
import functools

import jax
import jax.numpy as jnp
from jax import lax
from jax.experimental import pallas as pl
from jax.experimental.pallas import tpu as pltpu
from jax.sharding import PartitionSpec as P

absent_score = -1e30
LANES = 128
F32 = jnp.float32
BF16 = jnp.bfloat16
VMEM = pl.BlockSpec(memory_space=pltpu.VMEM)
SMEM = pl.BlockSpec(memory_space=pltpu.SMEM)
HBM = pl.BlockSpec(memory_space=pltpu.HBM)
ANY = pl.BlockSpec(memory_space=pl.ANY)
PARAMS = pltpu.CompilerParams(vmem_limit_bytes=16 * 1024 * 1024)
WHOLE = pltpu.CompilerParams(vmem_limit_bytes=62 * 1024 * 1024)


COST = pl.CostEstimate(flops=1000, bytes_accessed=1000, transcendentals=0)


def stage_kernel(devices, group, dest_hbm, k_ref, v_ref, buf, table, k_vm, v_vm, dest, counts, sem, load_sem):
    rows, heads = k_ref.shape[:2]
    small = pltpu.make_async_copy(dest_hbm, dest, sem.at[0])
    small.start()
    loads = []
    for row in range(rows):
        for which, (src, dst) in enumerate(((k_ref, k_vm), (v_ref, v_vm))):
            copy = pltpu.make_async_copy(src.at[row], dst.at[row], load_sem.at[which, row])
            copy.start()
            loads.append(copy)
    me = lax.axis_index("ctx")

    def clear(i, carry):
        counts[i] = 0
        for k in range(group):
            table[i * group + k] = -1
        return carry

    lax.fori_loop(0, devices, clear, 0)
    small.wait()
    for row in range(rows):
        loads[2 * row].wait()
        loads[2 * row + 1].wait()

        def send(head, carry):
            offset = dest[row, head, 0]
            rank = counts[offset]
            counts[offset] = rank + 1
            table[offset * group + rank] = row * heads + head
            slot = jnp.bitwise_and(me + offset, devices - 1) * group + rank
            pltpu.make_async_copy(k_vm.at[row, head], buf.at[slot, 0], sem.at[1]).start()
            pltpu.make_async_copy(v_vm.at[row, head], buf.at[slot, 1], sem.at[2]).start()
            return carry

        lax.fori_loop(0, heads, send, 0)
    pltpu.make_async_copy(k_ref, k_vm, sem.at[1]).wait()
    pltpu.make_async_copy(v_ref, v_vm, sem.at[2]).wait()


def attend_kernel(
    levels,
    table, len_hbm, kept_hbm, q_ref, k_ref, v_ref,
    stats_ref, *rest,
):
    chunks = rest[:levels // 2]
    len_ref, kept_ref, small_sem = rest[levels // 2:]
    rows, heads, tile, width = k_ref.shape
    steps, _, q_heads, _ = q_ref.shape
    per = q_heads // heads
    me = lax.axis_index("ctx")

    small = [
        pltpu.make_async_copy(len_hbm, len_ref, small_sem.at[0]),
        pltpu.make_async_copy(kept_hbm, kept_ref, small_sem.at[1]),
    ]
    for copy in small:
        copy.start()
    for copy in small:
        copy.wait()

    lane = lax.broadcasted_iota(jnp.int32, (per, tile), 1)
    pair_lane = lax.broadcasted_iota(jnp.int32, (steps * per, LANES), 1)
    peaks = jnp.full((steps * per, LANES), absent_score, F32)
    totals = jnp.zeros((steps * per, LANES), F32)
    order = [jnp.bitwise_xor(place_of(me), level) for level in range(levels)]
    scale = width ** -0.5
    block = steps * per
    for row in range(rows):
        queries = [q_ref[step, row].astype(F32) for step in order]
        live = []
        for step in order:
            limit = jnp.where(kept_ref[row, step, me] > 0, len_ref[row] - me * tile, 0)
            live.append(lane < limit)
        live = jnp.concatenate(live * heads, axis=0)
        scores = []
        for head in range(heads):
            q = jnp.concatenate([x[head * per:(head + 1) * per] for x in queries], axis=0).astype(BF16)
            scores.append(lax.dot_general(
                q, k_ref[row, head], (((1,), (1,)), ((), ())), preferred_element_type=F32
            ))
        scores = jnp.concatenate(scores, axis=0) * scale
        peak = jnp.max(jnp.where(live, scores, absent_score), axis=1, keepdims=True)
        weights = jnp.where(live, jnp.exp(scores - peak), 0.0)
        total = jnp.sum(weights, axis=1, keepdims=True)
        rounded = weights.astype(BF16)
        for head in range(heads):
            out = jnp.dot(
                rounded[head * block:(head + 1) * block], v_ref[row, head], preferred_element_type=F32
            )
            pair = row * heads + head
            for i in range(levels):
                chunks[i // 2][i % 2, pair * per:(pair + 1) * per, :] = out[i * per:(i + 1) * per]
            here = pair_lane == pair
            peaks = jnp.where(here, peak[head * block:(head + 1) * block], peaks)
            totals = jnp.where(here, total[head * block:(head + 1) * block], totals)
    base = rows * q_heads
    for i in range(levels):
        chunks[i // 2][i % 2, base:base + per, :] = peaks[i * per:(i + 1) * per]
        chunks[i // 2][i % 2, base + per:base + 2 * per, :] = totals[i * per:(i + 1) * per]
    stats_ref[0] = peaks
    stats_ref[1] = totals


def place_of(me):
    return lax.rem(me, 2) * 2 + lax.rem(me // 2, 2)


def merge(swap, own, got, pairs, per, own_stats=None, got_stats=None):
    def both(rows, own=own, got=got):
        x, y = own[rows, :], got[rows, :]
        return jnp.where(swap, y, x), jnp.where(swap, x, y)

    scaled = own_stats is not None
    base = 0 if scaled else pairs * per
    stats = (own_stats, got_stats) if scaled else (own, got)
    peaks = both(slice(base, base + per), *stats)
    totals = both(slice(base + per, base + 2 * per), *stats)
    peak = jnp.maximum(*peaks)
    factors = [jnp.exp(x - peak) for x in peaks]
    total = factors[0] * totals[0] + factors[1] * totals[1]
    if scaled:
        scales = both(slice(2 * per, 3 * per), *stats)
        factors = [f * x for f, x in zip(factors, scales)]

    def summed(pair):
        first, second = [jnp.broadcast_to(f[:, pair:pair + 1], (per, LANES)) for f in factors]
        x, y = both(slice(pair * per, (pair + 1) * per))
        return first * x + second * y

    return peak, total, summed


def merge_kernel(bit, pairs, per, own, got, *outs):
    swap = lax.rem(lax.axis_index("ctx") // bit, 2) == 1
    base = pairs * per
    for i, out in enumerate(outs):
        x, y = (own, got) if len(outs) == 1 else (own.at[i], got.at[i])
        peak, total, summed = merge(swap, x, y, pairs, per)
        for pair in range(pairs):
            out[pair * per:(pair + 1) * per, :] = summed(pair)
        out[base:base + per, :] = peak
        out[base + per:base + 2 * per, :] = total


def scale_kernel(pairs, per, block, sums, stats):
    lane = lax.broadcasted_iota(jnp.int32, (per, LANES), 1)
    base = pairs * per
    scales = jnp.ones((per, LANES), F32)
    for pair in range(pairs):
        x = block[pair * per:(pair + 1) * per, :]
        largest = jnp.max(jnp.abs(x), axis=1, keepdims=True)
        largest = jnp.where(largest > 0.0, largest, 1.0)
        sums[pair * per:(pair + 1) * per, :] = x / largest
        scales = jnp.where(lane == pair, largest, scales)
    stats[:2 * per, :] = block[base:base + 2 * per, :]
    stats[2 * per:, :] = scales


def last_kernel(bit, pairs, per, own, got, own_stats, got_stats, out):
    swap = lax.rem(lax.axis_index("ctx") // bit, 2) == 1
    base = pairs * per
    peak, total, summed = merge(swap, own, got, pairs, per, own_stats, got_stats)
    lane = lax.broadcasted_iota(jnp.int32, peak.shape, 1)
    total = jnp.where(lane < pairs, total, 1.0)
    peak = jnp.where(lane < pairs, peak, 0.0)

    def result(pair):
        return summed(pair) / jnp.broadcast_to(total[:, pair:pair + 1], (per, LANES))

    for pair in range(0, pairs, 2):
        both = jnp.concatenate([result(pair), result(pair + 1)], axis=0)
        out[pair * per:(pair + 2) * per, :] = both.astype(BF16)
    rest = jnp.concatenate([peak, total], axis=0)
    lane = lax.broadcasted_iota(jnp.int32, rest.shape, 1)
    parts = []
    for i in range(3):
        parts.append(rest.astype(BF16).astype(F32))
        rest = rest - parts[i]
    half = LANES // 2
    packed = jnp.where(lane < half, parts[0], pltpu.roll(parts[1], half, 1))
    out[base:base + 2 * per, :] = packed.astype(BF16)
    out[base + 2 * per:base + 4 * per, :] = parts[2].astype(BF16)


def finish_kernel(pairs, per, heads, levels, stats_ref, *refs):
    me = lax.axis_index("ctx")
    ins, (out, mass_ref, mass_vm, sem) = refs[:levels], refs[levels:]
    base = pairs * per
    copies = [
        pltpu.make_async_copy(
            ins[level].at[:base], out.at[jnp.bitwise_xor(place_of(me), level)], sem.at[level]
        )
        for level in range(levels)
    ]
    for copy in copies:
        copy.start()
    lane = lax.broadcasted_iota(jnp.int32, (2 * per, LANES), 1)
    mass = jnp.zeros((per, LANES), F32)
    for level in range(levels):
        packed = ins[level][base:base + 2 * per, :].astype(F32)
        third = ins[level][base + 2 * per:base + 4 * per, :].astype(F32)
        both = third + pltpu.roll(packed, LANES // 2, 1) + packed
        both = jnp.where(lane < pairs, both, 1.0)
        at = level * per
        coefficient = jnp.exp(jnp.minimum(stats_ref[0, at:at + per, :] - both[:per], 0.0)) / both[per:]
        mass = mass + stats_ref[1, at:at + per, :] * coefficient
    mass = jnp.sum(mass, axis=0, keepdims=True)
    for row in range(pairs // heads):
        mass_vm[row] = mass[:, row * heads:(row + 1) * heads]
    copies.append(pltpu.make_async_copy(mass_vm, mass_ref, sem.at[levels]))
    copies[-1].start()
    for copy in copies:
        copy.wait()


def place_kernel(devices, group, table, got_ref, k_ref, v_ref, sem):
    heads = k_ref.shape[1]
    me = lax.axis_index("ctx")
    for offset in range(devices):
        source = jnp.bitwise_and(me + devices - offset, devices - 1)
        for k in range(group):
            pair = table[offset * group + k]

            @pl.when(pair >= 0)
            def _():
                row, head = pair // heads, lax.rem(pair, heads)
                for which, ref in enumerate((k_ref, v_ref)):
                    src = got_ref.at[source * group + k, which]
                    pltpu.make_async_copy(src, ref.at[row, head], sem.at[which]).start()
    pltpu.make_async_copy(k_ref, k_ref, sem.at[0]).wait()
    pltpu.make_async_copy(v_ref, v_ref, sem.at[1]).wait()


def local(queries, key_cache, value_cache, row_lengths, kept_tiles, tile_dest):
    devices = lax.axis_size("ctx")
    rows, heads, span, width = key_cache.shape
    steps, _, q_heads, _ = queries.shape
    per = q_heads // heads
    pairs = rows * heads
    group = -(-pairs // devices)
    levels = 4
    assert steps == levels and tile_dest.shape[2] == devices and pairs % 2 == 0 and pairs <= LANES // 2
    assert devices > levels and devices & (devices - 1) == 0 and width == LANES

    kept = jnp.transpose(kept_tiles, (1, 0, 2))
    block_rows = rows * q_heads + 2 * per
    block_type = jax.ShapeDtypeStruct((block_rows, width), F32)
    message_type = jax.ShapeDtypeStruct((rows * q_heads + 4 * per, width), BF16)
    tiles_type = jax.ShapeDtypeStruct((devices * group, 2, span, width), BF16)

    tiles_out, table = pl.pallas_call(
        functools.partial(stage_kernel, devices, group),
        out_shape=[tiles_type, jax.ShapeDtypeStruct((devices * group,), jnp.int32)],
        in_specs=[HBM, HBM, HBM],
        out_specs=[HBM, SMEM],
        scratch_shapes=[
            pltpu.VMEM(key_cache.shape, BF16),
            pltpu.VMEM(value_cache.shape, BF16),
            pltpu.SMEM(tile_dest.shape, jnp.int32),
            pltpu.SMEM((devices,), jnp.int32),
            pltpu.SemaphoreType.DMA((3,)),
            pltpu.SemaphoreType.DMA((2, rows)),
        ],
        compiler_params=WHOLE,
        cost_estimate=COST,
        name="stage",
    )(tile_dest, key_cache, value_cache)
    tiles_in = lax.all_to_all(tiles_out, "ctx", split_axis=0, concat_axis=0, tiled=True)

    stats, *chunks = pl.pallas_call(
        functools.partial(attend_kernel, levels),
        out_shape=[
            jax.ShapeDtypeStruct((2, steps * per, LANES), F32),
        ] + [jax.ShapeDtypeStruct((2, block_rows, width), F32)] * 2,
        in_specs=[SMEM, HBM, HBM, VMEM, VMEM, VMEM],
        out_specs=[VMEM] * 3,
        scratch_shapes=[
            pltpu.SMEM(row_lengths.shape, jnp.int32),
            pltpu.SMEM(kept.shape, jnp.int32),
            pltpu.SemaphoreType.DMA((2,)),
        ],
        compiler_params=PARAMS,
        cost_estimate=COST,
        name="attend",
    )(table, row_lengths, kept, queries, key_cache, value_cache)

    def flip(x, bit):
        return lax.ppermute(x, "ctx", [(i, i ^ bit) for i in range(devices)])

    def local_call(kernel, name, out_shape, *operands):
        return pl.pallas_call(
            kernel,
            out_shape=out_shape,
            in_specs=[VMEM] * len(operands),
            out_specs=[VMEM] * len(out_shape),
            compiler_params=PARAMS,
            cost_estimate=COST,
            name=name,
        )(*operands)

    def merged(name, bit, own, got, out_shape):
        return local_call(functools.partial(merge_kernel, bit, pairs, per), name, out_shape, own, got)

    block, sent = merged("core", 1, chunks[0], flip(chunks[1], 1), [block_type] * 2)
    block, = merged("near", 2, block, flip(sent, 2), [block_type])
    bit = levels
    while 2 * bit < devices:
        block, = merged("far", bit, block, flip(block, bit), [block_type])
        bit *= 2
    sums_type = jax.ShapeDtypeStruct((rows * q_heads, width), F32)
    stats_type = jax.ShapeDtypeStruct((3 * per, width), F32)
    sums, sum_stats = local_call(functools.partial(scale_kernel, pairs, per), "scale", [sums_type, stats_type], block)
    sums = lax.reduce_precision(sums, 5, 10)
    got = flip(sums.astype(jnp.float16), bit).astype(F32)
    message, = local_call(
        functools.partial(last_kernel, bit, pairs, per), "last", [message_type],
        sums, got, sum_stats, flip(sum_stats, bit),
    )
    other = flip(message, 2)

    moved_keys, moved_values = pl.pallas_call(
        functools.partial(place_kernel, devices, group),
        out_shape=[
            jax.ShapeDtypeStruct(key_cache.shape, BF16),
            jax.ShapeDtypeStruct(value_cache.shape, BF16),
        ],
        in_specs=[SMEM, ANY],
        out_specs=[HBM, HBM],
        scratch_shapes=[pltpu.SemaphoreType.DMA((2,))],
        compiler_params=PARAMS,
        cost_estimate=COST,
        name="place",
    )(table, tiles_in)

    other, moved_keys = lax.optimization_barrier((other, moved_keys))
    arrived = [message, other, flip(message, 1), flip(other, 1)]

    attn_out, mass = pl.pallas_call(
        functools.partial(finish_kernel, pairs, per, heads, levels),
        out_shape=[
            jax.ShapeDtypeStruct((steps, rows * q_heads, width), BF16),
            jax.ShapeDtypeStruct((rows, 1, heads), F32),
        ],
        in_specs=[VMEM] * (1 + levels),
        out_specs=[HBM, HBM],
        scratch_shapes=[pltpu.VMEM((rows, 1, heads), F32), pltpu.SemaphoreType.DMA((levels + 1,))],
        compiler_params=PARAMS,
        cost_estimate=COST,
        name="finish",
    )(stats, *arrived)
    return attn_out.reshape(queries.shape), jnp.transpose(mass, (0, 2, 1)), moved_keys, moved_values


def solution(mesh):
    in_specs = (
        P(None, "grp", None, None),
        P("grp", None, "ctx", None),
        P("grp", None, "ctx", None),
        P("grp"),
        P(None, "grp", None),
        P("grp", None, None),
    )
    out_specs = (
        P(None, "grp", None, None),
        P("grp", None, "ctx"),
        P("grp", None, "ctx", None),
        P("grp", None, "ctx", None),
    )
    return jax.shard_map(local, mesh=mesh, in_specs=in_specs, out_specs=out_specs, check_vma=False)
```

```python
import functools

import jax
import jax.numpy as jnp
from jax import lax
from jax.experimental import pallas as pl
from jax.experimental.pallas import tpu as pltpu
from jax.sharding import PartitionSpec as P

absent_score = -1e30
LANES = 128
F32 = jnp.float32
BF16 = jnp.bfloat16
VMEM = pl.BlockSpec(memory_space=pltpu.VMEM)
SMEM = pl.BlockSpec(memory_space=pltpu.SMEM)
HBM = pl.BlockSpec(memory_space=pltpu.HBM)
ANY = pl.BlockSpec(memory_space=pl.ANY)
PARAMS = pltpu.CompilerParams(vmem_limit_bytes=16 * 1024 * 1024)
WHOLE = pltpu.CompilerParams(vmem_limit_bytes=62 * 1024 * 1024)


COST = pl.CostEstimate(flops=1000, bytes_accessed=1000, transcendentals=0)


def stage_kernel(devices, group, dest_hbm, k_ref, v_ref, buf, table, k_vm, v_vm, dest, counts, sem, load_sem):
    rows, heads = k_ref.shape[:2]
    small = pltpu.make_async_copy(dest_hbm, dest, sem.at[0])
    small.start()
    loads = []
    for row in range(rows):
        for which, (src, dst) in enumerate(((k_ref, k_vm), (v_ref, v_vm))):
            copy = pltpu.make_async_copy(src.at[row], dst.at[row], load_sem.at[which, row])
            copy.start()
            loads.append(copy)
    me = lax.axis_index("ctx")

    def clear(i, carry):
        counts[i] = 0
        for k in range(group):
            table[i * group + k] = -1
        return carry

    lax.fori_loop(0, devices, clear, 0)
    small.wait()
    for row in range(rows):
        loads[2 * row].wait()
        loads[2 * row + 1].wait()

        def send(head, carry):
            offset = dest[row, head, 0]
            rank = counts[offset]
            counts[offset] = rank + 1
            table[offset * group + rank] = row * heads + head
            slot = jnp.bitwise_and(me + offset, devices - 1) * group + rank
            pltpu.make_async_copy(k_vm.at[row, head], buf.at[slot, 0], sem.at[1]).start()
            pltpu.make_async_copy(v_vm.at[row, head], buf.at[slot, 1], sem.at[2]).start()
            return carry

        lax.fori_loop(0, heads, send, 0)
    pltpu.make_async_copy(k_ref, k_vm, sem.at[1]).wait()
    pltpu.make_async_copy(v_ref, v_vm, sem.at[2]).wait()


def attend_kernel(
    levels,
    table, len_hbm, kept_hbm, q_ref, k_ref, v_ref,
    stats_ref, *rest,
):
    chunks = rest[:levels // 2]
    len_ref, kept_ref, small_sem = rest[levels // 2:]
    rows, heads, tile, width = k_ref.shape
    steps, _, q_heads, _ = q_ref.shape
    per = q_heads // heads
    me = lax.axis_index("ctx")

    small = [
        pltpu.make_async_copy(len_hbm, len_ref, small_sem.at[0]),
        pltpu.make_async_copy(kept_hbm, kept_ref, small_sem.at[1]),
    ]
    for copy in small:
        copy.start()
    for copy in small:
        copy.wait()

    lane = lax.broadcasted_iota(jnp.int32, (per, tile), 1)
    pair_lane = lax.broadcasted_iota(jnp.int32, (steps * per, LANES), 1)
    peaks = jnp.full((steps * per, LANES), absent_score, F32)
    totals = jnp.zeros((steps * per, LANES), F32)
    order = [jnp.bitwise_xor(place_of(me), level) for level in range(levels)]
    scale = width ** -0.5
    block = steps * per
    for row in range(rows):
        queries = [q_ref[step, row].astype(F32) for step in order]
        live = []
        for step in order:
            limit = jnp.where(kept_ref[row, step, me] > 0, len_ref[row] - me * tile, 0)
            live.append(lane < limit)
        live = jnp.concatenate(live * heads, axis=0)
        scores = []
        for head in range(heads):
            q = jnp.concatenate([x[head * per:(head + 1) * per] for x in queries], axis=0).astype(BF16)
            scores.append(lax.dot_general(
                q, k_ref[row, head], (((1,), (1,)), ((), ())), preferred_element_type=F32
            ))
        scores = jnp.concatenate(scores, axis=0) * scale
        peak = jnp.max(jnp.where(live, scores, absent_score), axis=1, keepdims=True)
        weights = jnp.where(live, jnp.exp(scores - peak), 0.0)
        total = jnp.sum(weights, axis=1, keepdims=True)
        rounded = weights.astype(BF16)
        for head in range(heads):
            out = jnp.dot(
                rounded[head * block:(head + 1) * block], v_ref[row, head], preferred_element_type=F32
            )
            pair = row * heads + head
            for i in range(levels):
                chunks[i // 2][i % 2, pair * per:(pair + 1) * per, :] = out[i * per:(i + 1) * per]
            here = pair_lane == pair
            peaks = jnp.where(here, peak[head * block:(head + 1) * block], peaks)
            totals = jnp.where(here, total[head * block:(head + 1) * block], totals)
    base = rows * q_heads
    for i in range(levels):
        chunks[i // 2][i % 2, base:base + per, :] = peaks[i * per:(i + 1) * per]
        chunks[i // 2][i % 2, base + per:base + 2 * per, :] = totals[i * per:(i + 1) * per]
    stats_ref[0] = peaks
    stats_ref[1] = totals


def place_of(me):
    return lax.rem(me, 2) * 2 + lax.rem(me // 2, 2)


def merge(swap, own, got, pairs, per, own_stats=None, got_stats=None):
    def both(rows, own=own, got=got):
        x, y = own[rows, :], got[rows, :]
        return jnp.where(swap, y, x), jnp.where(swap, x, y)

    scaled = own_stats is not None
    base = 0 if scaled else pairs * per
    stats = (own_stats, got_stats) if scaled else (own, got)
    peaks = both(slice(base, base + per), *stats)
    totals = both(slice(base + per, base + 2 * per), *stats)
    peak = jnp.maximum(*peaks)
    factors = [jnp.exp(x - peak) for x in peaks]
    total = factors[0] * totals[0] + factors[1] * totals[1]
    if scaled:
        scales = both(slice(2 * per, 3 * per), *stats)
        factors = [f * x for f, x in zip(factors, scales)]

    def summed(pair):
        first, second = [jnp.broadcast_to(f[:, pair:pair + 1], (per, LANES)) for f in factors]
        x, y = both(slice(pair * per, (pair + 1) * per))
        return first * x + second * y

    return peak, total, summed


def merge_kernel(bit, pairs, per, own, got, *outs):
    swap = lax.rem(lax.axis_index("ctx") // bit, 2) == 1
    base = pairs * per
    for i, out in enumerate(outs):
        x, y = (own, got) if len(outs) == 1 else (own.at[i], got.at[i])
        peak, total, summed = merge(swap, x, y, pairs, per)
        for pair in range(pairs):
            out[pair * per:(pair + 1) * per, :] = summed(pair)
        out[base:base + per, :] = peak
        out[base + per:base + 2 * per, :] = total


def halve_kernel(bit, pairs, per, own, got, kept, sent, work):
    index = lax.axis_index("ctx")
    peak, total, summed = merge(lax.rem(index // bit, 2) == 1, own, got, pairs, per)
    share = pairs // 2
    base = share * per
    for half in range(2):
        for i in range(share):
            work[half, i * per:(i + 1) * per, :] = summed(half * share + i)
        for i, x in enumerate((peak, total)):
            at = base + i * per
            work[half, at:at + per, :] = pltpu.roll(x, LANES - share, 1) if half else x
    mine = lax.rem(index // (2 * bit), 2)
    kept[...] = work[mine]
    sent[...] = work[1 - mine]


def scale_kernel(pairs, per, block, sums, stats):
    lane = lax.broadcasted_iota(jnp.int32, (per, LANES), 1)
    base = pairs * per
    scales = jnp.ones((per, LANES), F32)
    for pair in range(pairs):
        x = block[pair * per:(pair + 1) * per, :]
        largest = jnp.max(jnp.abs(x), axis=1, keepdims=True)
        largest = jnp.where(largest > 0.0, largest, 1.0)
        sums[pair * per:(pair + 1) * per, :] = x / largest
        scales = jnp.where(lane == pair, largest, scales)
    stats[:2 * per, :] = block[base:base + 2 * per, :]
    stats[2 * per:, :] = scales


def last_kernel(bit, pairs, per, own, got, own_stats, got_stats, out):
    swap = lax.rem(lax.axis_index("ctx") // bit, 2) == 1
    base = pairs * per
    peak, total, summed = merge(swap, own, got, pairs, per, own_stats, got_stats)
    lane = lax.broadcasted_iota(jnp.int32, peak.shape, 1)
    total = jnp.where(lane < pairs, total, 1.0)
    peak = jnp.where(lane < pairs, peak, 0.0)

    def result(pair):
        return summed(pair) / jnp.broadcast_to(total[:, pair:pair + 1], (per, LANES))

    for pair in range(0, pairs, 2):
        both = jnp.concatenate([result(pair), result(pair + 1)], axis=0)
        out[pair * per:(pair + 2) * per, :] = both.astype(BF16)
    rest = jnp.concatenate([peak, total], axis=0)
    lane = lax.broadcasted_iota(jnp.int32, rest.shape, 1)
    parts = []
    for i in range(3):
        parts.append(rest.astype(BF16).astype(F32))
        rest = rest - parts[i]
    half = LANES // 2
    packed = jnp.where(lane < half, parts[0], pltpu.roll(parts[1], half, 1))
    out[base:base + 2 * per, :] = packed.astype(BF16)
    out[base + 2 * per:base + 4 * per, :] = parts[2].astype(BF16)


def finish_kernel(pairs, per, heads, levels, stats_ref, *refs):
    ins, (out, mass_ref, mass_vm, sem) = refs[:2 * levels], refs[2 * levels:]
    me = lax.axis_index("ctx")
    share = pairs // 2
    base = share * per
    mine = lax.rem(me // levels, 2)
    copies = []
    for level in range(levels):
        for far in range(2):
            step, half = jnp.bitwise_xor(place_of(me), level), jnp.bitwise_xor(mine, far)
            i = 2 * level + far
            copies.append(pltpu.make_async_copy(ins[i].at[:base], out.at[step, half], sem.at[i]))
            copies[i].start()
    lane = lax.broadcasted_iota(jnp.int32, (2 * per, LANES), 1)
    masses = [jnp.zeros((per, LANES), F32)] * 2
    for level in range(levels):
        rows = slice(level * per, (level + 1) * per)
        own_peak, own_total = stats_ref[0, rows, :], stats_ref[1, rows, :]
        for far in range(2):
            message = ins[2 * level + far]
            packed = message[base:base + 2 * per, :].astype(F32)
            third = message[base + 2 * per:base + 4 * per, :].astype(F32)
            both = third + pltpu.roll(packed, LANES // 2, 1) + packed
            both = jnp.where(lane < share, both, 1.0)
            second = jnp.bitwise_xor(mine, far) == 1
            peak, total = [
                jnp.where(second, pltpu.roll(x, LANES - share, 1), x) for x in (own_peak, own_total)
            ]
            mass = total * (jnp.exp(jnp.minimum(peak - both[:per], 0.0)) / both[per:])
            masses = [masses[0] + jnp.where(second, 0.0, mass), masses[1] + jnp.where(second, mass, 0.0)]
    for half in range(2):
        mass = jnp.sum(masses[half], axis=0, keepdims=True)
        for i in range(share // heads):
            mass_vm[half * (share // heads) + i] = mass[:, i * heads:(i + 1) * heads]
    copies.append(pltpu.make_async_copy(mass_vm, mass_ref, sem.at[2 * levels]))
    copies[-1].start()
    for copy in copies:
        copy.wait()


def place_kernel(devices, group, table, got_ref, k_ref, v_ref, sem):
    heads = k_ref.shape[1]
    me = lax.axis_index("ctx")
    for offset in range(devices):
        source = jnp.bitwise_and(me + devices - offset, devices - 1)
        for k in range(group):
            pair = table[offset * group + k]

            @pl.when(pair >= 0)
            def _():
                row, head = pair // heads, lax.rem(pair, heads)
                for which, ref in enumerate((k_ref, v_ref)):
                    src = got_ref.at[source * group + k, which]
                    pltpu.make_async_copy(src, ref.at[row, head], sem.at[which]).start()
    pltpu.make_async_copy(k_ref, k_ref, sem.at[0]).wait()
    pltpu.make_async_copy(v_ref, v_ref, sem.at[1]).wait()


def local(queries, key_cache, value_cache, row_lengths, kept_tiles, tile_dest):
    devices = lax.axis_size("ctx")
    rows, heads, span, width = key_cache.shape
    steps, _, q_heads, _ = queries.shape
    per = q_heads // heads
    pairs = rows * heads
    group = -(-pairs // devices)
    levels = 4
    assert steps == levels and tile_dest.shape[2] == devices and pairs % 2 == 0 and pairs <= LANES // 2
    assert devices > 2 * levels and devices & (devices - 1) == 0 and width == LANES
    assert pairs % (2 * heads) == 0
    share = pairs // 2

    kept = jnp.transpose(kept_tiles, (1, 0, 2))
    block_rows = rows * q_heads + 2 * per
    block_type = jax.ShapeDtypeStruct((block_rows, width), F32)
    half_type = jax.ShapeDtypeStruct((share * per + 2 * per, width), F32)
    message_type = jax.ShapeDtypeStruct((share * per + 4 * per, width), BF16)
    tiles_type = jax.ShapeDtypeStruct((devices * group, 2, span, width), BF16)

    tiles_out, table = pl.pallas_call(
        functools.partial(stage_kernel, devices, group),
        out_shape=[tiles_type, jax.ShapeDtypeStruct((devices * group,), jnp.int32)],
        in_specs=[HBM, HBM, HBM],
        out_specs=[HBM, SMEM],
        scratch_shapes=[
            pltpu.VMEM(key_cache.shape, BF16),
            pltpu.VMEM(value_cache.shape, BF16),
            pltpu.SMEM(tile_dest.shape, jnp.int32),
            pltpu.SMEM((devices,), jnp.int32),
            pltpu.SemaphoreType.DMA((3,)),
            pltpu.SemaphoreType.DMA((2, rows)),
        ],
        compiler_params=WHOLE,
        cost_estimate=COST,
        name="stage",
    )(tile_dest, key_cache, value_cache)
    tiles_in = lax.all_to_all(tiles_out, "ctx", split_axis=0, concat_axis=0, tiled=True)

    stats, *chunks = pl.pallas_call(
        functools.partial(attend_kernel, levels),
        out_shape=[
            jax.ShapeDtypeStruct((2, steps * per, LANES), F32),
        ] + [jax.ShapeDtypeStruct((2, block_rows, width), F32)] * 2,
        in_specs=[SMEM, HBM, HBM, VMEM, VMEM, VMEM],
        out_specs=[VMEM] * 3,
        scratch_shapes=[
            pltpu.SMEM(row_lengths.shape, jnp.int32),
            pltpu.SMEM(kept.shape, jnp.int32),
            pltpu.SemaphoreType.DMA((2,)),
        ],
        compiler_params=PARAMS,
        cost_estimate=COST,
        name="attend",
    )(table, row_lengths, kept, queries, key_cache, value_cache)

    def flip(x, bit):
        return lax.ppermute(x, "ctx", [(i, i ^ bit) for i in range(devices)])

    def local_call(kernel, name, out_shape, *operands, scratch=()):
        return pl.pallas_call(
            kernel,
            out_shape=out_shape,
            in_specs=[VMEM] * len(operands),
            out_specs=[VMEM] * len(out_shape),
            scratch_shapes=scratch,
            compiler_params=PARAMS,
            cost_estimate=COST,
            name=name,
        )(*operands)

    block, sent = local_call(
        functools.partial(merge_kernel, 1, pairs, per), "core", [block_type] * 2, chunks[0], flip(chunks[1], 1)
    )
    block, sent = local_call(
        functools.partial(halve_kernel, 2, pairs, per), "near", [half_type] * 2, block, flip(sent, 2),
        scratch=[pltpu.VMEM((2,) + half_type.shape, F32)],
    )
    bit, got = levels, flip(sent, levels)
    while True:
        block, = local_call(functools.partial(merge_kernel, bit, share, per), "far", [half_type], block, got)
        bit *= 2
        if 2 * bit == devices:
            break
        got = flip(block, bit)
    sums_type = jax.ShapeDtypeStruct((share * per, width), F32)
    stats_type = jax.ShapeDtypeStruct((3 * per, width), F32)
    sums, sum_stats = local_call(functools.partial(scale_kernel, share, per), "scale", [sums_type, stats_type], block)
    sums = lax.reduce_precision(sums, 5, 10)
    got = flip(sums.astype(jnp.float16), bit).astype(F32)
    message, = local_call(
        functools.partial(last_kernel, bit, share, per), "last", [message_type],
        sums, got, sum_stats, flip(sum_stats, bit),
    )
    near = [message, flip(message, levels), flip(message, 2), flip(message, 2 + levels)]

    moved_keys, moved_values = pl.pallas_call(
        functools.partial(place_kernel, devices, group),
        out_shape=[
            jax.ShapeDtypeStruct(key_cache.shape, BF16),
            jax.ShapeDtypeStruct(value_cache.shape, BF16),
        ],
        in_specs=[SMEM, ANY],
        out_specs=[HBM, HBM],
        scratch_shapes=[pltpu.SemaphoreType.DMA((2,))],
        compiler_params=PARAMS,
        cost_estimate=COST,
        name="place",
    )(table, tiles_in)

    *forward, moved_keys = lax.optimization_barrier((*near[1:], moved_keys))
    near = [message, *forward]
    arrived = near + [flip(x, 1) for x in near]

    attn_out, mass = pl.pallas_call(
        functools.partial(finish_kernel, pairs, per, heads, levels),
        out_shape=[
            jax.ShapeDtypeStruct((steps, 2, share * per, width), BF16),
            jax.ShapeDtypeStruct((rows, 1, heads), F32),
        ],
        in_specs=[VMEM] * (1 + 2 * levels),
        out_specs=[HBM, HBM],
        scratch_shapes=[pltpu.VMEM((rows, 1, heads), F32), pltpu.SemaphoreType.DMA((2 * levels + 1,))],
        compiler_params=PARAMS,
        cost_estimate=COST,
        name="finish",
    )(stats, *arrived)
    return attn_out.reshape(queries.shape), jnp.transpose(mass, (0, 2, 1)), moved_keys, moved_values


def solution(mesh):
    in_specs = (
        P(None, "grp", None, None),
        P("grp", None, "ctx", None),
        P("grp", None, "ctx", None),
        P("grp"),
        P(None, "grp", None),
        P("grp", None, None),
    )
    out_specs = (
        P(None, "grp", None, None),
        P("grp", None, "ctx"),
        P("grp", None, "ctx", None),
        P("grp", None, "ctx", None),
    )
    return jax.shard_map(local, mesh=mesh, in_specs=in_specs, out_specs=out_specs, check_vma=False)
```

```python
import functools

import jax
import jax.numpy as jnp
from jax import lax
from jax.experimental import pallas as pl
from jax.experimental.pallas import tpu as pltpu
from jax.sharding import PartitionSpec as P

absent_score = -1e30
LANES = 128
F32 = jnp.float32
BF16 = jnp.bfloat16
VMEM = pl.BlockSpec(memory_space=pltpu.VMEM)
SMEM = pl.BlockSpec(memory_space=pltpu.SMEM)
HBM = pl.BlockSpec(memory_space=pltpu.HBM)
ANY = pl.BlockSpec(memory_space=pl.ANY)
PARAMS = pltpu.CompilerParams(vmem_limit_bytes=16 * 1024 * 1024)
WHOLE = pltpu.CompilerParams(vmem_limit_bytes=62 * 1024 * 1024)


COST = pl.CostEstimate(flops=1000, bytes_accessed=1000, transcendentals=0)


def stage_kernel(
    devices, group, first, dest_hbm, k_ref, v_ref, buf, buf_rest, table, k_vm, v_vm, dest, counts, sem, load_sem
):
    rows, heads = k_ref.shape[:2]
    small = pltpu.make_async_copy(dest_hbm, dest, sem.at[0])
    small.start()
    loads = []
    for row in range(rows):
        for which, (src, dst) in enumerate(((k_ref, k_vm), (v_ref, v_vm))):
            copy = pltpu.make_async_copy(src.at[row], dst.at[row], load_sem.at[which, row])
            copy.start()
            loads.append(copy)
    me = lax.axis_index("ctx")

    def clear(i, carry):
        counts[i] = 0
        for k in range(group):
            table[i * group + k] = -1
        return carry

    lax.fori_loop(0, devices, clear, 0)
    small.wait()
    for row in range(rows):
        loads[2 * row].wait()
        loads[2 * row + 1].wait()

        def send(head, carry):
            offset = dest[row, head, 0]
            rank = counts[offset]
            counts[offset] = rank + 1
            table[offset * group + rank] = row * heads + head
            target = jnp.bitwise_and(me + offset, devices - 1)
            pltpu.make_async_copy(k_vm.at[row, head], buf.at[target * first + rank], sem.at[1]).start()

            @pl.when(rank < first - group)
            def _():
                at = target * first + group + rank
                pltpu.make_async_copy(v_vm.at[row, head], buf.at[at], sem.at[2]).start()

            @pl.when(rank >= first - group)
            def _():
                at = target * (2 * group - first) + rank + group - first
                pltpu.make_async_copy(v_vm.at[row, head], buf_rest.at[at], sem.at[2]).start()
            return carry

        lax.fori_loop(0, heads, send, 0)
    pltpu.make_async_copy(k_ref, k_vm, sem.at[1]).wait()
    pltpu.make_async_copy(v_ref, v_vm, sem.at[2]).wait()


def attend_kernel(
    levels,
    table, len_hbm, kept_hbm, q_ref, k_ref, v_ref,
    stats_ref, *rest,
):
    chunks = rest[:levels // 2]
    len_ref, kept_ref, small_sem = rest[levels // 2:]
    rows, heads, tile, width = k_ref.shape
    steps, _, q_heads, _ = q_ref.shape
    per = q_heads // heads
    me = lax.axis_index("ctx")

    small = [
        pltpu.make_async_copy(len_hbm, len_ref, small_sem.at[0]),
        pltpu.make_async_copy(kept_hbm, kept_ref, small_sem.at[1]),
    ]
    for copy in small:
        copy.start()
    for copy in small:
        copy.wait()

    lane = lax.broadcasted_iota(jnp.int32, (per, tile), 1)
    pair_lane = lax.broadcasted_iota(jnp.int32, (steps * per, LANES), 1)
    peaks = jnp.full((steps * per, LANES), absent_score, F32)
    totals = jnp.zeros((steps * per, LANES), F32)
    order = [jnp.bitwise_xor(place_of(me), level) for level in range(levels)]
    scale = width ** -0.5
    block = steps * per
    for row in range(rows):
        queries = [q_ref[step, row].astype(F32) for step in order]
        live = []
        for step in order:
            limit = jnp.where(kept_ref[row, step, me] > 0, len_ref[row] - me * tile, 0)
            live.append(lane < limit)
        live = jnp.concatenate(live * heads, axis=0)
        scores = []
        for head in range(heads):
            q = jnp.concatenate([x[head * per:(head + 1) * per] for x in queries], axis=0).astype(BF16)
            scores.append(lax.dot_general(
                q, k_ref[row, head], (((1,), (1,)), ((), ())), preferred_element_type=F32
            ))
        scores = jnp.concatenate(scores, axis=0) * scale
        peak = jnp.max(jnp.where(live, scores, absent_score), axis=1, keepdims=True)
        weights = jnp.where(live, jnp.exp(scores - peak), 0.0)
        total = jnp.sum(weights, axis=1, keepdims=True)
        rounded = weights.astype(BF16)
        for head in range(heads):
            out = jnp.dot(
                rounded[head * block:(head + 1) * block], v_ref[row, head], preferred_element_type=F32
            )
            pair = row * heads + head
            for i in range(levels):
                chunks[i // 2][i % 2, pair * per:(pair + 1) * per, :] = out[i * per:(i + 1) * per]
            here = pair_lane == pair
            peaks = jnp.where(here, peak[head * block:(head + 1) * block], peaks)
            totals = jnp.where(here, total[head * block:(head + 1) * block], totals)
    base = rows * q_heads
    for i in range(levels):
        chunks[i // 2][i % 2, base:base + per, :] = peaks[i * per:(i + 1) * per]
        chunks[i // 2][i % 2, base + per:base + 2 * per, :] = totals[i * per:(i + 1) * per]
    stats_ref[0] = peaks
    stats_ref[1] = totals


def place_of(me):
    return lax.rem(me, 2) * 2 + lax.rem(me // 2, 2)


def merge(swap, own, got, pairs, per, own_stats=None, got_stats=None):
    def both(rows, own=own, got=got):
        x, y = own[rows, :], got[rows, :]
        return jnp.where(swap, y, x), jnp.where(swap, x, y)

    scaled = own_stats is not None
    base = 0 if scaled else pairs * per
    stats = (own_stats, got_stats) if scaled else (own, got)
    peaks = both(slice(base, base + per), *stats)
    totals = both(slice(base + per, base + 2 * per), *stats)
    peak = jnp.maximum(*peaks)
    factors = [jnp.exp(x - peak) for x in peaks]
    total = factors[0] * totals[0] + factors[1] * totals[1]
    if scaled:
        scales = both(slice(2 * per, 3 * per), *stats)
        factors = [f * x for f, x in zip(factors, scales)]

    def summed(pair):
        first, second = [jnp.broadcast_to(f[:, pair:pair + 1], (per, LANES)) for f in factors]
        x, y = both(slice(pair * per, (pair + 1) * per))
        return first * x + second * y

    return peak, total, summed


def merge_kernel(bit, pairs, per, own, got, *outs):
    swap = lax.rem(lax.axis_index("ctx") // bit, 2) == 1
    base = pairs * per
    for i, out in enumerate(outs):
        x, y = (own, got) if len(outs) == 1 else (own.at[i], got.at[i])
        peak, total, summed = merge(swap, x, y, pairs, per)
        for pair in range(pairs):
            out[pair * per:(pair + 1) * per, :] = summed(pair)
        out[base:base + per, :] = peak
        out[base + per:base + 2 * per, :] = total


def halve_kernel(bit, pairs, per, own, got, kept, sent, work):
    index = lax.axis_index("ctx")
    peak, total, summed = merge(lax.rem(index // bit, 2) == 1, own, got, pairs, per)
    share = pairs // 2
    base = share * per
    for half in range(2):
        for i in range(share):
            work[half, i * per:(i + 1) * per, :] = summed(half * share + i)
        for i, x in enumerate((peak, total)):
            at = base + i * per
            work[half, at:at + per, :] = pltpu.roll(x, LANES - share, 1) if half else x
    mine = lax.rem(index // (2 * bit), 2)
    kept[...] = work[mine]
    sent[...] = work[1 - mine]


def scale_kernel(pairs, per, block, sums, stats):
    lane = lax.broadcasted_iota(jnp.int32, (per, LANES), 1)
    base = pairs * per
    scales = jnp.ones((per, LANES), F32)
    for pair in range(pairs):
        x = block[pair * per:(pair + 1) * per, :]
        largest = jnp.max(jnp.abs(x), axis=1, keepdims=True)
        largest = jnp.where(largest > 0.0, largest, 1.0)
        sums[pair * per:(pair + 1) * per, :] = x / largest
        scales = jnp.where(lane == pair, largest, scales)
    stats[:2 * per, :] = block[base:base + 2 * per, :]
    stats[2 * per:, :] = scales


def last_kernel(bit, pairs, per, own, got, own_stats, got_stats, out):
    swap = lax.rem(lax.axis_index("ctx") // bit, 2) == 1
    base = pairs * per
    peak, total, summed = merge(swap, own, got, pairs, per, own_stats, got_stats)
    lane = lax.broadcasted_iota(jnp.int32, peak.shape, 1)
    total = jnp.where(lane < pairs, total, 1.0)
    peak = jnp.where(lane < pairs, peak, 0.0)

    def result(pair):
        return summed(pair) / jnp.broadcast_to(total[:, pair:pair + 1], (per, LANES))

    for pair in range(0, pairs, 2):
        both = jnp.concatenate([result(pair), result(pair + 1)], axis=0)
        out[pair * per:(pair + 2) * per, :] = both.astype(BF16)
    rest = jnp.concatenate([peak, total], axis=0)
    lane = lax.broadcasted_iota(jnp.int32, rest.shape, 1)
    parts = []
    for i in range(3):
        parts.append(rest.astype(BF16).astype(F32))
        rest = rest - parts[i]
    half = LANES // 2
    packed = jnp.where(lane < half, parts[0], pltpu.roll(parts[1], half, 1))
    out[base:base + 2 * per, :] = packed.astype(BF16)
    out[base + 2 * per:base + 4 * per, :] = parts[2].astype(BF16)


def finish_kernel(pairs, per, heads, levels, stats_ref, *refs):
    ins, (out, mass_ref, mass_vm, sem) = refs[:2 * levels], refs[2 * levels:]
    me = lax.axis_index("ctx")
    share = pairs // 2
    base = share * per
    mine = lax.rem(me // levels, 2)
    copies = []
    for level in range(levels):
        for far in range(2):
            step, half = jnp.bitwise_xor(place_of(me), level), jnp.bitwise_xor(mine, far)
            i = 2 * level + far
            copies.append(pltpu.make_async_copy(ins[i].at[:base], out.at[step, half], sem.at[i]))
            copies[i].start()
    lane = lax.broadcasted_iota(jnp.int32, (2 * per, LANES), 1)
    masses = [jnp.zeros((per, LANES), F32)] * 2
    for level in range(levels):
        rows = slice(level * per, (level + 1) * per)
        own_peak, own_total = stats_ref[0, rows, :], stats_ref[1, rows, :]
        for far in range(2):
            message = ins[2 * level + far]
            packed = message[base:base + 2 * per, :].astype(F32)
            third = message[base + 2 * per:base + 4 * per, :].astype(F32)
            both = third + pltpu.roll(packed, LANES // 2, 1) + packed
            both = jnp.where(lane < share, both, 1.0)
            second = jnp.bitwise_xor(mine, far) == 1
            peak, total = [
                jnp.where(second, pltpu.roll(x, LANES - share, 1), x) for x in (own_peak, own_total)
            ]
            mass = total * (jnp.exp(jnp.minimum(peak - both[:per], 0.0)) / both[per:])
            masses = [masses[0] + jnp.where(second, 0.0, mass), masses[1] + jnp.where(second, mass, 0.0)]
    for half in range(2):
        mass = jnp.sum(masses[half], axis=0, keepdims=True)
        for i in range(share // heads):
            mass_vm[half * (share // heads) + i] = mass[:, i * heads:(i + 1) * heads]
    copies.append(pltpu.make_async_copy(mass_vm, mass_ref, sem.at[2 * levels]))
    copies[-1].start()
    for copy in copies:
        copy.wait()


def place_keys_kernel(devices, group, first, table, got, out, sem):
    heads = out.shape[1]
    me = lax.axis_index("ctx")
    for offset in range(devices):
        source = jnp.bitwise_and(me + devices - offset, devices - 1)
        for k in range(group):
            put(got.at[source * first + k], table[offset * group + k], heads, out, sem)
    pltpu.make_async_copy(out, out, sem).wait()


def place_values_kernel(devices, group, first, table, got, got_rest, out, sem):
    heads = out.shape[1]
    me = lax.axis_index("ctx")
    rest = 2 * group - first
    for offset in range(devices):
        source = jnp.bitwise_and(me + devices - offset, devices - 1)
        for k in range(group):
            at = group + k
            src = got.at[source * first + at] if at < first else got_rest.at[source * rest + at - first]
            put(src, table[offset * group + k], heads, out, sem)
    pltpu.make_async_copy(out, out, sem).wait()


def put(src, pair, heads, out, sem):
    @pl.when(pair >= 0)
    def _():
        pltpu.make_async_copy(src, out.at[pair // heads, lax.rem(pair, heads)], sem).start()


def local(queries, key_cache, value_cache, row_lengths, kept_tiles, tile_dest):
    devices = lax.axis_size("ctx")
    rows, heads, span, width = key_cache.shape
    steps, _, q_heads, _ = queries.shape
    per = q_heads // heads
    pairs = rows * heads
    group = -(-pairs // devices)
    levels = 4
    assert steps == levels and tile_dest.shape[2] == devices and pairs % 2 == 0 and pairs <= LANES // 2
    assert devices > 2 * levels and devices & (devices - 1) == 0 and width == LANES
    assert pairs % (2 * heads) == 0
    share = pairs // 2

    kept = jnp.transpose(kept_tiles, (1, 0, 2))
    block_rows = rows * q_heads + 2 * per
    block_type = jax.ShapeDtypeStruct((block_rows, width), F32)
    half_type = jax.ShapeDtypeStruct((share * per + 2 * per, width), F32)
    message_type = jax.ShapeDtypeStruct((share * per + 4 * per, width), BF16)
    first = 2 * group - max(1, 2 * group // 3)

    def tiles_type(count):
        return jax.ShapeDtypeStruct((devices * count, span, width), BF16)

    def exchange(x):
        return lax.all_to_all(x, "ctx", split_axis=0, concat_axis=0, tiled=True)


    tiles_out, rest_out, table = pl.pallas_call(
        functools.partial(stage_kernel, devices, group, first),
        out_shape=[
            tiles_type(first), tiles_type(2 * group - first),
            jax.ShapeDtypeStruct((devices * group,), jnp.int32),
        ],
        in_specs=[HBM, HBM, HBM],
        out_specs=[HBM, HBM, SMEM],
        scratch_shapes=[
            pltpu.VMEM(key_cache.shape, BF16),
            pltpu.VMEM(value_cache.shape, BF16),
            pltpu.SMEM(tile_dest.shape, jnp.int32),
            pltpu.SMEM((devices,), jnp.int32),
            pltpu.SemaphoreType.DMA((3,)),
            pltpu.SemaphoreType.DMA((2, rows)),
        ],
        compiler_params=WHOLE,
        cost_estimate=COST,
        name="stage",
    )(tile_dest, key_cache, value_cache)
    tiles_in = exchange(tiles_out)

    stats, *chunks = pl.pallas_call(
        functools.partial(attend_kernel, levels),
        out_shape=[
            jax.ShapeDtypeStruct((2, steps * per, LANES), F32),
        ] + [jax.ShapeDtypeStruct((2, block_rows, width), F32)] * 2,
        in_specs=[SMEM, HBM, HBM, VMEM, VMEM, VMEM],
        out_specs=[VMEM] * 3,
        scratch_shapes=[
            pltpu.SMEM(row_lengths.shape, jnp.int32),
            pltpu.SMEM(kept.shape, jnp.int32),
            pltpu.SemaphoreType.DMA((2,)),
        ],
        compiler_params=PARAMS,
        cost_estimate=COST,
        name="attend",
    )(table, row_lengths, kept, queries, key_cache, value_cache)

    def flip(x, bit):
        return lax.ppermute(x, "ctx", [(i, i ^ bit) for i in range(devices)])

    def local_call(kernel, name, out_shape, *operands, scratch=()):
        return pl.pallas_call(
            kernel,
            out_shape=out_shape,
            in_specs=[VMEM] * len(operands),
            out_specs=[VMEM] * len(out_shape),
            scratch_shapes=scratch,
            compiler_params=PARAMS,
            cost_estimate=COST,
            name=name,
        )(*operands)

    block, sent = local_call(
        functools.partial(merge_kernel, 1, pairs, per), "core", [block_type] * 2, chunks[0], flip(chunks[1], 1)
    )
    block, sent = local_call(
        functools.partial(halve_kernel, 2, pairs, per), "near", [half_type] * 2, block, flip(sent, 2),
        scratch=[pltpu.VMEM((2,) + half_type.shape, F32)],
    )
    bit, got = levels, flip(sent, levels)
    while True:
        block, = local_call(functools.partial(merge_kernel, bit, share, per), "far", [half_type], block, got)
        bit *= 2
        if 2 * bit == devices:
            break
        got = flip(block, bit)
    sums_type = jax.ShapeDtypeStruct((share * per, width), F32)
    stats_type = jax.ShapeDtypeStruct((3 * per, width), F32)
    sums, sum_stats = local_call(functools.partial(scale_kernel, share, per), "scale", [sums_type, stats_type], block)
    sums = lax.reduce_precision(sums, 5, 10)
    got = flip(sums.astype(jnp.float16), bit).astype(F32)
    got, got_stats, rest_out = lax.optimization_barrier((got, flip(sum_stats, bit), rest_out))
    rest_in = exchange(rest_out)
    message, = local_call(
        functools.partial(last_kernel, bit, share, per), "last", [message_type], sums, got, sum_stats, got_stats,
    )
    near = [message, flip(message, levels), flip(message, 2), flip(message, 2 + levels)]

    def place(kernel, name, *got):
        return pl.pallas_call(
            functools.partial(kernel, devices, group, first),
            out_shape=jax.ShapeDtypeStruct(key_cache.shape, BF16),
            in_specs=[SMEM] + [ANY] * len(got),
            out_specs=HBM,
            scratch_shapes=[pltpu.SemaphoreType.DMA],
            compiler_params=PARAMS,
            cost_estimate=COST,
            name=name,
        )(table, *got)

    moved_keys = place(place_keys_kernel, "place_keys", tiles_in)
    moved_values = place(place_values_kernel, "place_values", tiles_in, rest_in)
    arrived = near + [flip(x, 1) for x in near]

    attn_out, mass = pl.pallas_call(
        functools.partial(finish_kernel, pairs, per, heads, levels),
        out_shape=[
            jax.ShapeDtypeStruct((steps, 2, share * per, width), BF16),
            jax.ShapeDtypeStruct((rows, 1, heads), F32),
        ],
        in_specs=[VMEM] * (1 + 2 * levels),
        out_specs=[HBM, HBM],
        scratch_shapes=[pltpu.VMEM((rows, 1, heads), F32), pltpu.SemaphoreType.DMA((2 * levels + 1,))],
        compiler_params=PARAMS,
        cost_estimate=COST,
        name="finish",
    )(stats, *arrived)
    return attn_out.reshape(queries.shape), jnp.transpose(mass, (0, 2, 1)), moved_keys, moved_values


def solution(mesh):
    in_specs = (
        P(None, "grp", None, None),
        P("grp", None, "ctx", None),
        P("grp", None, "ctx", None),
        P("grp"),
        P(None, "grp", None),
        P("grp", None, None),
    )
    out_specs = (
        P(None, "grp", None, None),
        P("grp", None, "ctx"),
        P("grp", None, "ctx", None),
        P("grp", None, "ctx", None),
    )
    return jax.shard_map(local, mesh=mesh, in_specs=in_specs, out_specs=out_specs, check_vma=False)
```

```python
import functools

import jax
import jax.numpy as jnp
from jax import lax
from jax.experimental import pallas as pl
from jax.experimental.pallas import tpu as pltpu
from jax.sharding import PartitionSpec as P

absent_score = -1e30
LANES = 128
F32 = jnp.float32
BF16 = jnp.bfloat16
VMEM = pl.BlockSpec(memory_space=pltpu.VMEM)
SMEM = pl.BlockSpec(memory_space=pltpu.SMEM)
HBM = pl.BlockSpec(memory_space=pltpu.HBM)
ANY = pl.BlockSpec(memory_space=pl.ANY)
PARAMS = pltpu.CompilerParams(vmem_limit_bytes=16 * 1024 * 1024)
WHOLE = pltpu.CompilerParams(vmem_limit_bytes=62 * 1024 * 1024)


COST = pl.CostEstimate(flops=1000, bytes_accessed=1000, transcendentals=0)


def stage_kernel(
    devices, group, first, dest_hbm, k_ref, v_ref, buf, buf_rest, table, k_vm, v_vm, dest, counts, sem, load_sem
):
    rows, heads = k_ref.shape[:2]
    small = pltpu.make_async_copy(dest_hbm, dest, sem.at[0])
    small.start()
    loads = []
    for row in range(rows):
        for which, (src, dst) in enumerate(((k_ref, k_vm), (v_ref, v_vm))):
            copy = pltpu.make_async_copy(src.at[row], dst.at[row], load_sem.at[which, row])
            copy.start()
            loads.append(copy)
    me = lax.axis_index("ctx")

    def clear(i, carry):
        counts[i] = 0
        for k in range(group):
            table[i * group + k] = -1
        return carry

    lax.fori_loop(0, devices, clear, 0)
    small.wait()
    for row in range(rows):
        loads[2 * row].wait()
        loads[2 * row + 1].wait()

        def send(head, carry):
            offset = dest[row, head, 0]
            rank = counts[offset]
            counts[offset] = rank + 1
            table[offset * group + rank] = row * heads + head
            target = jnp.bitwise_and(me + offset, devices - 1)
            pltpu.make_async_copy(k_vm.at[row, head], buf.at[target * first + rank], sem.at[1]).start()

            @pl.when(rank < first - group)
            def _():
                at = target * first + group + rank
                pltpu.make_async_copy(v_vm.at[row, head], buf.at[at], sem.at[2]).start()

            @pl.when(rank >= first - group)
            def _():
                at = target * (2 * group - first) + rank + group - first
                pltpu.make_async_copy(v_vm.at[row, head], buf_rest.at[at], sem.at[2]).start()
            return carry

        lax.fori_loop(0, heads, send, 0)
    pltpu.make_async_copy(k_ref, k_vm, sem.at[1]).wait()
    pltpu.make_async_copy(v_ref, v_vm, sem.at[2]).wait()


def attend_kernel(
    levels,
    table, len_hbm, kept_hbm, q_ref, k_ref, v_ref,
    stats_ref, *rest,
):
    chunks = rest[:levels // 2]
    len_ref, kept_ref, small_sem = rest[levels // 2:]
    rows, heads, tile, width = k_ref.shape
    steps, _, q_heads, _ = q_ref.shape
    per = q_heads // heads
    me = lax.axis_index("ctx")

    small = [
        pltpu.make_async_copy(len_hbm, len_ref, small_sem.at[0]),
        pltpu.make_async_copy(kept_hbm, kept_ref, small_sem.at[1]),
    ]
    for copy in small:
        copy.start()
    for copy in small:
        copy.wait()

    lane = lax.broadcasted_iota(jnp.int32, (per, tile), 1)
    pair_lane = lax.broadcasted_iota(jnp.int32, (steps * per, LANES), 1)
    peaks = jnp.full((steps * per, LANES), absent_score, F32)
    totals = jnp.zeros((steps * per, LANES), F32)
    order = [jnp.bitwise_xor(place_of(me), level) for level in range(levels)]
    scale = width ** -0.5
    block = steps * per
    for row in range(rows):
        queries = [q_ref[step, row].astype(F32) for step in order]
        live = []
        for step in order:
            limit = jnp.where(kept_ref[row, step, me] > 0, len_ref[row] - me * tile, 0)
            live.append(lane < limit)
        live = jnp.concatenate(live * heads, axis=0)
        scores = []
        for head in range(heads):
            q = jnp.concatenate([x[head * per:(head + 1) * per] for x in queries], axis=0).astype(BF16)
            scores.append(lax.dot_general(
                q, k_ref[row, head], (((1,), (1,)), ((), ())), preferred_element_type=F32
            ))
        scores = jnp.concatenate(scores, axis=0) * scale
        peak = jnp.max(jnp.where(live, scores, absent_score), axis=1, keepdims=True)
        weights = jnp.where(live, jnp.exp(scores - peak), 0.0)
        total = jnp.sum(weights, axis=1, keepdims=True)
        rounded = weights.astype(BF16)
        for head in range(heads):
            out = jnp.dot(
                rounded[head * block:(head + 1) * block], v_ref[row, head], preferred_element_type=F32
            )
            pair = row * heads + head
            for i in range(levels):
                chunks[i // 2][i % 2, pair * per:(pair + 1) * per, :] = out[i * per:(i + 1) * per]
            here = pair_lane == pair
            peaks = jnp.where(here, peak[head * block:(head + 1) * block], peaks)
            totals = jnp.where(here, total[head * block:(head + 1) * block], totals)
    base = rows * q_heads
    for i in range(levels):
        chunks[i // 2][i % 2, base:base + per, :] = peaks[i * per:(i + 1) * per]
        chunks[i // 2][i % 2, base + per:base + 2 * per, :] = totals[i * per:(i + 1) * per]
    stats_ref[0] = peaks
    stats_ref[1] = totals


def place_of(me):
    return lax.rem(me, 2) * 2 + lax.rem(me // 2, 2)


def merge(swap, own, got, pairs, per, own_stats=None, got_stats=None):
    def both(rows, own=own, got=got):
        x, y = own[rows, :], got[rows, :]
        return jnp.where(swap, y, x), jnp.where(swap, x, y)

    scaled = own_stats is not None
    base = 0 if scaled else pairs * per
    stats = (own_stats, got_stats) if scaled else (own, got)
    peaks = both(slice(base, base + per), *stats)
    totals = both(slice(base + per, base + 2 * per), *stats)
    peak = jnp.maximum(*peaks)
    factors = [jnp.exp(x - peak) for x in peaks]
    total = factors[0] * totals[0] + factors[1] * totals[1]
    if scaled:
        scales = both(slice(2 * per, 3 * per), *stats)
        factors = [f * x for f, x in zip(factors, scales)]

    def summed(pair):
        first, second = [jnp.broadcast_to(f[:, pair:pair + 1], (per, LANES)) for f in factors]
        x, y = both(slice(pair * per, (pair + 1) * per))
        return first * x + second * y

    return peak, total, summed


def merge_kernel(bit, pairs, per, own, got, *outs):
    swap = lax.rem(lax.axis_index("ctx") // bit, 2) == 1
    base = pairs * per
    for i, out in enumerate(outs):
        x, y = (own, got) if len(outs) == 1 else (own.at[i], got.at[i])
        peak, total, summed = merge(swap, x, y, pairs, per)
        for pair in range(pairs):
            out[pair * per:(pair + 1) * per, :] = summed(pair)
        out[base:base + per, :] = peak
        out[base + per:base + 2 * per, :] = total


def halve_kernel(bit, pairs, per, own, got, kept, sent, work):
    index = lax.axis_index("ctx")
    peak, total, summed = merge(lax.rem(index // bit, 2) == 1, own, got, pairs, per)
    share = pairs // 2
    base = share * per
    for half in range(2):
        for i in range(share):
            work[half, i * per:(i + 1) * per, :] = summed(half * share + i)
        for i, x in enumerate((peak, total)):
            at = base + i * per
            work[half, at:at + per, :] = pltpu.roll(x, LANES - share, 1) if half else x
    mine = lax.rem(index // (2 * bit), 2)
    kept[...] = work[mine]
    sent[...] = work[1 - mine]


def scale_kernel(pairs, per, block, sums, stats):
    lane = lax.broadcasted_iota(jnp.int32, (per, LANES), 1)
    base = pairs * per
    scales = jnp.ones((per, LANES), F32)
    for pair in range(pairs):
        x = block[pair * per:(pair + 1) * per, :]
        largest = jnp.max(jnp.abs(x), axis=1, keepdims=True)
        largest = jnp.where(largest > 0.0, largest, 1.0)
        sums[pair * per:(pair + 1) * per, :] = x / largest
        scales = jnp.where(lane == pair, largest, scales)
    stats[:2 * per, :] = block[base:base + 2 * per, :]
    stats[2 * per:, :] = scales


def last_kernel(bit, pairs, per, own, got, own_stats, got_stats, out):
    swap = lax.rem(lax.axis_index("ctx") // bit, 2) == 1
    base = pairs * per
    peak, total, summed = merge(swap, own, got, pairs, per, own_stats, got_stats)
    lane = lax.broadcasted_iota(jnp.int32, peak.shape, 1)
    total = jnp.where(lane < pairs, total, 1.0)
    peak = jnp.where(lane < pairs, peak, 0.0)

    def result(pair):
        return summed(pair) / jnp.broadcast_to(total[:, pair:pair + 1], (per, LANES))

    for pair in range(0, pairs, 2):
        both = jnp.concatenate([result(pair), result(pair + 1)], axis=0)
        out[pair * per:(pair + 2) * per, :] = both.astype(BF16)
    rest = jnp.concatenate([peak, total], axis=0)
    lane = lax.broadcasted_iota(jnp.int32, rest.shape, 1)
    parts = []
    for i in range(3):
        parts.append(rest.astype(BF16).astype(F32))
        rest = rest - parts[i]
    half = LANES // 2
    packed = jnp.where(lane < half, parts[0], pltpu.roll(parts[1], half, 1))
    out[base:base + 2 * per, :] = packed.astype(BF16)
    out[base + 2 * per:base + 4 * per, :] = parts[2].astype(BF16)


def finish_kernel(pairs, per, heads, levels, stats_ref, *refs):
    ins, (out, mass_ref, mass_vm, sem) = refs[:2 * levels], refs[2 * levels:]
    me = lax.axis_index("ctx")
    share = pairs // 2
    base = share * per
    mine = lax.rem(me // levels, 2)
    copies = []
    for level in range(levels):
        for far in range(2):
            step, half = jnp.bitwise_xor(place_of(me), level), jnp.bitwise_xor(mine, far)
            i = 2 * level + far
            copies.append(pltpu.make_async_copy(ins[i].at[:base], out.at[step, half], sem.at[i]))
            copies[i].start()
    lane = lax.broadcasted_iota(jnp.int32, (2 * per, LANES), 1)
    masses = [jnp.zeros((per, LANES), F32)] * 2
    for level in range(levels):
        rows = slice(level * per, (level + 1) * per)
        own_peak, own_total = stats_ref[0, rows, :], stats_ref[1, rows, :]
        for far in range(2):
            message = ins[2 * level + far]
            packed = message[base:base + 2 * per, :].astype(F32)
            third = message[base + 2 * per:base + 4 * per, :].astype(F32)
            both = third + pltpu.roll(packed, LANES // 2, 1) + packed
            both = jnp.where(lane < share, both, 1.0)
            second = jnp.bitwise_xor(mine, far) == 1
            peak, total = [
                jnp.where(second, pltpu.roll(x, LANES - share, 1), x) for x in (own_peak, own_total)
            ]
            mass = total * (jnp.exp(jnp.minimum(peak - both[:per], 0.0)) / both[per:])
            masses = [masses[0] + jnp.where(second, 0.0, mass), masses[1] + jnp.where(second, mass, 0.0)]
    for half in range(2):
        mass = jnp.sum(masses[half], axis=0, keepdims=True)
        for i in range(share // heads):
            mass_vm[half * (share // heads) + i] = mass[:, i * heads:(i + 1) * heads]
    copies.append(pltpu.make_async_copy(mass_vm, mass_ref, sem.at[2 * levels]))
    copies[-1].start()
    for copy in copies:
        copy.wait()


def place_keys_kernel(devices, group, first, table, got, out, sem):
    heads = out.shape[1]
    me = lax.axis_index("ctx")
    for offset in range(devices):
        source = jnp.bitwise_and(me + devices - offset, devices - 1)
        for k in range(group):
            put(got.at[source * first + k], table[offset * group + k], heads, out, sem)
    pltpu.make_async_copy(out, out, sem).wait()


def place_values_kernel(devices, group, first, table, got, got_rest, out, sem):
    heads = out.shape[1]
    me = lax.axis_index("ctx")
    rest = 2 * group - first
    for offset in range(devices):
        source = jnp.bitwise_and(me + devices - offset, devices - 1)
        for k in range(group):
            at = group + k
            src = got.at[source * first + at] if at < first else got_rest.at[source * rest + at - first]
            put(src, table[offset * group + k], heads, out, sem)
    pltpu.make_async_copy(out, out, sem).wait()


def put(src, pair, heads, out, sem):
    @pl.when(pair >= 0)
    def _():
        pltpu.make_async_copy(src, out.at[pair // heads, lax.rem(pair, heads)], sem).start()


def local(queries, key_cache, value_cache, row_lengths, kept_tiles, tile_dest):
    devices = lax.axis_size("ctx")
    rows, heads, span, width = key_cache.shape
    steps, _, q_heads, _ = queries.shape
    per = q_heads // heads
    pairs = rows * heads
    group = -(-pairs // devices)
    levels = 4
    assert steps == levels and tile_dest.shape[2] == devices and pairs % 2 == 0 and pairs <= LANES // 2
    assert devices > 2 * levels and devices & (devices - 1) == 0 and width == LANES
    assert pairs % (2 * heads) == 0
    share = pairs // 2

    kept = jnp.transpose(kept_tiles, (1, 0, 2))
    block_rows = rows * q_heads + 2 * per
    block_type = jax.ShapeDtypeStruct((block_rows, width), F32)
    half_type = jax.ShapeDtypeStruct((share * per + 2 * per, width), F32)
    message_type = jax.ShapeDtypeStruct((share * per + 4 * per, width), BF16)
    first = 2 * group - max(1, 2 * group // 3)

    def tiles_type(count):
        return jax.ShapeDtypeStruct((devices * count, span, width), BF16)

    def exchange(x):
        return lax.all_to_all(x, "ctx", split_axis=0, concat_axis=0, tiled=True)


    tiles_out, rest_out, table = pl.pallas_call(
        functools.partial(stage_kernel, devices, group, first),
        out_shape=[
            tiles_type(first), tiles_type(2 * group - first),
            jax.ShapeDtypeStruct((devices * group,), jnp.int32),
        ],
        in_specs=[HBM, HBM, HBM],
        out_specs=[HBM, HBM, SMEM],
        scratch_shapes=[
            pltpu.VMEM(key_cache.shape, BF16),
            pltpu.VMEM(value_cache.shape, BF16),
            pltpu.SMEM(tile_dest.shape, jnp.int32),
            pltpu.SMEM((devices,), jnp.int32),
            pltpu.SemaphoreType.DMA((3,)),
            pltpu.SemaphoreType.DMA((2, rows)),
        ],
        compiler_params=WHOLE,
        cost_estimate=COST,
        name="stage",
    )(tile_dest, key_cache, value_cache)
    tiles_in = exchange(tiles_out)

    stats, *chunks = pl.pallas_call(
        functools.partial(attend_kernel, levels),
        out_shape=[
            jax.ShapeDtypeStruct((2, steps * per, LANES), F32),
        ] + [jax.ShapeDtypeStruct((2, block_rows, width), F32)] * 2,
        in_specs=[SMEM, HBM, HBM, VMEM, VMEM, VMEM],
        out_specs=[VMEM] * 3,
        scratch_shapes=[
            pltpu.SMEM(row_lengths.shape, jnp.int32),
            pltpu.SMEM(kept.shape, jnp.int32),
            pltpu.SemaphoreType.DMA((2,)),
        ],
        compiler_params=PARAMS,
        cost_estimate=COST,
        name="attend",
    )(table, row_lengths, kept, queries, key_cache, value_cache)

    def flip(x, bit):
        return lax.ppermute(x, "ctx", [(i, i ^ bit) for i in range(devices)])

    def local_call(kernel, name, out_shape, *operands, scratch=()):
        return pl.pallas_call(
            kernel,
            out_shape=out_shape,
            in_specs=[VMEM] * len(operands),
            out_specs=[VMEM] * len(out_shape),
            scratch_shapes=scratch,
            compiler_params=PARAMS,
            cost_estimate=COST,
            name=name,
        )(*operands)

    block, sent = local_call(
        functools.partial(merge_kernel, 1, pairs, per), "core", [block_type] * 2, chunks[0], flip(chunks[1], 1)
    )
    block, sent = local_call(
        functools.partial(halve_kernel, 2, pairs, per), "near", [half_type] * 2, block, flip(sent, 2),
        scratch=[pltpu.VMEM((2,) + half_type.shape, F32)],
    )
    bit, got = levels, flip(sent, levels)
    while True:
        block, = local_call(functools.partial(merge_kernel, bit, share, per), "far", [half_type], block, got)
        bit *= 2
        if 2 * bit == devices:
            break
        got = flip(block, bit)
    sums_type = jax.ShapeDtypeStruct((share * per, width), F32)
    stats_type = jax.ShapeDtypeStruct((3 * per, width), F32)
    sums, sum_stats = local_call(functools.partial(scale_kernel, share, per), "scale", [sums_type, stats_type], block)
    sums = lax.reduce_precision(sums, 5, 10)
    got = flip(sums.astype(jnp.float16), bit).astype(F32)
    got, got_stats, rest_out = lax.optimization_barrier((got, flip(sum_stats, bit), rest_out))
    rest_in = exchange(rest_out)
    message, = local_call(
        functools.partial(last_kernel, bit, share, per), "last", [message_type], sums, got, sum_stats, got_stats,
    )
    near = [message, flip(message, levels), flip(message, 2), flip(message, 2 + levels)]

    def place(kernel, name, *got):
        return pl.pallas_call(
            functools.partial(kernel, devices, group, first),
            out_shape=jax.ShapeDtypeStruct(key_cache.shape, BF16),
            in_specs=[SMEM] + [ANY] * len(got),
            out_specs=HBM,
            scratch_shapes=[pltpu.SemaphoreType.DMA],
            compiler_params=PARAMS,
            cost_estimate=COST,
            name=name,
        )(table, *got)

    moved_keys = place(place_keys_kernel, "place_keys", tiles_in)
    moved_values = place(place_values_kernel, "place_values", tiles_in, rest_in)
    *forward, moved_keys = lax.optimization_barrier((*near[1:], moved_keys))
    near = [message, *forward]
    arrived = near + [flip(x, 1) for x in near]

    attn_out, mass = pl.pallas_call(
        functools.partial(finish_kernel, pairs, per, heads, levels),
        out_shape=[
            jax.ShapeDtypeStruct((steps, 2, share * per, width), BF16),
            jax.ShapeDtypeStruct((rows, 1, heads), F32),
        ],
        in_specs=[VMEM] * (1 + 2 * levels),
        out_specs=[HBM, HBM],
        scratch_shapes=[pltpu.VMEM((rows, 1, heads), F32), pltpu.SemaphoreType.DMA((2 * levels + 1,))],
        compiler_params=PARAMS,
        cost_estimate=COST,
        name="finish",
    )(stats, *arrived)
    return attn_out.reshape(queries.shape), jnp.transpose(mass, (0, 2, 1)), moved_keys, moved_values


def solution(mesh):
    in_specs = (
        P(None, "grp", None, None),
        P("grp", None, "ctx", None),
        P("grp", None, "ctx", None),
        P("grp"),
        P(None, "grp", None),
        P("grp", None, None),
    )
    out_specs = (
        P(None, "grp", None, None),
        P("grp", None, "ctx"),
        P("grp", None, "ctx", None),
        P("grp", None, "ctx", None),
    )
    return jax.shard_map(local, mesh=mesh, in_specs=in_specs, out_specs=out_specs, check_vma=False)
```

```python
import functools

import jax
import jax.numpy as jnp
from jax import lax
from jax.experimental import pallas as pl
from jax.experimental.pallas import tpu as pltpu
from jax.sharding import PartitionSpec as P

absent_score = -1e30
LANES = 128
F32 = jnp.float32
BF16 = jnp.bfloat16
VMEM = pl.BlockSpec(memory_space=pltpu.VMEM)
SMEM = pl.BlockSpec(memory_space=pltpu.SMEM)
HBM = pl.BlockSpec(memory_space=pltpu.HBM)
ANY = pl.BlockSpec(memory_space=pl.ANY)
PARAMS = pltpu.CompilerParams(vmem_limit_bytes=16 * 1024 * 1024)
WHOLE = pltpu.CompilerParams(vmem_limit_bytes=62 * 1024 * 1024)


COST = pl.CostEstimate(flops=1000, bytes_accessed=1000, transcendentals=0)


def stage_kernel(
    devices, group, first, dest_hbm, k_ref, v_ref, buf, buf_rest, table, k_vm, v_vm, dest, counts, sem, load_sem
):
    rows, heads = k_ref.shape[:2]
    small = pltpu.make_async_copy(dest_hbm, dest, sem.at[0])
    small.start()
    loads = []
    for row in range(rows):
        for which, (src, dst) in enumerate(((k_ref, k_vm), (v_ref, v_vm))):
            copy = pltpu.make_async_copy(src.at[row], dst.at[row], load_sem.at[which, row])
            copy.start()
            loads.append(copy)
    me = lax.axis_index("ctx")

    def clear(i, carry):
        counts[i] = 0
        for k in range(group):
            table[i * group + k] = -1
        return carry

    lax.fori_loop(0, devices, clear, 0)
    small.wait()
    for row in range(rows):
        loads[2 * row].wait()
        loads[2 * row + 1].wait()

        def send(head, carry):
            offset = dest[row, head, 0]
            rank = counts[offset]
            counts[offset] = rank + 1
            table[offset * group + rank] = row * heads + head
            target = jnp.bitwise_and(me + offset, devices - 1)
            pltpu.make_async_copy(k_vm.at[row, head], buf.at[target * first + rank], sem.at[1]).start()

            @pl.when(rank < first - group)
            def _():
                at = target * first + group + rank
                pltpu.make_async_copy(v_vm.at[row, head], buf.at[at], sem.at[2]).start()

            @pl.when(rank >= first - group)
            def _():
                at = target * (2 * group - first) + rank + group - first
                pltpu.make_async_copy(v_vm.at[row, head], buf_rest.at[at], sem.at[2]).start()
            return carry

        lax.fori_loop(0, heads, send, 0)
    pltpu.make_async_copy(k_ref, k_vm, sem.at[1]).wait()
    pltpu.make_async_copy(v_ref, v_vm, sem.at[2]).wait()


def attend_kernel(
    levels,
    table, len_hbm, kept_hbm, q_ref, k_ref, v_ref,
    stats_ref, *rest,
):
    chunks = rest[:levels // 2]
    len_ref, kept_ref, small_sem = rest[levels // 2:]
    rows, heads, tile, width = k_ref.shape
    steps, _, q_heads, _ = q_ref.shape
    per = q_heads // heads
    me = lax.axis_index("ctx")

    small = [
        pltpu.make_async_copy(len_hbm, len_ref, small_sem.at[0]),
        pltpu.make_async_copy(kept_hbm, kept_ref, small_sem.at[1]),
    ]
    for copy in small:
        copy.start()
    for copy in small:
        copy.wait()

    lane = lax.broadcasted_iota(jnp.int32, (per, tile), 1)
    pair_lane = lax.broadcasted_iota(jnp.int32, (steps * per, LANES), 1)
    peaks = jnp.full((steps * per, LANES), absent_score, F32)
    totals = jnp.zeros((steps * per, LANES), F32)
    order = [jnp.bitwise_xor(place_of(me), level) for level in range(levels)]
    scale = width ** -0.5
    block = steps * per
    for row in range(rows):
        queries = [q_ref[step, row].astype(F32) for step in order]
        live = []
        for step in order:
            limit = jnp.where(kept_ref[row, step, me] > 0, len_ref[row] - me * tile, 0)
            live.append(lane < limit)
        live = jnp.concatenate(live * heads, axis=0)
        scores = []
        for head in range(heads):
            q = jnp.concatenate([x[head * per:(head + 1) * per] for x in queries], axis=0).astype(BF16)
            scores.append(lax.dot_general(
                q, k_ref[row, head], (((1,), (1,)), ((), ())), preferred_element_type=F32
            ))
        scores = jnp.concatenate(scores, axis=0) * scale
        peak = jnp.max(jnp.where(live, scores, absent_score), axis=1, keepdims=True)
        weights = jnp.where(live, jnp.exp(scores - peak), 0.0)
        total = jnp.sum(weights, axis=1, keepdims=True)
        rounded = weights.astype(BF16)
        for head in range(heads):
            out = jnp.dot(
                rounded[head * block:(head + 1) * block], v_ref[row, head], preferred_element_type=F32
            )
            pair = row * heads + head
            for i in range(levels):
                chunks[i // 2][i % 2, pair * per:(pair + 1) * per, :] = out[i * per:(i + 1) * per]
            here = pair_lane == pair
            peaks = jnp.where(here, peak[head * block:(head + 1) * block], peaks)
            totals = jnp.where(here, total[head * block:(head + 1) * block], totals)
    base = rows * q_heads
    for i in range(levels):
        chunks[i // 2][i % 2, base:base + per, :] = peaks[i * per:(i + 1) * per]
        chunks[i // 2][i % 2, base + per:base + 2 * per, :] = totals[i * per:(i + 1) * per]
    stats_ref[0] = peaks
    stats_ref[1] = totals


def place_of(me):
    return lax.rem(me, 2) * 2 + lax.rem(me // 2, 2)


def merge(swap, own, got, pairs, per, own_stats=None, got_stats=None):
    def both(rows, own=own, got=got):
        x, y = own[rows, :], got[rows, :]
        return jnp.where(swap, y, x), jnp.where(swap, x, y)

    scaled = own_stats is not None
    base = 0 if scaled else pairs * per
    stats = (own_stats, got_stats) if scaled else (own, got)
    peaks = both(slice(base, base + per), *stats)
    totals = both(slice(base + per, base + 2 * per), *stats)
    peak = jnp.maximum(*peaks)
    factors = [jnp.exp(x - peak) for x in peaks]
    total = factors[0] * totals[0] + factors[1] * totals[1]
    if scaled:
        scales = both(slice(2 * per, 3 * per), *stats)
        factors = [f * x for f, x in zip(factors, scales)]

    def summed(pair):
        first, second = [jnp.broadcast_to(f[:, pair:pair + 1], (per, LANES)) for f in factors]
        x, y = both(slice(pair * per, (pair + 1) * per))
        return first * x + second * y

    return peak, total, summed


def merge_kernel(bit, pairs, per, own, got, *outs):
    swap = lax.rem(lax.axis_index("ctx") // bit, 2) == 1
    base = pairs * per
    for i, out in enumerate(outs):
        x, y = (own, got) if len(outs) == 1 else (own.at[i], got.at[i])
        peak, total, summed = merge(swap, x, y, pairs, per)
        for pair in range(pairs):
            out[pair * per:(pair + 1) * per, :] = summed(pair)
        out[base:base + per, :] = peak
        out[base + per:base + 2 * per, :] = total


def halve_kernel(bit, pairs, per, own, got, kept, sent, work):
    index = lax.axis_index("ctx")
    peak, total, summed = merge(lax.rem(index // bit, 2) == 1, own, got, pairs, per)
    share = pairs // 2
    base = share * per
    for half in range(2):
        for i in range(share):
            work[half, i * per:(i + 1) * per, :] = summed(half * share + i)
        for i, x in enumerate((peak, total)):
            at = base + i * per
            work[half, at:at + per, :] = pltpu.roll(x, LANES - share, 1) if half else x
    mine = lax.rem(index // (2 * bit), 2)
    kept[...] = work[mine]
    sent[...] = work[1 - mine]


def scale_kernel(pairs, per, block, sums, stats):
    lane = lax.broadcasted_iota(jnp.int32, (per, LANES), 1)
    base = pairs * per
    scales = jnp.ones((per, LANES), F32)
    for pair in range(pairs):
        x = block[pair * per:(pair + 1) * per, :]
        largest = jnp.max(jnp.abs(x), axis=1, keepdims=True)
        largest = jnp.where(largest > 0.0, largest, 1.0)
        sums[pair * per:(pair + 1) * per, :] = x / largest
        scales = jnp.where(lane == pair, largest, scales)
    stats[:2 * per, :] = block[base:base + 2 * per, :]
    stats[2 * per:, :] = scales


def last_kernel(bit, pairs, per, own, got, own_stats, got_stats, out):
    swap = lax.rem(lax.axis_index("ctx") // bit, 2) == 1
    base = pairs * per
    peak, total, summed = merge(swap, own, got, pairs, per, own_stats, got_stats)
    lane = lax.broadcasted_iota(jnp.int32, peak.shape, 1)
    total = jnp.where(lane < pairs, total, 1.0)
    peak = jnp.where(lane < pairs, peak, 0.0)

    def result(pair):
        return summed(pair) / jnp.broadcast_to(total[:, pair:pair + 1], (per, LANES))

    for pair in range(0, pairs, 2):
        both = jnp.concatenate([result(pair), result(pair + 1)], axis=0)
        out[pair * per:(pair + 2) * per, :] = both.astype(BF16)
    rest = jnp.concatenate([peak, total], axis=0)
    lane = lax.broadcasted_iota(jnp.int32, rest.shape, 1)
    parts = []
    for i in range(3):
        parts.append(rest.astype(BF16).astype(F32))
        rest = rest - parts[i]
    half = LANES // 2
    packed = jnp.where(lane < half, parts[0], pltpu.roll(parts[1], half, 1))
    out[base:base + 2 * per, :] = packed.astype(BF16)
    out[base + 2 * per:base + 4 * per, :] = parts[2].astype(BF16)


def finish_kernel(pairs, per, heads, levels, stats_ref, *refs):
    ins, (out, mass_ref, mass_vm, sem) = refs[:2 * levels], refs[2 * levels:]
    me = lax.axis_index("ctx")
    share = pairs // 2
    base = share * per
    mine = lax.rem(me // levels, 2)
    copies = []
    for level in range(levels):
        for far in range(2):
            step, half = jnp.bitwise_xor(place_of(me), level), jnp.bitwise_xor(mine, far)
            i = 2 * level + far
            copies.append(pltpu.make_async_copy(ins[i].at[:base], out.at[step, half], sem.at[i]))
            copies[i].start()
    lane = lax.broadcasted_iota(jnp.int32, (2 * per, LANES), 1)
    masses = [jnp.zeros((per, LANES), F32)] * 2
    for level in range(levels):
        rows = slice(level * per, (level + 1) * per)
        own_peak, own_total = stats_ref[0, rows, :], stats_ref[1, rows, :]
        for far in range(2):
            message = ins[2 * level + far]
            packed = message[base:base + 2 * per, :].astype(F32)
            third = message[base + 2 * per:base + 4 * per, :].astype(F32)
            both = third + pltpu.roll(packed, LANES // 2, 1) + packed
            both = jnp.where(lane < share, both, 1.0)
            second = jnp.bitwise_xor(mine, far) == 1
            peak, total = [
                jnp.where(second, pltpu.roll(x, LANES - share, 1), x) for x in (own_peak, own_total)
            ]
            mass = total * (jnp.exp(jnp.minimum(peak - both[:per], 0.0)) / both[per:])
            masses = [masses[0] + jnp.where(second, 0.0, mass), masses[1] + jnp.where(second, mass, 0.0)]
    for half in range(2):
        mass = jnp.sum(masses[half], axis=0, keepdims=True)
        for i in range(share // heads):
            mass_vm[half * (share // heads) + i] = mass[:, i * heads:(i + 1) * heads]
    copies.append(pltpu.make_async_copy(mass_vm, mass_ref, sem.at[2 * levels]))
    copies[-1].start()
    for copy in copies:
        copy.wait()


def place_keys_kernel(devices, group, first, table, got, out, sem):
    heads = out.shape[1]
    me = lax.axis_index("ctx")
    for offset in range(devices):
        source = jnp.bitwise_and(me + devices - offset, devices - 1)
        for k in range(group):
            put(got.at[source * first + k], table[offset * group + k], heads, out, sem)
    pltpu.make_async_copy(out, out, sem).wait()


def place_values_kernel(devices, group, first, table, got, got_rest, out, sem):
    heads = out.shape[1]
    me = lax.axis_index("ctx")
    rest = 2 * group - first
    for offset in range(devices):
        source = jnp.bitwise_and(me + devices - offset, devices - 1)
        for k in range(group):
            at = group + k
            src = got.at[source * first + at] if at < first else got_rest.at[source * rest + at - first]
            put(src, table[offset * group + k], heads, out, sem)
    pltpu.make_async_copy(out, out, sem).wait()


def put(src, pair, heads, out, sem):
    @pl.when(pair >= 0)
    def _():
        pltpu.make_async_copy(src, out.at[pair // heads, lax.rem(pair, heads)], sem).start()


def local(queries, key_cache, value_cache, row_lengths, kept_tiles, tile_dest):
    devices = lax.axis_size("ctx")
    rows, heads, span, width = key_cache.shape
    steps, _, q_heads, _ = queries.shape
    per = q_heads // heads
    pairs = rows * heads
    group = -(-pairs // devices)
    levels = 4
    assert steps == levels and tile_dest.shape[2] == devices and pairs % 2 == 0 and pairs <= LANES // 2
    assert devices > 2 * levels and devices & (devices - 1) == 0 and width == LANES
    assert pairs % (2 * heads) == 0
    share = pairs // 2

    kept = jnp.transpose(kept_tiles, (1, 0, 2))
    block_rows = rows * q_heads + 2 * per
    block_type = jax.ShapeDtypeStruct((block_rows, width), F32)
    half_type = jax.ShapeDtypeStruct((share * per + 2 * per, width), F32)
    message_type = jax.ShapeDtypeStruct((share * per + 4 * per, width), BF16)
    first = 2 * group - max(1, 2 * group // 3)

    def tiles_type(count):
        return jax.ShapeDtypeStruct((devices * count, span, width), BF16)

    def exchange(x):
        return lax.all_to_all(x, "ctx", split_axis=0, concat_axis=0, tiled=True)


    tiles_out, rest_out, table = pl.pallas_call(
        functools.partial(stage_kernel, devices, group, first),
        out_shape=[
            tiles_type(first), tiles_type(2 * group - first),
            jax.ShapeDtypeStruct((devices * group,), jnp.int32),
        ],
        in_specs=[HBM, HBM, HBM],
        out_specs=[HBM, HBM, SMEM],
        scratch_shapes=[
            pltpu.VMEM(key_cache.shape, BF16),
            pltpu.VMEM(value_cache.shape, BF16),
            pltpu.SMEM(tile_dest.shape, jnp.int32),
            pltpu.SMEM((devices,), jnp.int32),
            pltpu.SemaphoreType.DMA((3,)),
            pltpu.SemaphoreType.DMA((2, rows)),
        ],
        compiler_params=WHOLE,
        cost_estimate=COST,
        name="stage",
    )(tile_dest, key_cache, value_cache)
    tiles_in = exchange(tiles_out)

    stats, *chunks = pl.pallas_call(
        functools.partial(attend_kernel, levels),
        out_shape=[
            jax.ShapeDtypeStruct((2, steps * per, LANES), F32),
        ] + [jax.ShapeDtypeStruct((2, block_rows, width), F32)] * 2,
        in_specs=[SMEM, HBM, HBM, VMEM, VMEM, VMEM],
        out_specs=[VMEM] * 3,
        scratch_shapes=[
            pltpu.SMEM(row_lengths.shape, jnp.int32),
            pltpu.SMEM(kept.shape, jnp.int32),
            pltpu.SemaphoreType.DMA((2,)),
        ],
        compiler_params=PARAMS,
        cost_estimate=COST,
        name="attend",
    )(table, row_lengths, kept, queries, key_cache, value_cache)

    def flip(x, bit):
        return lax.ppermute(x, "ctx", [(i, i ^ bit) for i in range(devices)])

    def local_call(kernel, name, out_shape, *operands, scratch=()):
        return pl.pallas_call(
            kernel,
            out_shape=out_shape,
            in_specs=[VMEM] * len(operands),
            out_specs=[VMEM] * len(out_shape),
            scratch_shapes=scratch,
            compiler_params=PARAMS,
            cost_estimate=COST,
            name=name,
        )(*operands)

    block, sent = local_call(
        functools.partial(merge_kernel, 1, pairs, per), "core", [block_type] * 2, chunks[0], flip(chunks[1], 1)
    )
    block, sent = local_call(
        functools.partial(halve_kernel, 2, pairs, per), "near", [half_type] * 2, block, flip(sent, 2),
        scratch=[pltpu.VMEM((2,) + half_type.shape, F32)],
    )
    bit, got = levels, flip(sent, levels)
    while True:
        block, = local_call(functools.partial(merge_kernel, bit, share, per), "far", [half_type], block, got)
        bit *= 2
        if 2 * bit == devices:
            break
        got = flip(block, bit)
    sums_type = jax.ShapeDtypeStruct((share * per, width), F32)
    stats_type = jax.ShapeDtypeStruct((3 * per, width), F32)
    sums, sum_stats = local_call(functools.partial(scale_kernel, share, per), "scale", [sums_type, stats_type], block)
    sums = lax.reduce_precision(sums, 5, 10)
    got = flip(sums.astype(jnp.float16), bit).astype(F32)
    got, got_stats, rest_out = lax.optimization_barrier((got, flip(sum_stats, bit), rest_out))
    rest_in = exchange(rest_out)
    message, = local_call(
        functools.partial(last_kernel, bit, share, per), "last", [message_type], sums, got, sum_stats, got_stats,
    )
    near = [message, flip(message, levels), flip(message, 2), flip(message, 2 + levels)]

    def place(kernel, name, *got):
        return pl.pallas_call(
            functools.partial(kernel, devices, group, first),
            out_shape=jax.ShapeDtypeStruct(key_cache.shape, BF16),
            in_specs=[SMEM] + [ANY] * len(got),
            out_specs=HBM,
            scratch_shapes=[pltpu.SemaphoreType.DMA],
            compiler_params=PARAMS,
            cost_estimate=COST,
            name=name,
        )(table, *got)

    moved_keys = place(place_keys_kernel, "place_keys", tiles_in)
    *forward, moved_keys = lax.optimization_barrier((*near[1:], moved_keys))
    near = [message, *forward]
    arrived = near + [flip(x, 1) for x in near]

    attn_out, mass = pl.pallas_call(
        functools.partial(finish_kernel, pairs, per, heads, levels),
        out_shape=[
            jax.ShapeDtypeStruct((steps, 2, share * per, width), BF16),
            jax.ShapeDtypeStruct((rows, 1, heads), F32),
        ],
        in_specs=[VMEM] * (1 + 2 * levels),
        out_specs=[HBM, HBM],
        scratch_shapes=[pltpu.VMEM((rows, 1, heads), F32), pltpu.SemaphoreType.DMA((2 * levels + 1,))],
        compiler_params=PARAMS,
        cost_estimate=COST,
        name="finish",
    )(stats, *arrived)
    rest_in, mass = lax.optimization_barrier((rest_in, mass))
    moved_values = place(place_values_kernel, "place_values", tiles_in, rest_in)
    return attn_out.reshape(queries.shape), jnp.transpose(mass, (0, 2, 1)), moved_keys, moved_values


def solution(mesh):
    in_specs = (
        P(None, "grp", None, None),
        P("grp", None, "ctx", None),
        P("grp", None, "ctx", None),
        P("grp"),
        P(None, "grp", None),
        P("grp", None, None),
    )
    out_specs = (
        P(None, "grp", None, None),
        P("grp", None, "ctx"),
        P("grp", None, "ctx", None),
        P("grp", None, "ctx", None),
    )
    return jax.shard_map(local, mesh=mesh, in_specs=in_specs, out_specs=out_specs, check_vma=False)
```

```python
import functools

import jax
import jax.numpy as jnp
from jax import lax
from jax.experimental import pallas as pl
from jax.experimental.pallas import tpu as pltpu
from jax.sharding import PartitionSpec as P

absent_score = -1e30
LANES = 128
F32 = jnp.float32
BF16 = jnp.bfloat16
VMEM = pl.BlockSpec(memory_space=pltpu.VMEM)
SMEM = pl.BlockSpec(memory_space=pltpu.SMEM)
HBM = pl.BlockSpec(memory_space=pltpu.HBM)
ANY = pl.BlockSpec(memory_space=pl.ANY)
PARAMS = pltpu.CompilerParams(vmem_limit_bytes=16 * 1024 * 1024)
WHOLE = pltpu.CompilerParams(vmem_limit_bytes=62 * 1024 * 1024)


COST = pl.CostEstimate(flops=1000, bytes_accessed=1000, transcendentals=0)


def stage_kernel(
    devices, group, first, dest_hbm, k_ref, v_ref, buf, buf_rest, table, k_vm, v_vm, dest, counts, sem, load_sem
):
    rows, heads = k_ref.shape[:2]
    small = pltpu.make_async_copy(dest_hbm, dest, sem.at[0])
    small.start()
    loads = []
    for row in range(rows):
        for which, (src, dst) in enumerate(((k_ref, k_vm), (v_ref, v_vm))):
            copy = pltpu.make_async_copy(src.at[row], dst.at[row], load_sem.at[which, row])
            copy.start()
            loads.append(copy)
    me = lax.axis_index("ctx")

    def clear(i, carry):
        counts[i] = 0
        for k in range(group):
            table[i * group + k] = -1
        return carry

    lax.fori_loop(0, devices, clear, 0)
    small.wait()
    for row in range(rows):
        loads[2 * row].wait()
        loads[2 * row + 1].wait()

        def send(head, carry):
            offset = dest[row, head, 0]
            rank = counts[offset]
            counts[offset] = rank + 1
            table[offset * group + rank] = row * heads + head
            target = jnp.bitwise_and(me + offset, devices - 1)
            pltpu.make_async_copy(k_vm.at[row, head], buf.at[target * first + rank], sem.at[1]).start()

            @pl.when(rank < first - group)
            def _():
                at = target * first + group + rank
                pltpu.make_async_copy(v_vm.at[row, head], buf.at[at], sem.at[2]).start()

            @pl.when(rank >= first - group)
            def _():
                at = target * (2 * group - first) + rank + group - first
                pltpu.make_async_copy(v_vm.at[row, head], buf_rest.at[at], sem.at[2]).start()
            return carry

        lax.fori_loop(0, heads, send, 0)
    pltpu.make_async_copy(k_ref, k_vm, sem.at[1]).wait()
    pltpu.make_async_copy(v_ref, v_vm, sem.at[2]).wait()


def attend_kernel(
    levels,
    table, len_hbm, kept_hbm, q_ref, k_ref, v_ref,
    stats_ref, *rest,
):
    chunks = rest[:levels // 2]
    len_ref, kept_ref, small_sem = rest[levels // 2:]
    rows, heads, tile, width = k_ref.shape
    steps, _, q_heads, _ = q_ref.shape
    per = q_heads // heads
    me = lax.axis_index("ctx")

    small = [
        pltpu.make_async_copy(len_hbm, len_ref, small_sem.at[0]),
        pltpu.make_async_copy(kept_hbm, kept_ref, small_sem.at[1]),
    ]
    for copy in small:
        copy.start()
    for copy in small:
        copy.wait()

    lane = lax.broadcasted_iota(jnp.int32, (per, tile), 1)
    pair_lane = lax.broadcasted_iota(jnp.int32, (steps * per, LANES), 1)
    peaks = jnp.full((steps * per, LANES), absent_score, F32)
    totals = jnp.zeros((steps * per, LANES), F32)
    order = [jnp.bitwise_xor(place_of(me), level) for level in range(levels)]
    scale = width ** -0.5
    block = steps * per
    for row in range(rows):
        queries = [q_ref[step, row].astype(F32) for step in order]
        live = []
        for step in order:
            limit = jnp.where(kept_ref[row, step, me] > 0, len_ref[row] - me * tile, 0)
            live.append(lane < limit)
        live = jnp.concatenate(live * heads, axis=0)
        scores = []
        for head in range(heads):
            q = jnp.concatenate([x[head * per:(head + 1) * per] for x in queries], axis=0).astype(BF16)
            scores.append(lax.dot_general(
                q, k_ref[row, head], (((1,), (1,)), ((), ())), preferred_element_type=F32
            ))
        scores = jnp.concatenate(scores, axis=0) * scale
        peak = jnp.max(jnp.where(live, scores, absent_score), axis=1, keepdims=True)
        weights = jnp.where(live, jnp.exp(scores - peak), 0.0)
        total = jnp.sum(weights, axis=1, keepdims=True)
        rounded = weights.astype(BF16)
        for head in range(heads):
            out = jnp.dot(
                rounded[head * block:(head + 1) * block], v_ref[row, head], preferred_element_type=F32
            )
            pair = row * heads + head
            for i in range(levels):
                chunks[i // 2][i % 2, pair * per:(pair + 1) * per, :] = out[i * per:(i + 1) * per]
            here = pair_lane == pair
            peaks = jnp.where(here, peak[head * block:(head + 1) * block], peaks)
            totals = jnp.where(here, total[head * block:(head + 1) * block], totals)
    base = rows * q_heads
    for i in range(levels):
        chunks[i // 2][i % 2, base:base + per, :] = peaks[i * per:(i + 1) * per]
        chunks[i // 2][i % 2, base + per:base + 2 * per, :] = totals[i * per:(i + 1) * per]
    stats_ref[0] = peaks
    stats_ref[1] = totals


def place_of(me):
    return lax.rem(me, 2) * 2 + lax.rem(me // 2, 2)


def merge(swap, own, got, pairs, per, own_stats=None, got_stats=None):
    def both(rows, own=own, got=got):
        x, y = own[rows, :], got[rows, :]
        return jnp.where(swap, y, x), jnp.where(swap, x, y)

    scaled = own_stats is not None
    base = 0 if scaled else pairs * per
    stats = (own_stats, got_stats) if scaled else (own, got)
    peaks = both(slice(base, base + per), *stats)
    totals = both(slice(base + per, base + 2 * per), *stats)
    peak = jnp.maximum(*peaks)
    factors = [jnp.exp(x - peak) for x in peaks]
    total = factors[0] * totals[0] + factors[1] * totals[1]
    if scaled:
        scales = both(slice(2 * per, 3 * per), *stats)
        factors = [f * x for f, x in zip(factors, scales)]

    def summed(pair):
        first, second = [jnp.broadcast_to(f[:, pair:pair + 1], (per, LANES)) for f in factors]
        x, y = both(slice(pair * per, (pair + 1) * per))
        return first * x + second * y

    return peak, total, summed


def merge_kernel(bit, pairs, per, own, got, *outs):
    swap = lax.rem(lax.axis_index("ctx") // bit, 2) == 1
    base = pairs * per
    for i, out in enumerate(outs):
        x, y = (own, got) if len(outs) == 1 else (own.at[i], got.at[i])
        peak, total, summed = merge(swap, x, y, pairs, per)
        for pair in range(pairs):
            out[pair * per:(pair + 1) * per, :] = summed(pair)
        out[base:base + per, :] = peak
        out[base + per:base + 2 * per, :] = total


def halve_kernel(bit, pairs, per, own, got, kept, sent, work):
    index = lax.axis_index("ctx")
    peak, total, summed = merge(lax.rem(index // bit, 2) == 1, own, got, pairs, per)
    share = pairs // 2
    base = share * per
    for half in range(2):
        for i in range(share):
            work[half, i * per:(i + 1) * per, :] = summed(half * share + i)
        for i, x in enumerate((peak, total)):
            at = base + i * per
            work[half, at:at + per, :] = pltpu.roll(x, LANES - share, 1) if half else x
    mine = lax.rem(index // (2 * bit), 2)
    kept[...] = work[mine]
    sent[...] = work[1 - mine]


def scale_kernel(pairs, per, block, sums, stats):
    lane = lax.broadcasted_iota(jnp.int32, (per, LANES), 1)
    base = pairs * per
    scales = jnp.ones((per, LANES), F32)
    for pair in range(pairs):
        x = block[pair * per:(pair + 1) * per, :]
        largest = jnp.max(jnp.abs(x), axis=1, keepdims=True)
        largest = jnp.where(largest > 0.0, largest, 1.0)
        sums[pair * per:(pair + 1) * per, :] = x / largest
        scales = jnp.where(lane == pair, largest, scales)
    stats[:2 * per, :] = block[base:base + 2 * per, :]
    stats[2 * per:, :] = scales


def last_kernel(bit, pairs, per, own, got, own_stats, got_stats, out):
    swap = lax.rem(lax.axis_index("ctx") // bit, 2) == 1
    base = pairs * per
    peak, total, summed = merge(swap, own, got, pairs, per, own_stats, got_stats)
    lane = lax.broadcasted_iota(jnp.int32, peak.shape, 1)
    total = jnp.where(lane < pairs, total, 1.0)
    peak = jnp.where(lane < pairs, peak, 0.0)

    def result(pair):
        return summed(pair) / jnp.broadcast_to(total[:, pair:pair + 1], (per, LANES))

    for pair in range(0, pairs, 2):
        both = jnp.concatenate([result(pair), result(pair + 1)], axis=0)
        out[pair * per:(pair + 2) * per, :] = both.astype(BF16)
    rest = jnp.concatenate([peak, total], axis=0)
    lane = lax.broadcasted_iota(jnp.int32, rest.shape, 1)
    parts = []
    for i in range(3):
        parts.append(rest.astype(BF16).astype(F32))
        rest = rest - parts[i]
    half = LANES // 2
    packed = jnp.where(lane < half, parts[0], pltpu.roll(parts[1], half, 1))
    out[base:base + 2 * per, :] = packed.astype(BF16)
    out[base + 2 * per:base + 4 * per, :] = parts[2].astype(BF16)


def finish_kernel(pairs, per, heads, levels, stats_ref, *refs):
    ins, (out, mass_ref, mass_vm, sem) = refs[:2 * levels], refs[2 * levels:]
    me = lax.axis_index("ctx")
    share = pairs // 2
    base = share * per
    mine = lax.rem(me // levels, 2)
    copies = []
    for level in range(levels):
        for far in range(2):
            step, half = jnp.bitwise_xor(place_of(me), level), jnp.bitwise_xor(mine, far)
            i = 2 * level + far
            copies.append(pltpu.make_async_copy(ins[i].at[:base], out.at[step, half], sem.at[i]))
            copies[i].start()
    lane = lax.broadcasted_iota(jnp.int32, (2 * per, LANES), 1)
    masses = [jnp.zeros((per, LANES), F32)] * 2
    for level in range(levels):
        rows = slice(level * per, (level + 1) * per)
        own_peak, own_total = stats_ref[0, rows, :], stats_ref[1, rows, :]
        for far in range(2):
            message = ins[2 * level + far]
            packed = message[base:base + 2 * per, :].astype(F32)
            third = message[base + 2 * per:base + 4 * per, :].astype(F32)
            both = third + pltpu.roll(packed, LANES // 2, 1) + packed
            both = jnp.where(lane < share, both, 1.0)
            second = jnp.bitwise_xor(mine, far) == 1
            peak, total = [
                jnp.where(second, pltpu.roll(x, LANES - share, 1), x) for x in (own_peak, own_total)
            ]
            mass = total * (jnp.exp(jnp.minimum(peak - both[:per], 0.0)) / both[per:])
            masses = [masses[0] + jnp.where(second, 0.0, mass), masses[1] + jnp.where(second, mass, 0.0)]
    for half in range(2):
        mass = jnp.sum(masses[half], axis=0, keepdims=True)
        for i in range(share // heads):
            mass_vm[half * (share // heads) + i] = mass[:, i * heads:(i + 1) * heads]
    copies.append(pltpu.make_async_copy(mass_vm, mass_ref, sem.at[2 * levels]))
    copies[-1].start()
    for copy in copies:
        copy.wait()


def place_keys_kernel(devices, group, first, table, got, out, sem):
    heads = out.shape[1]
    me = lax.axis_index("ctx")
    for offset in range(devices):
        source = jnp.bitwise_and(me + devices - offset, devices - 1)
        for k in range(group):
            put(got.at[source * first + k], table[offset * group + k], heads, out, sem)
    pltpu.make_async_copy(out, out, sem).wait()


def place_values_kernel(devices, group, first, table, got, got_rest, out, sem):
    heads = out.shape[1]
    me = lax.axis_index("ctx")
    rest = 2 * group - first
    for offset in range(devices):
        source = jnp.bitwise_and(me + devices - offset, devices - 1)
        for k in range(group):
            at = group + k
            src = got.at[source * first + at] if at < first else got_rest.at[source * rest + at - first]
            put(src, table[offset * group + k], heads, out, sem)


def end_kernel(devices, group, first, pairs, per, levels, table, got, got_rest, stats_ref, *refs):
    ins, (values, out, mass_ref, mass_vm, sem, place_sem) = refs[:2 * levels], refs[2 * levels:]
    place_values_kernel(devices, group, first, table, got, got_rest, values, place_sem)
    finish_kernel(pairs, per, values.shape[1], levels, stats_ref, *ins, out, mass_ref, mass_vm, sem)
    pltpu.make_async_copy(values, values, place_sem).wait()


def put(src, pair, heads, out, sem):
    @pl.when(pair >= 0)
    def _():
        pltpu.make_async_copy(src, out.at[pair // heads, lax.rem(pair, heads)], sem).start()


def local(queries, key_cache, value_cache, row_lengths, kept_tiles, tile_dest):
    devices = lax.axis_size("ctx")
    rows, heads, span, width = key_cache.shape
    steps, _, q_heads, _ = queries.shape
    per = q_heads // heads
    pairs = rows * heads
    group = -(-pairs // devices)
    levels = 4
    assert steps == levels and tile_dest.shape[2] == devices and pairs % 2 == 0 and pairs <= LANES // 2
    assert devices > 2 * levels and devices & (devices - 1) == 0 and width == LANES
    assert pairs % (2 * heads) == 0
    share = pairs // 2

    kept = jnp.transpose(kept_tiles, (1, 0, 2))
    block_rows = rows * q_heads + 2 * per
    block_type = jax.ShapeDtypeStruct((block_rows, width), F32)
    half_type = jax.ShapeDtypeStruct((share * per + 2 * per, width), F32)
    message_type = jax.ShapeDtypeStruct((share * per + 4 * per, width), BF16)
    first = 2 * group - max(1, 2 * group // 3)

    def tiles_type(count):
        return jax.ShapeDtypeStruct((devices * count, span, width), BF16)

    def exchange(x):
        return lax.all_to_all(x, "ctx", split_axis=0, concat_axis=0, tiled=True)


    tiles_out, rest_out, table = pl.pallas_call(
        functools.partial(stage_kernel, devices, group, first),
        out_shape=[
            tiles_type(first), tiles_type(2 * group - first),
            jax.ShapeDtypeStruct((devices * group,), jnp.int32),
        ],
        in_specs=[HBM, HBM, HBM],
        out_specs=[HBM, HBM, SMEM],
        scratch_shapes=[
            pltpu.VMEM(key_cache.shape, BF16),
            pltpu.VMEM(value_cache.shape, BF16),
            pltpu.SMEM(tile_dest.shape, jnp.int32),
            pltpu.SMEM((devices,), jnp.int32),
            pltpu.SemaphoreType.DMA((3,)),
            pltpu.SemaphoreType.DMA((2, rows)),
        ],
        compiler_params=WHOLE,
        cost_estimate=COST,
        name="stage",
    )(tile_dest, key_cache, value_cache)
    tiles_in = exchange(tiles_out)

    stats, *chunks = pl.pallas_call(
        functools.partial(attend_kernel, levels),
        out_shape=[
            jax.ShapeDtypeStruct((2, steps * per, LANES), F32),
        ] + [jax.ShapeDtypeStruct((2, block_rows, width), F32)] * 2,
        in_specs=[SMEM, HBM, HBM, VMEM, VMEM, VMEM],
        out_specs=[VMEM] * 3,
        scratch_shapes=[
            pltpu.SMEM(row_lengths.shape, jnp.int32),
            pltpu.SMEM(kept.shape, jnp.int32),
            pltpu.SemaphoreType.DMA((2,)),
        ],
        compiler_params=PARAMS,
        cost_estimate=COST,
        name="attend",
    )(table, row_lengths, kept, queries, key_cache, value_cache)

    def flip(x, bit):
        return lax.ppermute(x, "ctx", [(i, i ^ bit) for i in range(devices)])

    def local_call(kernel, name, out_shape, *operands, scratch=()):
        return pl.pallas_call(
            kernel,
            out_shape=out_shape,
            in_specs=[VMEM] * len(operands),
            out_specs=[VMEM] * len(out_shape),
            scratch_shapes=scratch,
            compiler_params=PARAMS,
            cost_estimate=COST,
            name=name,
        )(*operands)

    block, sent = local_call(
        functools.partial(merge_kernel, 1, pairs, per), "core", [block_type] * 2, chunks[0], flip(chunks[1], 1)
    )
    block, sent = local_call(
        functools.partial(halve_kernel, 2, pairs, per), "near", [half_type] * 2, block, flip(sent, 2),
        scratch=[pltpu.VMEM((2,) + half_type.shape, F32)],
    )
    bit, got = levels, flip(sent, levels)
    while True:
        block, = local_call(functools.partial(merge_kernel, bit, share, per), "far", [half_type], block, got)
        bit *= 2
        if 2 * bit == devices:
            break
        got = flip(block, bit)
    sums_type = jax.ShapeDtypeStruct((share * per, width), F32)
    stats_type = jax.ShapeDtypeStruct((3 * per, width), F32)
    sums, sum_stats = local_call(functools.partial(scale_kernel, share, per), "scale", [sums_type, stats_type], block)
    sums = lax.reduce_precision(sums, 5, 10)
    got = flip(sums.astype(jnp.float16), bit).astype(F32)
    got, got_stats, rest_out = lax.optimization_barrier((got, flip(sum_stats, bit), rest_out))
    rest_in = exchange(rest_out)
    message, = local_call(
        functools.partial(last_kernel, bit, share, per), "last", [message_type], sums, got, sum_stats, got_stats,
    )
    near = [message, flip(message, levels), flip(message, 2), flip(message, 2 + levels)]

    def place(kernel, name, *got):
        return pl.pallas_call(
            functools.partial(kernel, devices, group, first),
            out_shape=jax.ShapeDtypeStruct(key_cache.shape, BF16),
            in_specs=[SMEM] + [ANY] * len(got),
            out_specs=HBM,
            scratch_shapes=[pltpu.SemaphoreType.DMA],
            compiler_params=PARAMS,
            cost_estimate=COST,
            name=name,
        )(table, *got)

    moved_keys = place(place_keys_kernel, "place_keys", tiles_in)
    *forward, moved_keys = lax.optimization_barrier((*near[1:], moved_keys))
    near = [message, *forward]
    arrived = near + [flip(x, 1) for x in near]

    moved_values, attn_out, mass = pl.pallas_call(
        functools.partial(end_kernel, devices, group, first, pairs, per, levels),
        out_shape=[
            jax.ShapeDtypeStruct(value_cache.shape, BF16),
            jax.ShapeDtypeStruct((steps, 2, share * per, width), BF16),
            jax.ShapeDtypeStruct((rows, 1, heads), F32),
        ],
        in_specs=[SMEM, ANY, ANY] + [VMEM] * (1 + 2 * levels),
        out_specs=[HBM, HBM, HBM],
        scratch_shapes=[
            pltpu.VMEM((rows, 1, heads), F32),
            pltpu.SemaphoreType.DMA((2 * levels + 1,)),
            pltpu.SemaphoreType.DMA,
        ],
        compiler_params=PARAMS,
        cost_estimate=COST,
        name="end",
    )(table, tiles_in, rest_in, stats, *arrived)
    return attn_out.reshape(queries.shape), jnp.transpose(mass, (0, 2, 1)), moved_keys, moved_values


def solution(mesh):
    in_specs = (
        P(None, "grp", None, None),
        P("grp", None, "ctx", None),
        P("grp", None, "ctx", None),
        P("grp"),
        P(None, "grp", None),
        P("grp", None, None),
    )
    out_specs = (
        P(None, "grp", None, None),
        P("grp", None, "ctx"),
        P("grp", None, "ctx", None),
        P("grp", None, "ctx", None),
    )
    return jax.shard_map(local, mesh=mesh, in_specs=in_specs, out_specs=out_specs, check_vma=False)
```

```python
import functools

import jax
import jax.numpy as jnp
from jax import lax
from jax.experimental import pallas as pl
from jax.experimental.pallas import tpu as pltpu
from jax.sharding import PartitionSpec as P

absent_score = -1e30
LANES = 128
F32 = jnp.float32
BF16 = jnp.bfloat16
VMEM = pl.BlockSpec(memory_space=pltpu.VMEM)
SMEM = pl.BlockSpec(memory_space=pltpu.SMEM)
HBM = pl.BlockSpec(memory_space=pltpu.HBM)
ANY = pl.BlockSpec(memory_space=pl.ANY)
PARAMS = pltpu.CompilerParams(vmem_limit_bytes=16 * 1024 * 1024)
WHOLE = pltpu.CompilerParams(vmem_limit_bytes=62 * 1024 * 1024)


COST = pl.CostEstimate(flops=1000, bytes_accessed=1000, transcendentals=0)


def stage_kernel(
    devices, group, first, dest_hbm, k_ref, v_ref, buf, buf_rest, table, k_vm, v_vm, dest, counts, sem, load_sem
):
    rows, heads = k_ref.shape[:2]
    small = pltpu.make_async_copy(dest_hbm, dest, sem.at[0])
    small.start()
    loads = []
    for row in range(rows):
        for which, (src, dst) in enumerate(((k_ref, k_vm), (v_ref, v_vm))):
            copy = pltpu.make_async_copy(src.at[row], dst.at[row], load_sem.at[which, row])
            copy.start()
            loads.append(copy)
    me = lax.axis_index("ctx")

    def clear(i, carry):
        counts[i] = 0
        for k in range(group):
            table[i * group + k] = -1
        return carry

    lax.fori_loop(0, devices, clear, 0)
    small.wait()
    for row in range(rows):
        loads[2 * row].wait()
        loads[2 * row + 1].wait()

        def send(head, carry):
            offset = dest[row, head, 0]
            rank = counts[offset]
            counts[offset] = rank + 1
            table[offset * group + rank] = row * heads + head
            target = jnp.bitwise_and(me + offset, devices - 1)
            pltpu.make_async_copy(k_vm.at[row, head], buf.at[target * first + rank], sem.at[1]).start()

            @pl.when(rank < first - group)
            def _():
                at = target * first + group + rank
                pltpu.make_async_copy(v_vm.at[row, head], buf.at[at], sem.at[2]).start()

            @pl.when(rank >= first - group)
            def _():
                at = target * (2 * group - first) + rank + group - first
                pltpu.make_async_copy(v_vm.at[row, head], buf_rest.at[at], sem.at[2]).start()
            return carry

        lax.fori_loop(0, heads, send, 0, unroll=True)
    pltpu.make_async_copy(k_ref, k_vm, sem.at[1]).wait()
    pltpu.make_async_copy(v_ref, v_vm, sem.at[2]).wait()


def attend_kernel(
    levels,
    table, len_hbm, kept_hbm, q_ref, k_ref, v_ref,
    stats_ref, *rest,
):
    chunks = rest[:levels // 2]
    len_ref, kept_ref, small_sem = rest[levels // 2:]
    rows, heads, tile, width = k_ref.shape
    steps, _, q_heads, _ = q_ref.shape
    per = q_heads // heads
    me = lax.axis_index("ctx")

    small = [
        pltpu.make_async_copy(len_hbm, len_ref, small_sem.at[0]),
        pltpu.make_async_copy(kept_hbm, kept_ref, small_sem.at[1]),
    ]
    for copy in small:
        copy.start()
    for copy in small:
        copy.wait()

    lane = lax.broadcasted_iota(jnp.int32, (per, tile), 1)
    pair_lane = lax.broadcasted_iota(jnp.int32, (steps * per, LANES), 1)
    peaks = jnp.full((steps * per, LANES), absent_score, F32)
    totals = jnp.zeros((steps * per, LANES), F32)
    order = [jnp.bitwise_xor(place_of(me), level) for level in range(levels)]
    scale = width ** -0.5
    block = steps * per
    for row in range(rows):
        queries = [q_ref[step, row].astype(F32) for step in order]
        live = []
        for step in order:
            limit = jnp.where(kept_ref[row, step, me] > 0, len_ref[row] - me * tile, 0)
            live.append(lane < limit)
        live = jnp.concatenate(live * heads, axis=0)
        scores = []
        for head in range(heads):
            q = jnp.concatenate([x[head * per:(head + 1) * per] for x in queries], axis=0).astype(BF16)
            scores.append(lax.dot_general(
                q, k_ref[row, head], (((1,), (1,)), ((), ())), preferred_element_type=F32
            ))
        scores = jnp.concatenate(scores, axis=0) * scale
        peak = jnp.max(jnp.where(live, scores, absent_score), axis=1, keepdims=True)
        weights = jnp.where(live, jnp.exp(scores - peak), 0.0)
        total = jnp.sum(weights, axis=1, keepdims=True)
        rounded = weights.astype(BF16)
        for head in range(heads):
            out = jnp.dot(
                rounded[head * block:(head + 1) * block], v_ref[row, head], preferred_element_type=F32
            )
            pair = row * heads + head
            for i in range(levels):
                chunks[i // 2][i % 2, pair * per:(pair + 1) * per, :] = out[i * per:(i + 1) * per]
            here = pair_lane == pair
            peaks = jnp.where(here, peak[head * block:(head + 1) * block], peaks)
            totals = jnp.where(here, total[head * block:(head + 1) * block], totals)
    base = rows * q_heads
    for i in range(levels):
        chunks[i // 2][i % 2, base:base + per, :] = peaks[i * per:(i + 1) * per]
        chunks[i // 2][i % 2, base + per:base + 2 * per, :] = totals[i * per:(i + 1) * per]
    stats_ref[0] = peaks
    stats_ref[1] = totals


def place_of(me):
    return lax.rem(me, 2) * 2 + lax.rem(me // 2, 2)


def merge(swap, own, got, pairs, per, own_stats=None, got_stats=None):
    def both(rows, own=own, got=got):
        x, y = own[rows, :], got[rows, :]
        return jnp.where(swap, y, x), jnp.where(swap, x, y)

    scaled = own_stats is not None
    base = 0 if scaled else pairs * per
    stats = (own_stats, got_stats) if scaled else (own, got)
    peaks = both(slice(base, base + per), *stats)
    totals = both(slice(base + per, base + 2 * per), *stats)
    peak = jnp.maximum(*peaks)
    factors = [jnp.exp(x - peak) for x in peaks]
    total = factors[0] * totals[0] + factors[1] * totals[1]
    if scaled:
        scales = both(slice(2 * per, 3 * per), *stats)
        factors = [f * x for f, x in zip(factors, scales)]

    def summed(pair):
        first, second = [jnp.broadcast_to(f[:, pair:pair + 1], (per, LANES)) for f in factors]
        x, y = both(slice(pair * per, (pair + 1) * per))
        return first * x + second * y

    return peak, total, summed


def merge_kernel(bit, pairs, per, own, got, *outs):
    swap = lax.rem(lax.axis_index("ctx") // bit, 2) == 1
    base = pairs * per
    for i, out in enumerate(outs):
        x, y = (own, got) if len(outs) == 1 else (own.at[i], got.at[i])
        peak, total, summed = merge(swap, x, y, pairs, per)
        for pair in range(pairs):
            out[pair * per:(pair + 1) * per, :] = summed(pair)
        out[base:base + per, :] = peak
        out[base + per:base + 2 * per, :] = total


def halve_kernel(bit, pairs, per, own, got, kept, sent, work):
    index = lax.axis_index("ctx")
    peak, total, summed = merge(lax.rem(index // bit, 2) == 1, own, got, pairs, per)
    share = pairs // 2
    base = share * per
    for half in range(2):
        for i in range(share):
            work[half, i * per:(i + 1) * per, :] = summed(half * share + i)
        for i, x in enumerate((peak, total)):
            at = base + i * per
            work[half, at:at + per, :] = pltpu.roll(x, LANES - share, 1) if half else x
    mine = lax.rem(index // (2 * bit), 2)
    kept[...] = work[mine]
    sent[...] = work[1 - mine]


def scale_kernel(pairs, per, block, sums, stats):
    lane = lax.broadcasted_iota(jnp.int32, (per, LANES), 1)
    base = pairs * per
    scales = jnp.ones((per, LANES), F32)
    for pair in range(pairs):
        x = block[pair * per:(pair + 1) * per, :]
        largest = jnp.max(jnp.abs(x), axis=1, keepdims=True)
        largest = jnp.where(largest > 0.0, largest, 1.0)
        sums[pair * per:(pair + 1) * per, :] = x / largest
        scales = jnp.where(lane == pair, largest, scales)
    stats[:2 * per, :] = block[base:base + 2 * per, :]
    stats[2 * per:, :] = scales


def last_kernel(bit, pairs, per, own, got, own_stats, got_stats, out):
    swap = lax.rem(lax.axis_index("ctx") // bit, 2) == 1
    base = pairs * per
    peak, total, summed = merge(swap, own, got, pairs, per, own_stats, got_stats)
    lane = lax.broadcasted_iota(jnp.int32, peak.shape, 1)
    total = jnp.where(lane < pairs, total, 1.0)
    peak = jnp.where(lane < pairs, peak, 0.0)

    def result(pair):
        return summed(pair) / jnp.broadcast_to(total[:, pair:pair + 1], (per, LANES))

    for pair in range(0, pairs, 2):
        both = jnp.concatenate([result(pair), result(pair + 1)], axis=0)
        out[pair * per:(pair + 2) * per, :] = both.astype(BF16)
    rest = jnp.concatenate([peak, total], axis=0)
    lane = lax.broadcasted_iota(jnp.int32, rest.shape, 1)
    parts = []
    for i in range(3):
        parts.append(rest.astype(BF16).astype(F32))
        rest = rest - parts[i]
    half = LANES // 2
    packed = jnp.where(lane < half, parts[0], pltpu.roll(parts[1], half, 1))
    out[base:base + 2 * per, :] = packed.astype(BF16)
    out[base + 2 * per:base + 4 * per, :] = parts[2].astype(BF16)


def finish_kernel(pairs, per, heads, levels, stats_ref, *refs):
    ins, (out, mass_ref, mass_vm, sem) = refs[:2 * levels], refs[2 * levels:]
    me = lax.axis_index("ctx")
    share = pairs // 2
    base = share * per
    mine = lax.rem(me // levels, 2)
    copies = []
    for level in range(levels):
        for far in range(2):
            step, half = jnp.bitwise_xor(place_of(me), level), jnp.bitwise_xor(mine, far)
            i = 2 * level + far
            copies.append(pltpu.make_async_copy(ins[i].at[:base], out.at[step, half], sem.at[i]))
            copies[i].start()
    lane = lax.broadcasted_iota(jnp.int32, (2 * per, LANES), 1)
    masses = [jnp.zeros((per, LANES), F32)] * 2
    for level in range(levels):
        rows = slice(level * per, (level + 1) * per)
        own_peak, own_total = stats_ref[0, rows, :], stats_ref[1, rows, :]
        for far in range(2):
            message = ins[2 * level + far]
            packed = message[base:base + 2 * per, :].astype(F32)
            third = message[base + 2 * per:base + 4 * per, :].astype(F32)
            both = third + pltpu.roll(packed, LANES // 2, 1) + packed
            both = jnp.where(lane < share, both, 1.0)
            second = jnp.bitwise_xor(mine, far) == 1
            peak, total = [
                jnp.where(second, pltpu.roll(x, LANES - share, 1), x) for x in (own_peak, own_total)
            ]
            mass = total * (jnp.exp(jnp.minimum(peak - both[:per], 0.0)) / both[per:])
            masses = [masses[0] + jnp.where(second, 0.0, mass), masses[1] + jnp.where(second, mass, 0.0)]
    for half in range(2):
        mass = jnp.sum(masses[half], axis=0, keepdims=True)
        for i in range(share // heads):
            mass_vm[half * (share // heads) + i] = mass[:, i * heads:(i + 1) * heads]
    copies.append(pltpu.make_async_copy(mass_vm, mass_ref, sem.at[2 * levels]))
    copies[-1].start()
    for copy in copies:
        copy.wait()


def place_keys_kernel(devices, group, first, table, got, out, sem):
    heads = out.shape[1]
    me = lax.axis_index("ctx")
    for offset in range(devices):
        source = jnp.bitwise_and(me + devices - offset, devices - 1)
        for k in range(group):
            put(got.at[source * first + k], table[offset * group + k], heads, out, sem)
    pltpu.make_async_copy(out, out, sem).wait()


def place_values_kernel(devices, group, first, table, got, got_rest, out, sem):
    heads = out.shape[1]
    me = lax.axis_index("ctx")
    rest = 2 * group - first
    for offset in range(devices):
        source = jnp.bitwise_and(me + devices - offset, devices - 1)
        for k in range(group):
            at = group + k
            src = got.at[source * first + at] if at < first else got_rest.at[source * rest + at - first]
            put(src, table[offset * group + k], heads, out, sem)


def end_kernel(devices, group, first, pairs, per, levels, table, got, got_rest, stats_ref, *refs):
    ins, (values, out, mass_ref, mass_vm, sem, place_sem) = refs[:2 * levels], refs[2 * levels:]
    place_values_kernel(devices, group, first, table, got, got_rest, values, place_sem)
    finish_kernel(pairs, per, values.shape[1], levels, stats_ref, *ins, out, mass_ref, mass_vm, sem)
    pltpu.make_async_copy(values, values, place_sem).wait()


def put(src, pair, heads, out, sem):
    @pl.when(pair >= 0)
    def _():
        pltpu.make_async_copy(src, out.at[pair // heads, lax.rem(pair, heads)], sem).start()


def local(queries, key_cache, value_cache, row_lengths, kept_tiles, tile_dest):
    devices = lax.axis_size("ctx")
    rows, heads, span, width = key_cache.shape
    steps, _, q_heads, _ = queries.shape
    per = q_heads // heads
    pairs = rows * heads
    group = -(-pairs // devices)
    levels = 4
    assert steps == levels and tile_dest.shape[2] == devices and pairs % 2 == 0 and pairs <= LANES // 2
    assert devices > 2 * levels and devices & (devices - 1) == 0 and width == LANES
    assert pairs % (2 * heads) == 0
    share = pairs // 2

    kept = jnp.transpose(kept_tiles, (1, 0, 2))
    block_rows = rows * q_heads + 2 * per
    block_type = jax.ShapeDtypeStruct((block_rows, width), F32)
    half_type = jax.ShapeDtypeStruct((share * per + 2 * per, width), F32)
    message_type = jax.ShapeDtypeStruct((share * per + 4 * per, width), BF16)
    first = 2 * group - max(1, 2 * group // 3)

    def tiles_type(count):
        return jax.ShapeDtypeStruct((devices * count, span, width), BF16)

    def exchange(x):
        return lax.all_to_all(x, "ctx", split_axis=0, concat_axis=0, tiled=True)


    tiles_out, rest_out, table = pl.pallas_call(
        functools.partial(stage_kernel, devices, group, first),
        out_shape=[
            tiles_type(first), tiles_type(2 * group - first),
            jax.ShapeDtypeStruct((devices * group,), jnp.int32),
        ],
        in_specs=[HBM, HBM, HBM],
        out_specs=[HBM, HBM, SMEM],
        scratch_shapes=[
            pltpu.VMEM(key_cache.shape, BF16),
            pltpu.VMEM(value_cache.shape, BF16),
            pltpu.SMEM(tile_dest.shape, jnp.int32),
            pltpu.SMEM((devices,), jnp.int32),
            pltpu.SemaphoreType.DMA((3,)),
            pltpu.SemaphoreType.DMA((2, rows)),
        ],
        compiler_params=WHOLE,
        cost_estimate=COST,
        name="stage",
    )(tile_dest, key_cache, value_cache)
    tiles_in = exchange(tiles_out)

    stats, *chunks = pl.pallas_call(
        functools.partial(attend_kernel, levels),
        out_shape=[
            jax.ShapeDtypeStruct((2, steps * per, LANES), F32),
        ] + [jax.ShapeDtypeStruct((2, block_rows, width), F32)] * 2,
        in_specs=[SMEM, HBM, HBM, VMEM, VMEM, VMEM],
        out_specs=[VMEM] * 3,
        scratch_shapes=[
            pltpu.SMEM(row_lengths.shape, jnp.int32),
            pltpu.SMEM(kept.shape, jnp.int32),
            pltpu.SemaphoreType.DMA((2,)),
        ],
        compiler_params=PARAMS,
        cost_estimate=COST,
        name="attend",
    )(table, row_lengths, kept, queries, key_cache, value_cache)

    def flip(x, bit):
        return lax.ppermute(x, "ctx", [(i, i ^ bit) for i in range(devices)])

    def local_call(kernel, name, out_shape, *operands, scratch=()):
        return pl.pallas_call(
            kernel,
            out_shape=out_shape,
            in_specs=[VMEM] * len(operands),
            out_specs=[VMEM] * len(out_shape),
            scratch_shapes=scratch,
            compiler_params=PARAMS,
            cost_estimate=COST,
            name=name,
        )(*operands)

    block, sent = local_call(
        functools.partial(merge_kernel, 1, pairs, per), "core", [block_type] * 2, chunks[0], flip(chunks[1], 1)
    )
    block, sent = local_call(
        functools.partial(halve_kernel, 2, pairs, per), "near", [half_type] * 2, block, flip(sent, 2),
        scratch=[pltpu.VMEM((2,) + half_type.shape, F32)],
    )
    bit, got = levels, flip(sent, levels)
    while True:
        block, = local_call(functools.partial(merge_kernel, bit, share, per), "far", [half_type], block, got)
        bit *= 2
        if 2 * bit == devices:
            break
        got = flip(block, bit)
    sums_type = jax.ShapeDtypeStruct((share * per, width), F32)
    stats_type = jax.ShapeDtypeStruct((3 * per, width), F32)
    sums, sum_stats = local_call(functools.partial(scale_kernel, share, per), "scale", [sums_type, stats_type], block)
    sums = lax.reduce_precision(sums, 5, 10)
    got = flip(sums.astype(jnp.float16), bit).astype(F32)
    got, got_stats, rest_out = lax.optimization_barrier((got, flip(sum_stats, bit), rest_out))
    rest_in = exchange(rest_out)
    message, = local_call(
        functools.partial(last_kernel, bit, share, per), "last", [message_type], sums, got, sum_stats, got_stats,
    )
    near = [message, flip(message, levels), flip(message, 2), flip(message, 2 + levels)]

    def place(kernel, name, *got):
        return pl.pallas_call(
            functools.partial(kernel, devices, group, first),
            out_shape=jax.ShapeDtypeStruct(key_cache.shape, BF16),
            in_specs=[SMEM] + [ANY] * len(got),
            out_specs=HBM,
            scratch_shapes=[pltpu.SemaphoreType.DMA],
            compiler_params=PARAMS,
            cost_estimate=COST,
            name=name,
        )(table, *got)

    moved_keys = place(place_keys_kernel, "place_keys", tiles_in)
    *forward, moved_keys = lax.optimization_barrier((*near[1:], moved_keys))
    near = [message, *forward]
    arrived = near + [flip(x, 1) for x in near]

    moved_values, attn_out, mass = pl.pallas_call(
        functools.partial(end_kernel, devices, group, first, pairs, per, levels),
        out_shape=[
            jax.ShapeDtypeStruct(value_cache.shape, BF16),
            jax.ShapeDtypeStruct((steps, 2, share * per, width), BF16),
            jax.ShapeDtypeStruct((rows, 1, heads), F32),
        ],
        in_specs=[SMEM, ANY, ANY] + [VMEM] * (1 + 2 * levels),
        out_specs=[HBM, HBM, HBM],
        scratch_shapes=[
            pltpu.VMEM((rows, 1, heads), F32),
            pltpu.SemaphoreType.DMA((2 * levels + 1,)),
            pltpu.SemaphoreType.DMA,
        ],
        compiler_params=PARAMS,
        cost_estimate=COST,
        name="end",
    )(table, tiles_in, rest_in, stats, *arrived)
    return attn_out.reshape(queries.shape), jnp.transpose(mass, (0, 2, 1)), moved_keys, moved_values


def solution(mesh):
    in_specs = (
        P(None, "grp", None, None),
        P("grp", None, "ctx", None),
        P("grp", None, "ctx", None),
        P("grp"),
        P(None, "grp", None),
        P("grp", None, None),
    )
    out_specs = (
        P(None, "grp", None, None),
        P("grp", None, "ctx"),
        P("grp", None, "ctx", None),
        P("grp", None, "ctx", None),
    )
    return jax.shard_map(local, mesh=mesh, in_specs=in_specs, out_specs=out_specs, check_vma=False)
```
